512 devices in a mesh: dp: 32 (over z, x), fsdp: 16 (over y, core).
Axes of the slice: x: 4, y: 8, z: 8, core: 2. Of those that a mesh axis runs over, the one named last changes fastest.
Arguments:
- attended: bfloat16 [2048, 16384], P(None, 'dp'), may hold values from -6 to 6
- residual: bfloat16 [3200, 16384], P('fsdp', 'dp'), may hold values from -6 to 6
- grad_out: bfloat16 [3200, 12288], P('fsdp', 'dp'), may hold values from -10 to 10
- out_weight: bfloat16 [3200, 2048], P('fsdp'), may hold values from -0.125 to 0.125
- layer_scale: float32 [3200], P('fsdp'), may hold values from 0.1 to 1.9
- frames: int32 [32], replicated, may hold values from 0 to 2, as said below
- partner: int32 [32], replicated, may hold values from 0 to 31, as said below
- moved_tiles: int32 [32], replicated, may hold values from 0 to 16, as said below
- owner_slot: int32 [16], replicated, may hold values from 0 to 15, each once
Outputs:
- layer_out: bfloat16 [3200, 12288], P('fsdp', 'dp')
- input_grad: bfloat16 [2048, 16384], P('fsdp', 'dp')
- scale_grad: float32 [3200], P('fsdp')
- ortho_update: bfloat16 [3200, 16, 128], P(None, 'fsdp')
The draws below stay inside these ranges and needn't reach their ends.
Inputs may be any that keep to these rules, and one draw needn't show every extreme that they name: In each pair of partners one replica holds 2 frames and the other at most half of 2. partner[partner[i]] = i and partner[i] != i. Replica i sends the last moved_tiles[i] tiles of 16 patches of its live slots to partner[i]; only the replica of a pair that holds 2 frames sends; after the moves every replica holds at most 24 tiles, and some pair holds exactly 24 tiles on both sides. `owner_slot`: each slot once.
All inputs are finite; a program needn't handle non-finite values.
Results may differ from the reference program's by a relative error of at most 0.022.
Values may be sent and summed in bfloat16 or wider, within the bound.
No kernel may reach another device: no remote copies, remote signals or barrier semaphores. Data moves between devices by JAX's collectives and lax.ppermute only.
A program may use at most 64 MiB of HBM per device.

```python
import math
import jax
import jax.numpy as jnp
from jax import lax

D = 3200
HEADS = 16
HD = 128
FRAME = 256
TILE = 16
FMAX = 2
ITERS = 5
A = 2048
CAP_ROWS = 512
MOVE_ROWS = 256
BAL_ROWS = 384
N_DP = 32
N_FSDP = 16


def pair_table(key):
    shuffled = jax.random.permutation(jax.random.fold_in(key, 1), N_DP).astype(jnp.int32)
    pair_count = N_DP // 2
    heavy_side = shuffled[0::2]
    light_side = shuffled[1::2]
    frame_tiles = FRAME // TILE
    light_frames = jax.random.randint(jax.random.fold_in(key, 2), (pair_count,), 0, FMAX // 2 + 1).astype(jnp.int32)
    light_frames = light_frames.at[0].set(0).at[1].set(FMAX // 2)
    lower_bound = FMAX * frame_tiles // 4
    upper_bound = jnp.minimum(FMAX * frame_tiles // 2, 3 * FMAX * frame_tiles // 4 - light_frames * frame_tiles)
    raw_draws = jax.random.randint(jax.random.fold_in(key, 3), (pair_count,), 0, 1048576).astype(jnp.int32)
    move_count = lower_bound + raw_draws % (upper_bound - lower_bound + 1)
    move_count = move_count.at[0].set(FMAX * frame_tiles // 2)
    zeros_table = jnp.zeros((N_DP,), jnp.int32)
    frame_table = zeros_table.at[heavy_side].set(FMAX).at[light_side].set(light_frames)
    partner_table = zeros_table.at[heavy_side].set(light_side).at[light_side].set(heavy_side)
    moved_table = zeros_table.at[heavy_side].set(move_count)
    return (frame_table, partner_table, moved_table)


def draw_frames(key, part):
    tables = pair_table(key)
    return tables[0]


def draw_partner(key, part):
    tables = pair_table(key)
    return tables[1]


def draw_moved_tiles(key, part):
    tables = pair_table(key)
    return tables[2]


def draw_grad_out(key, part):
    key = jax.random.fold_in(key, 31)
    scale_key, value_key = jax.random.split(key, 2)
    scales = jnp.exp(jax.random.uniform(scale_key, (D, 1), jnp.float32, math.log(0.25), math.log(2.5)))
    values = jnp.clip(jax.random.normal(value_key, (D, N_DP * BAL_ROWS), jnp.float32), -4.0, 4.0)
    return (values * scales).astype(jnp.bfloat16)


def levels(stream_key, shape, cuts, smallest, largest):
    gain, own = 1.0, jax.random.fold_in(stream_key, 6)
    for position, parts in cuts:
        heights = jnp.exp(jax.random.uniform(jax.random.fold_in(own, position), (parts,), jnp.float32, smallest / len(cuts), largest / len(cuts)))
        gain = gain * jnp.repeat(heights, shape[position] // parts).reshape([-1 if axis == position else 1 for axis in range(len(shape))])
    return gain


def normal_values(key, shape, scale, reach, cuts=(), held_as=jnp.bfloat16):
    drawn = scale * jax.random.normal(key, shape, jnp.float32)
    if cuts:
        drawn = drawn * levels(key, shape, cuts, -0.22, 0.18)
    return jnp.clip(drawn, -reach, reach).astype(held_as)


def setup_inputs(seed: int = 0) -> dict:
    key_of = jax.random.split(jax.random.key(seed), 10)
    attended = normal_values(key_of[0], (A, N_DP * CAP_ROWS), 1.0, 6.0, ((1, 32),))
    residual = normal_values(key_of[1], (D, N_DP * CAP_ROWS), 1.0, 6.0, ((0, 16), (1, 32)))
    grad_out = draw_grad_out(jax.random.fold_in(key_of[9], 71), 0)
    out_weight = normal_values(key_of[3], (D, A), A ** -0.5, 0.125, ((0, 16),))
    layer_scale = jnp.clip(1.0 + 0.18 * jax.random.normal(key_of[4], (D,), jnp.float32), 0.1, 1.9)
    frames = draw_frames(jax.random.fold_in(key_of[9], 71), 0)
    partner = draw_partner(jax.random.fold_in(key_of[9], 71), 0)
    moved_tiles = draw_moved_tiles(jax.random.fold_in(key_of[9], 71), 0)
    owner_slot = jax.random.permutation(key_of[8], HEADS).astype(jnp.int32)
    return {"attended": attended, "residual": residual, "grad_out": grad_out, "out_weight": out_weight, "layer_scale": layer_scale, "frames": frames, "partner": partner, "moved_tiles": moved_tiles, "owner_slot": owner_slot}


coeff_linear = 3.4445
coeff_square = -4.775
coeff_cubic = 2.0315
EPSILON = 1e-07

def positions(shape, dimension):
    return lax.broadcasted_iota(jnp.int32, shape, dimension)

def pad_along(values, before, after, dimension):
    widths = [(0, 0)] * values.ndim
    widths[dimension] = (before, after)
    return jnp.pad(values, widths)

def send_window(rows, live, sent, dimension):
    begin = jnp.maximum(live - MOVE_ROWS, 0)
    window = lax.dynamic_slice_in_dim(rows, begin, MOVE_ROWS, dimension)
    chosen = positions(window.shape, dimension) >= MOVE_ROWS - sent
    return jnp.where(chosen, window, jnp.zeros_like(window))

def place_received(own_rows, received, kept, incoming, dimension):
    own_part = lax.slice_in_dim(own_rows, 0, BAL_ROWS, axis=dimension)
    own_part = jnp.where(positions(own_part.shape, dimension) < kept, own_part, jnp.zeros_like(own_part))
    padded = pad_along(received, BAL_ROWS, BAL_ROWS, dimension)
    begin = BAL_ROWS + MOVE_ROWS - incoming - kept
    return own_part + lax.dynamic_slice_in_dim(padded, begin, BAL_ROWS, dimension)

def return_window(balanced, kept, incoming, dimension):
    padded = pad_along(balanced, MOVE_ROWS, MOVE_ROWS, dimension)
    window = lax.dynamic_slice_in_dim(padded, kept + incoming, MOVE_ROWS, dimension)
    chosen = positions(window.shape, dimension) >= MOVE_ROWS - incoming
    return jnp.where(chosen, window, jnp.zeros_like(window))

def place_returned(balanced, returned, live, kept, dimension):
    own_part = pad_along(balanced, 0, CAP_ROWS - BAL_ROWS, dimension)
    own_part = jnp.where(positions(own_part.shape, dimension) < kept, own_part, jnp.zeros_like(own_part))
    padded = pad_along(returned, CAP_ROWS, CAP_ROWS, dimension)
    begin = CAP_ROWS + MOVE_ROWS - live
    return own_part + lax.dynamic_slice_in_dim(padded, begin, CAP_ROWS, dimension)

def newton_schulz(matrix):
    highest = lax.Precision.HIGHEST
    iterate = matrix / (jnp.sqrt(jnp.sum(matrix * matrix)) + EPSILON)
    for sweep in range(ITERS):
        gram_matrix = jnp.dot(iterate.T, iterate, precision=highest)
        square = jnp.dot(gram_matrix, gram_matrix, precision=highest)
        polynomial = coeff_square * gram_matrix + coeff_cubic * square
        iterate = coeff_linear * iterate + jnp.dot(iterate, polynomial, precision=highest)
    return (0.2 * math.sqrt(D) * iterate).astype(jnp.bfloat16)

def reference(attended, residual, grad_out, out_weight, layer_scale, frames, partner, moved_tiles, owner_slot):
    width_a = attended.shape[0]
    live_rows = frames * FRAME
    sent_rows = moved_tiles * TILE
    kept_rows = live_rows - sent_rows
    incoming = jnp.take(sent_rows, partner)
    attended_rep = attended.reshape(width_a, N_DP, CAP_ROWS).transpose(1, 0, 2)
    residual_rep = residual.reshape(D, N_DP, CAP_ROWS).transpose(1, 0, 2)
    send_all = jax.vmap(send_window, in_axes=(0, 0, 0, None))
    place_all = jax.vmap(place_received, in_axes=(0, 0, 0, 0, None))
    attended_win = jnp.take(send_all(attended_rep, live_rows, sent_rows, 1), partner, axis=0)
    residual_win = jnp.take(send_all(residual_rep, live_rows, sent_rows, 1), partner, axis=0)
    attended_bal = place_all(attended_rep, attended_win, kept_rows, incoming, 1)
    attended_bal = attended_bal.transpose(1, 0, 2).reshape(width_a, N_DP * BAL_ROWS)
    residual_bal = place_all(residual_rep, residual_win, kept_rows, incoming, 1)
    residual_bal = residual_bal.transpose(1, 0, 2).reshape(D, N_DP * BAL_ROWS)
    projected = jnp.dot(out_weight, attended_bal, preferred_element_type=jnp.float32)
    gains = layer_scale[:, None]
    layer_out = (residual_bal.astype(jnp.float32) + gains * projected).astype(jnp.bfloat16)
    scaled = (grad_out.astype(jnp.float32) * gains).astype(jnp.bfloat16)
    inverse_root = 1.0 / math.sqrt(N_DP * BAL_ROWS)
    scale_grad = lax.optimization_barrier(jnp.sum(grad_out.astype(jnp.float32) * projected, axis=1)) * inverse_root
    weight_grad = lax.dot_general(scaled, attended_bal, (((1,), (1,)), ((), ())), preferred_element_type=jnp.float32)
    block_rows = D // N_FSDP
    weight_blocks = out_weight.reshape(N_FSDP, block_rows, width_a)
    scaled_blocks = scaled.reshape(N_FSDP, block_rows, N_DP * BAL_ROWS)

    def add_block(total, operands):
        term = lax.dot_general(operands[0], operands[1], (((0,), (0,)), ((), ())), preferred_element_type=jnp.float32)
        term = lax.optimization_barrier(term.astype(jnp.bfloat16))
        return (total + term.astype(jnp.float32), None)
    summed, unused = lax.scan(add_block, jnp.zeros((width_a, N_DP * BAL_ROWS), jnp.float32), (weight_blocks, scaled_blocks))
    input_bal = summed.astype(jnp.bfloat16)
    input_rep = input_bal.reshape(width_a, N_DP, BAL_ROWS).transpose(1, 0, 2)
    back_win = jax.vmap(return_window, in_axes=(0, 0, 0, None))(input_rep, kept_rows, incoming, 1)
    back_win = jnp.take(back_win, partner, axis=0)
    input_orig = jax.vmap(place_returned, in_axes=(0, 0, 0, 0, None))(input_rep, back_win, live_rows, kept_rows, 1)
    input_grad = input_orig.transpose(1, 0, 2).reshape(width_a, N_DP * CAP_ROWS)
    blocks = weight_grad.reshape(D, HEADS, HD).transpose(1, 0, 2)
    ortho = lax.map(newton_schulz, blocks)
    ortho_update = jnp.zeros((D, HEADS, HD), jnp.bfloat16).at[:, owner_slot, :].set(ortho.transpose(1, 0, 2))
    return (layer_out, input_grad, scale_grad, ortho_update)
```

```python
import math

import jax
import jax.numpy as jnp
from jax import lax
from jax.experimental import pallas as pl
from jax.experimental.pallas import tpu as pltpu
from jax.sharding import PartitionSpec as P

D = 3200
HEADS = 16
HD = 128
FRAME = 256
TILE = 16
ITERS = 5
A = 2048
CAP_ROWS = 512
MOVE_ROWS = 256
BAL_ROWS = 384
N_DP = 32
N_FSDP = 16

ROWS = D // N_FSDP
SHARE = HD // N_DP
WIDE = 3456
PAD_ROWS = 256
CHIPS = N_FSDP // 2

coeff_linear = 3.4445
coeff_square = -4.775
coeff_cubic = 2.0315
EPSILON = 1e-07
INVERSE_ROOT = 1.0 / math.sqrt(N_DP * BAL_ROWS)

bf16 = jnp.bfloat16
f32 = jnp.float32

ROWS_BY_COLS = (((0,), (0,)), ((), ()))
COLS_BY_COLS = (((1,), (1,)), ((), ()))


def positions(shape, dimension):
    return lax.broadcasted_iota(jnp.int32, shape, dimension)


def dot(a, b, dims=(((1,), (0,)), ((), ()))):
    return lax.dot_general(a, b, dims, preferred_element_type=f32)


def same(size):
    return positions((size, size), 0) == positions((size, size), 1)


def to_column(row):
    size = row.shape[1]
    return jnp.sum(jnp.where(same(size), row, 0.0), axis=1, keepdims=True)


def to_row(column):
    size = column.shape[0]
    return jnp.sum(jnp.where(same(size), column, 0.0), axis=0, keepdims=True)


def my_counts(index_ref, frames_ref, partner_ref, moved_ref):
    replica = index_ref[0]
    mate = partner_ref[replica]
    kept = frames_ref[replica] * FRAME - moved_ref[replica] * TILE
    incoming = moved_ref[mate] * TILE
    holds_two = (frames_ref[replica] > frames_ref[mate]).astype(jnp.int32)
    return kept, incoming, holds_two


def light_places(kept, incoming):
    bal_col = positions((BAL_ROWS, MOVE_ROWS), 0)
    win_col = positions((BAL_ROWS, MOVE_ROWS), 1)
    hit = bal_col == win_col + (kept + incoming - MOVE_ROWS)
    hit = hit & (win_col >= MOVE_ROWS - incoming)
    return jnp.where(hit, 1.0, 0.0).astype(bf16)


def project_kernel(
    index_ref, frames_ref, partner_ref, moved_ref,
    attended_ref, residual_ref, grad_ref, weight_ref, scale_ref,
    projected_ref, layer_ref, window_ref,
):
    kept, incoming, holds_two = my_counts(index_ref, frames_ref, partner_ref, moved_ref)
    gains = to_column(scale_ref[...])
    projected = dot(weight_ref[...], attended_ref[...])
    projected_ref[...] = projected
    layer = (residual_ref[...].astype(f32) + gains * projected).astype(bf16)
    layer_ref[...] = layer
    grad_win = dot(grad_ref[...], light_places(kept, incoming))
    layer_win = layer[:, MOVE_ROWS:].astype(f32)
    window = jnp.where(holds_two == 1, layer_win, grad_win).astype(bf16)
    window_ref[pl.ds(0, ROWS), :] = window
    window_ref[pl.ds(ROWS, PAD_ROWS - ROWS), :] = jnp.zeros(
        (PAD_ROWS - ROWS, MOVE_ROWS), bf16
    )


def weight_grad_kernel(
    index_ref, frames_ref, partner_ref, moved_ref, slot_ref,
    attended_ref, grad_ref, got_ref, projected_ref, scale_ref,
    scaled_ref, pieces_ref,
    head_of, wide,
):
    kept, incoming, holds_two = my_counts(index_ref, frames_ref, partner_ref, moved_ref)
    for head in range(HEADS):
        head_of[slot_ref[head]] = head
    own = grad_ref[...].astype(f32)
    own = jnp.concatenate([own, jnp.zeros((ROWS, CAP_ROWS - BAL_ROWS), f32)], axis=1)
    got = got_ref[pl.ds(0, ROWS), :].astype(f32)
    got = jnp.where(holds_two == 1, got, 0.0)
    got = jnp.concatenate([jnp.zeros((ROWS, CAP_ROWS - MOVE_ROWS), f32), got], axis=1)
    grad = jnp.where(positions((ROWS, CAP_ROWS), 1) < kept, own, got)
    scaled = (grad * to_column(scale_ref[...])).astype(bf16)
    scaled_ref[...] = scaled
    part = jnp.sum(grad * projected_ref[...], axis=1, keepdims=True) * INVERSE_ROOT
    part = to_row(part)
    high = part.astype(bf16).astype(f32)
    low = part - high
    wide[:, pl.ds(D, WIDE - D)] = jnp.zeros((HD, WIDE - D), f32)
    for slot in range(HEADS):
        first = pl.multiple_of(head_of[slot] * HD, HD)
        wide[:, pl.ds(slot * ROWS, ROWS)] = dot(
            attended_ref[pl.ds(first, HD), :], scaled, COLS_BY_COLS
        )
    for piece in range(N_DP):
        pieces_ref[piece] = wide[pl.ds(piece * SHARE, SHARE), :].astype(bf16)
        pieces_ref[piece, pl.ds(0, 2), pl.ds(D, ROWS)] = jnp.concatenate(
            [high, low], axis=0
        ).astype(bf16)


def input_kernel(
    index_ref, frames_ref, partner_ref, moved_ref,
    weight_ref, scaled_ref, layer_ref, got_ref,
    layer_out_ref, mine_ref, theirs_ref,
):
    kept, incoming, holds_two = my_counts(index_ref, frames_ref, partner_ref, moved_ref)
    core = index_ref[1]
    scaled = scaled_ref[...]
    for chip in range(CHIPS):
        first = pl.multiple_of((2 * chip + core) * HD, HD)
        mine_ref[chip] = dot(weight_ref[:, pl.ds(first, HD)], scaled, ROWS_BY_COLS).astype(bf16)
        first = pl.multiple_of((2 * chip + 1 - core) * HD, HD)
        theirs_ref[chip] = dot(weight_ref[:, pl.ds(first, HD)], scaled, ROWS_BY_COLS).astype(bf16)
    received = dot(got_ref[pl.ds(0, ROWS), :], light_places(kept, incoming), COLS_BY_COLS)
    own = layer_ref[:, pl.ds(0, BAL_ROWS)].astype(f32)
    keep = positions((ROWS, BAL_ROWS), 1) < kept
    layer_out_ref[...] = jnp.where(keep, own, received).astype(bf16)


def slots_kernel(pieces_ref, by_slot_ref, scale_grad_ref):
    total = pieces_ref[0].astype(f32)
    for piece in range(1, N_DP):
        total = total + pieces_ref[piece].astype(f32)
    for slot in range(HEADS):
        by_slot_ref[slot] = total[:, slot * ROWS : (slot + 1) * ROWS].astype(bf16)
    scale_grad_ref[...] = total[0:1, D : D + ROWS] + total[1:2, D : D + ROWS]


def spread_kernel(owned_ref, copies_ref, joined):
    for block in range(N_FSDP):
        joined[:, pl.ds(block * ROWS, ROWS)] = owned_ref[block].astype(f32)
    whole = joined[...].astype(bf16)
    for piece in range(N_DP):
        copies_ref[piece] = whole


def ortho_kernel(pieces_ref, out_ref, joined):
    def mul(a, b):
        return jnp.dot(a, b, precision=lax.Precision.HIGHEST, preferred_element_type=f32)

    for piece in range(N_DP):
        joined[pl.ds(piece * SHARE, SHARE), :] = pieces_ref[piece].astype(f32)
    grad = joined[...].astype(bf16)
    gram = dot(grad, grad, COLS_BY_COLS)
    eye = jnp.where(same(HD), 1.0, 0.0).astype(f32)
    squares = jnp.sum(jnp.sum(gram * eye, axis=1, keepdims=True), axis=0, keepdims=True)
    norm = jnp.sqrt(squares) + EPSILON
    gram = gram / norm / norm
    total = None
    for sweep in range(ITERS):
        step = coeff_linear * eye + coeff_square * gram + coeff_cubic * mul(gram, gram)
        total = step if total is None else mul(total, step)
        if sweep < ITERS - 1:
            gram = mul(mul(step, gram), step)
    total = total * (0.2 * math.sqrt(D) / norm)
    high = total.astype(bf16)
    low = (total - high.astype(f32)).astype(bf16)
    out = dot(grad, high, ROWS_BY_COLS) + dot(grad, low, ROWS_BY_COLS)
    out_ref[...] = out.astype(bf16)


def call(kernel, name, scalars, arrays, outs, scratch=()):
    smem = pl.BlockSpec(memory_space=pltpu.SMEM)
    vmem = pl.BlockSpec(memory_space=pltpu.VMEM)
    return pl.pallas_call(
        kernel,
        out_shape=[jax.ShapeDtypeStruct(shape, dtype) for shape, dtype in outs],
        in_specs=[smem] * len(scalars) + [vmem] * len(arrays),
        out_specs=[vmem] * len(outs),
        scratch_shapes=list(scratch),
        compiler_params=pltpu.CompilerParams(vmem_limit_bytes=40 * 1024 * 1024),
        name=name,
    )(*scalars, *arrays)


def exchange(pieces, axis, groups=None):
    return lax.all_to_all(
        pieces, axis, split_axis=0, concat_axis=0, tiled=True, axis_index_groups=groups
    )


def body(
    attended, residual, grad_out, out_weight, layer_scale, frames, partner, moved_tiles, owner_slot
):
    index = jnp.stack([lax.axis_index("dp"), lax.axis_index("fsdp") % 2])
    counts = (index, frames, partner, moved_tiles)
    scale_row = layer_scale[None, :]

    projected, layer_own, window = call(
        project_kernel, "project", counts,
        (attended, residual, grad_out, out_weight, scale_row),
        [((ROWS, CAP_ROWS), f32), ((ROWS, CAP_ROWS), bf16), ((PAD_ROWS, MOVE_ROWS), bf16)],
    )
    pieces = exchange(window.reshape(N_DP, PAD_ROWS // N_DP, MOVE_ROWS), "dp")
    pieces = exchange(jnp.take(pieces, partner, axis=0), "dp")
    got = pieces.reshape(PAD_ROWS, MOVE_ROWS)

    scaled, pieces = call(
        weight_grad_kernel, "weight_grad", (*counts, owner_slot),
        (attended, grad_out, got, projected, scale_row),
        [((ROWS, CAP_ROWS), bf16), ((N_DP, SHARE, WIDE), bf16)],
        [pltpu.SMEM((HEADS,), jnp.int32), pltpu.VMEM((HD, WIDE), f32)],
    )
    pieces = exchange(pieces, "dp")

    layer_out, mine, theirs = call(
        input_kernel, "input_grad", counts,
        (out_weight, scaled, layer_own, got),
        [((ROWS, BAL_ROWS), bf16)] + [((CHIPS, HD, CAP_ROWS), bf16)] * 2,
    )
    theirs = lax.ppermute(theirs, "fsdp", [(i, i ^ 1) for i in range(N_FSDP)])
    mine = (mine.astype(f32) + theirs.astype(f32)).astype(bf16)
    cores = [[2 * chip + core for chip in range(CHIPS)] for core in range(2)]
    mine = exchange(mine, "fsdp", cores)
    input_grad = jnp.sum(mine.astype(f32), axis=0).astype(bf16)

    by_slot, scale_grad = call(
        slots_kernel, "slots", (), (pieces,),
        [((HEADS, SHARE, ROWS), bf16), ((1, ROWS), f32)],
    )
    owned = exchange(by_slot, "fsdp")
    (copies,) = call(
        spread_kernel, "spread", (), (owned,),
        [((N_DP, SHARE, D), bf16)],
        [pltpu.VMEM((SHARE, D), f32)],
    )
    whole = exchange(copies, "dp")
    (ortho_update,) = call(
        ortho_kernel, "ortho", (), (whole,), [((D, HD), bf16)], [pltpu.VMEM((HD, D), f32)]
    )
    return (layer_out, input_grad, scale_grad.reshape(ROWS), ortho_update[:, None, :])


def solution(mesh):
    placed = (
        P(None, "dp"),
        P("fsdp", "dp"),
        P("fsdp", "dp"),
        P("fsdp", None),
        P("fsdp"),
        P(),
        P(),
        P(),
        P(),
    )
    return jax.shard_map(
        body,
        mesh=mesh,
        in_specs=placed,
        out_specs=(P("fsdp", "dp"), P("fsdp", "dp"), P("fsdp"), P(None, "fsdp", None)),
        check_vma=False,
    )
```

```python
import math

import jax
import jax.numpy as jnp
from jax import lax
from jax.experimental import pallas as pl
from jax.experimental.pallas import tpu as pltpu
from jax.sharding import Mesh, PartitionSpec as P

D = 3200
HEADS = 16
HD = 128
FRAME = 256
TILE = 16
ITERS = 5
A = 2048
CAP_ROWS = 512
MOVE_ROWS = 256
BAL_ROWS = 384
N_DP = 32
N_FSDP = 16

NZ, NX, NY, NC = 8, 4, 8, 2
ROWS = D // N_FSDP
BY_X = HD // NX
BY_ZX = BY_X // NZ
WIDE = D + HD
PAD_ROWS = 256
CHUNK = 512

coeff_linear = 3.4445
coeff_square = -4.775
coeff_cubic = 2.0315
EPSILON = 1e-07
INVERSE_ROOT = 1.0 / math.sqrt(N_DP * BAL_ROWS)

bf16 = jnp.bfloat16
f32 = jnp.float32

ROWS_BY_COLS = (((0,), (0,)), ((), ()))
COLS_BY_COLS = (((1,), (1,)), ((), ()))


def positions(shape, dimension):
    return lax.broadcasted_iota(jnp.int32, shape, dimension)


def dot(a, b, dims=(((1,), (0,)), ((), ()))):
    return lax.dot_general(a, b, dims, preferred_element_type=f32)


def same(size):
    return positions((size, size), 0) == positions((size, size), 1)


def to_column(row):
    size = row.shape[1]
    return jnp.sum(jnp.where(same(size), row, 0.0), axis=1, keepdims=True)


def to_row(column):
    size = column.shape[0]
    return jnp.sum(jnp.where(same(size), column, 0.0), axis=0, keepdims=True)


def my_counts(frames_ref, partner_ref, moved_ref):
    replica = lax.axis_index("z") * NX + lax.axis_index("x")
    mate = partner_ref[replica]
    kept = frames_ref[replica] * FRAME - moved_ref[replica] * TILE
    incoming = moved_ref[mate] * TILE
    holds_two = (frames_ref[replica] > frames_ref[mate]).astype(jnp.int32)
    return kept, incoming, holds_two


def light_places(kept, incoming):
    bal_col = positions((BAL_ROWS, MOVE_ROWS), 0)
    win_col = positions((BAL_ROWS, MOVE_ROWS), 1)
    hit = bal_col == win_col + (kept + incoming - MOVE_ROWS)
    hit = hit & (win_col >= MOVE_ROWS - incoming)
    return jnp.where(hit, 1.0, 0.0).astype(bf16)


def start(sems, *pairs):
    copies = [pltpu.make_async_copy(a, b, sems.at[i]) for i, (a, b) in enumerate(pairs)]
    for copy in copies:
        copy.start()
    return copies


def wait(copies):
    for copy in copies:
        copy.wait()


def project_kernel(
    frames_hbm, partner_hbm, moved_hbm,
    attended_hbm, residual_hbm, grad_hbm, weight_hbm, scale_hbm,
    projected_hbm, layer_hbm, window_hbm,
    frames_ref, partner_ref, moved_ref,
    attended_ref, residual_ref, grad_ref, weight_ref, scale_ref,
    projected_ref, layer_ref, window_ref,
    small_sems, attended_sems, weight_sems, out_sems,
):
    small = start(
        small_sems,
        (frames_hbm, frames_ref),
        (partner_hbm, partner_ref),
        (moved_hbm, moved_ref),
        (scale_hbm, scale_ref),
        (grad_hbm, grad_ref),
        (residual_hbm, residual_ref),
    )
    cuts = [pl.ds(first, CHUNK) for first in range(0, A, CHUNK)]
    attended = start(
        attended_sems, *[(attended_hbm.at[cut, :], attended_ref.at[cut, :]) for cut in cuts]
    )
    weight = start(
        weight_sems, *[(weight_hbm.at[:, cut], weight_ref.at[:, cut]) for cut in cuts]
    )
    wait(small[:5])
    kept, incoming, holds_two = my_counts(frames_ref, partner_ref, moved_ref)
    gains = to_column(scale_ref[...])
    grad_win = dot(grad_ref[...], light_places(kept, incoming))
    window_ref[pl.ds(ROWS, PAD_ROWS - ROWS), :] = jnp.zeros(
        (PAD_ROWS - ROWS, MOVE_ROWS), bf16
    )
    projected = None
    for index, cut in enumerate(cuts):
        attended[index].wait()
        weight[index].wait()
        part = dot(weight_ref[:, cut], attended_ref[cut, :])
        projected = part if projected is None else projected + part
    small[5].wait()
    layer = (residual_ref[...].astype(f32) + gains * projected).astype(bf16)
    layer_win = layer[:, MOVE_ROWS:].astype(f32)
    window_ref[pl.ds(0, ROWS), :] = jnp.where(holds_two == 1, layer_win, grad_win).astype(bf16)
    out = start(out_sems, (window_ref, window_hbm))
    projected_ref[...] = projected
    layer_ref[...] = layer
    out += start(
        out_sems.at[pl.ds(1, 2)], (projected_ref, projected_hbm), (layer_ref, layer_hbm)
    )
    wait(out)


def weight_grad_kernel(
    frames_ref, partner_ref, moved_ref, slot_ref,
    attended_ref, grad_ref, scale_ref, got_ref, projected_hbm,
    scaled_hbm, pieces_hbm,
    head_of, wide, projected_ref, scaled_ref, pieces_ref, sems,
):
    (fetch,) = start(sems, (projected_hbm, projected_ref))
    kept, incoming, holds_two = my_counts(frames_ref, partner_ref, moved_ref)
    for head in range(HEADS):
        head_of[slot_ref[head]] = head
    own = grad_ref[...].astype(f32)
    own = jnp.concatenate([own, jnp.zeros((ROWS, CAP_ROWS - BAL_ROWS), f32)], axis=1)
    got = got_ref[pl.ds(0, ROWS), :].astype(f32)
    got = jnp.where(holds_two == 1, got, 0.0)
    got = jnp.concatenate([jnp.zeros((ROWS, CAP_ROWS - MOVE_ROWS), f32), got], axis=1)
    grad = jnp.where(positions((ROWS, CAP_ROWS), 1) < kept, own, got)
    scaled = (grad * to_column(scale_ref[...])).astype(bf16)
    scaled_ref[...] = scaled
    (store,) = start(sems.at[pl.ds(1, 1)], (scaled_ref, scaled_hbm))
    for slot in range(HEADS):
        first = pl.multiple_of(head_of[slot] * HD, HD)
        wide[:, pl.ds(slot * ROWS, ROWS)] = dot(
            attended_ref[pl.ds(first, HD), :], scaled, COLS_BY_COLS
        )
    fetch.wait()
    part = jnp.sum(grad * projected_ref[...], axis=1, keepdims=True) * INVERSE_ROOT
    part = to_row(part)
    high = part.astype(bf16).astype(f32)
    low = part - high
    rest = ROWS - HD
    zeros = jnp.zeros((1, HD - rest), f32)
    lines = [
        high[:, :HD],
        jnp.concatenate([high[:, HD:], zeros], axis=1),
        low[:, :HD],
        jnp.concatenate([low[:, HD:], zeros], axis=1),
        jnp.zeros((BY_X - 4, HD), f32),
    ]
    lines = jnp.concatenate(lines, axis=0).astype(bf16)
    stores = [store]
    for x in range(NX):
        pieces_ref[x, :, pl.ds(0, D)] = wide[pl.ds(x * BY_X, BY_X), :].astype(bf16)
        pieces_ref[x, :, pl.ds(D, HD)] = lines
        stores += start(sems.at[pl.ds(2 + x, 1)], (pieces_ref.at[x], pieces_hbm.at[x]))
    wait(stores)


def input_kernel(
    frames_ref, partner_ref, moved_ref,
    weight_ref, got_ref, scaled_hbm, layer_hbm,
    even_ref, odd_ref, layer_out_ref,
    scaled_ref, layer_ref, sems,
):
    fetch = start(sems, (scaled_hbm, scaled_ref), (layer_hbm, layer_ref))
    kept, incoming, holds_two = my_counts(frames_ref, partner_ref, moved_ref)
    block = lax.axis_index("y") * NC + lax.axis_index("c")
    fetch[0].wait()
    scaled = scaled_ref[...]
    for index, other in enumerate(EVEN):
        for ref, partner in ((even_ref, other), (odd_ref, other + 1)):
            first = pl.multiple_of((block ^ partner) * HD, HD)
            part = dot(weight_ref[:, pl.ds(first, HD)], scaled, ROWS_BY_COLS)
            ref[pl.ds(index * HD, HD), :] = part.astype(bf16)
    fetch[1].wait()
    received = dot(got_ref[pl.ds(0, ROWS), :], light_places(kept, incoming), COLS_BY_COLS)
    own = layer_ref[:, pl.ds(0, BAL_ROWS)].astype(f32)
    keep = positions((ROWS, BAL_ROWS), 1) < kept
    layer_out_ref[...] = jnp.where(keep, own, received).astype(bf16)


def slots_kernel(pieces_ref, by_slot_ref, scale_ref):
    total = pieces_ref[0].astype(f32)
    for x in range(1, NX):
        total = total + pieces_ref[x].astype(f32)
    for slot in range(HEADS):
        part = total[:, slot * ROWS : (slot + 1) * ROWS]
        for z in range(NZ):
            by_slot_ref[z * HEADS + slot] = part[z * BY_ZX : (z + 1) * BY_ZX, :].astype(bf16)
    lines = total[0:2, D:] + total[2:4, D:]
    high = lines.astype(bf16).astype(f32)
    scale_ref[...] = jnp.concatenate([high, lines - high], axis=0).astype(bf16)


def spread_kernel(owned_ref, scale_ref, copies_hbm, joined, whole, sems):
    for block in range(N_FSDP):
        total = owned_ref[block].astype(f32)
        for z in range(1, NZ):
            total = total + owned_ref[z * N_FSDP + block].astype(f32)
        joined[:, pl.ds(block * ROWS, ROWS)] = total
    joined[:, pl.ds(D, HD)] = scale_ref[...].astype(f32)
    whole[...] = joined[...].astype(bf16)
    wait(start(sems, *[(whole, copies_hbm.at[z]) for z in range(NZ)]))


def join_kernel(pieces_ref, copies_hbm, scale_grad_ref, joined, whole, sems):
    for z in range(NZ):
        joined[pl.ds(z * BY_ZX, BY_ZX), :] = pieces_ref[z, :, pl.ds(0, D)].astype(f32)
    whole[...] = joined[...].astype(bf16)
    copies = start(sems, *[(whole, copies_hbm.at[x]) for x in range(NX)])
    lines = pieces_ref[0, :, pl.ds(D, HD)].astype(f32)
    for z in range(1, NZ):
        lines = lines + pieces_ref[z, :, pl.ds(D, HD)].astype(f32)
    lines = lines[0:2, :] + lines[2:4, :]
    scale_grad_ref[...] = jnp.concatenate([lines[0:1, :], lines[1:2, : ROWS - HD]], axis=1)
    wait(copies)


def ortho_kernel(grad_ref, out_ref):
    def mul(a, b):
        return jnp.dot(a, b, precision=lax.Precision.HIGHEST, preferred_element_type=f32)

    grad = grad_ref[...]
    gram = dot(grad, grad, COLS_BY_COLS)
    eye = jnp.where(same(HD), 1.0, 0.0).astype(f32)
    squares = jnp.sum(jnp.sum(gram * eye, axis=1, keepdims=True), axis=0, keepdims=True)
    norm = jnp.sqrt(squares) + EPSILON
    gram = gram / norm / norm
    total = None
    for sweep in range(ITERS):
        step = coeff_linear * eye + coeff_square * gram + coeff_cubic * mul(gram, gram)
        total = step if total is None else mul(total, step)
        if sweep < ITERS - 1:
            gram = mul(mul(step, gram), step)
    total = total * (0.2 * math.sqrt(D) / norm)
    high = total.astype(bf16)
    low = (total - high.astype(f32)).astype(bf16)
    out = dot(grad, high, ROWS_BY_COLS) + dot(grad, low, ROWS_BY_COLS)
    out_ref[...] = out.astype(bf16)


S, V, H = pltpu.SMEM, pltpu.VMEM, pltpu.HBM


def call(kernel, name, places, arrays, outs, scratch=()):
    arrays = [
        pltpu.with_memory_space_constraint(array, H) if place is H else array
        for array, place in zip(arrays, places)
    ]
    return pl.pallas_call(
        kernel,
        out_shape=[
            H(shape, dtype) if place is H else jax.ShapeDtypeStruct(shape, dtype)
            for shape, dtype, place in outs
        ],
        in_specs=[pl.BlockSpec(memory_space=place) for place in places],
        out_specs=[pl.BlockSpec(memory_space=place) for shape, dtype, place in outs],
        scratch_shapes=list(scratch),
        compiler_params=pltpu.CompilerParams(vmem_limit_bytes=32 * 1024 * 1024),
        name=name,
    )(*arrays)


def exchange(pieces, axes):
    return lax.all_to_all(pieces, axes, split_axis=0, concat_axis=0, tiled=True)


def crossed(array, axis, size, bit):
    return lax.ppermute(array, axis, [(i, i ^ bit) for i in range(size)])


def add(a, b):
    return (a.astype(f32) + b.astype(f32)).astype(bf16)


EVEN = (0, 8, 4, 12, 2, 10, 6, 14)


def sum_blocks(even, odd):
    left = add(even, crossed(odd, "c", NC, 1))
    for bit in (1, 2, 4):
        half = left.shape[0] // 2
        left = add(left[:half], crossed(left[half:], "y", NY, bit))
    return left


def body(
    attended, residual, grad_out, out_weight, layer_scale, frames, partner, moved_tiles, owner_slot
):
    scale_row = layer_scale[None, :]
    ints = pltpu.SMEM((N_DP,), jnp.int32)
    dma = pltpu.SemaphoreType.DMA

    projected, layer_own, window = call(
        project_kernel, "project", [H] * 8,
        (frames, partner, moved_tiles, attended, residual, grad_out, out_weight, scale_row),
        [((ROWS, CAP_ROWS), f32, H), ((ROWS, CAP_ROWS), bf16, H), ((PAD_ROWS, MOVE_ROWS), bf16, H)],
        [
            ints, ints, ints,
            V((A, CAP_ROWS), bf16), V((ROWS, CAP_ROWS), bf16), V((ROWS, BAL_ROWS), bf16),
            V((ROWS, A), bf16), V((1, ROWS), f32),
            V((ROWS, CAP_ROWS), f32), V((ROWS, CAP_ROWS), bf16), V((PAD_ROWS, MOVE_ROWS), bf16),
            dma((6,)), dma((A // CHUNK,)), dma((A // CHUNK,)), dma((3,)),
        ],
    )
    pieces = exchange(window.reshape(N_DP, PAD_ROWS // N_DP, MOVE_ROWS), ("z", "x"))
    pieces = exchange(jnp.take(pieces, partner, axis=0), ("z", "x"))
    got = pieces.reshape(PAD_ROWS, MOVE_ROWS)

    scaled, pieces = call(
        weight_grad_kernel, "weight_grad", [S] * 4 + [V] * 4 + [H],
        (frames, partner, moved_tiles, owner_slot, attended, grad_out, scale_row, got, projected),
        [((ROWS, CAP_ROWS), bf16, H), ((NX, BY_X, WIDE), bf16, H)],
        [
            pltpu.SMEM((HEADS,), jnp.int32), V((HD, D), f32),
            V((ROWS, CAP_ROWS), f32), V((ROWS, CAP_ROWS), bf16),
            V((NX, BY_X, WIDE), bf16), dma((2 + NX,)),
        ],
    )
    pieces = exchange(pieces, "x")

    half = ((A // 2, CAP_ROWS), bf16, V)
    even, odd, layer_out = call(
        input_kernel, "input_grad", [S] * 3 + [V] * 2 + [H] * 2,
        (frames, partner, moved_tiles, out_weight, got, scaled, layer_own),
        [half, half, ((ROWS, BAL_ROWS), bf16, V)],
        [V((ROWS, CAP_ROWS), bf16), V((ROWS, CAP_ROWS), bf16), dma((2,))],
    )
    input_grad = sum_blocks(even, odd)

    by_slot, scale_lines = call(
        slots_kernel, "slots", [V], (pieces,),
        [((NZ * HEADS, BY_ZX, ROWS), bf16, V), ((4, HD), bf16, V)],
    )
    owned = exchange(by_slot, ("z", "y", "c"))
    (copies,) = call(
        spread_kernel, "spread", [V] * 2, (owned, scale_lines),
        [((NZ, BY_ZX, WIDE), bf16, H)],
        [V((BY_ZX, WIDE), f32), V((BY_ZX, WIDE), bf16), dma((NZ,))],
    )
    copies, scale_grad = call(
        join_kernel, "join", [V], (exchange(copies, "z"),),
        [((NX, BY_X, D), bf16, H), ((1, ROWS), f32, V)],
        [V((BY_X, D), f32), V((BY_X, D), bf16), dma((NX,))],
    )
    whole = exchange(copies, "x").reshape(HD, D)
    (ortho_update,) = call(ortho_kernel, "ortho", [V], (whole,), [((D, HD), bf16, V)])
    return (layer_out, input_grad, scale_grad.reshape(ROWS), ortho_update[:, None, :])


def solution(mesh):
    chips = Mesh(mesh.devices.reshape(NZ, NX, NY, NC), ("z", "x", "y", "c"))
    dp, fsdp = ("z", "x"), ("y", "c")
    placed = (
        P(None, dp),
        P(fsdp, dp),
        P(fsdp, dp),
        P(fsdp, None),
        P(fsdp),
        P(),
        P(),
        P(),
        P(),
    )
    return jax.shard_map(
        body,
        mesh=chips,
        in_specs=placed,
        out_specs=(P(fsdp, dp), P(fsdp, dp), P(fsdp), P(None, fsdp, None)),
        check_vma=False,
    )
```

```python
import math

import jax
import jax.numpy as jnp
from jax import lax
from jax.experimental import pallas as pl
from jax.experimental.pallas import tpu as pltpu
from jax.sharding import Mesh, PartitionSpec as P

D = 3200
HEADS = 16
HD = 128
FRAME = 256
TILE = 16
ITERS = 5
A = 2048
CAP_ROWS = 512
MOVE_ROWS = 256
BAL_ROWS = 384
N_DP = 32
N_FSDP = 16

NZ, NX, NY, NC = 8, 4, 8, 2
ROWS = D // N_FSDP
BY_X = HD // NX
SHARE = HD // N_DP
WIDE = D + HD
PAD_ROWS = 256
CHUNK = 512

coeff_linear = 3.4445
coeff_square = -4.775
coeff_cubic = 2.0315
EPSILON = 1e-07
INVERSE_ROOT = 1.0 / math.sqrt(N_DP * BAL_ROWS)

bf16 = jnp.bfloat16
f32 = jnp.float32

ROWS_BY_COLS = (((0,), (0,)), ((), ()))
COLS_BY_COLS = (((1,), (1,)), ((), ()))


def positions(shape, dimension):
    return lax.broadcasted_iota(jnp.int32, shape, dimension)


def dot(a, b, dims=(((1,), (0,)), ((), ()))):
    return lax.dot_general(a, b, dims, preferred_element_type=f32)


def same(size):
    return positions((size, size), 0) == positions((size, size), 1)


def to_column(row):
    size = row.shape[1]
    return jnp.sum(jnp.where(same(size), row, 0.0), axis=1, keepdims=True)


def to_row(column):
    size = column.shape[0]
    return jnp.sum(jnp.where(same(size), column, 0.0), axis=0, keepdims=True)


def my_counts(frames_ref, partner_ref, moved_ref):
    replica = lax.axis_index("z") * NX + lax.axis_index("x")
    mate = partner_ref[replica]
    kept = frames_ref[replica] * FRAME - moved_ref[replica] * TILE
    incoming = moved_ref[mate] * TILE
    holds_two = (frames_ref[replica] > frames_ref[mate]).astype(jnp.int32)
    return kept, incoming, holds_two


def light_places(kept, incoming):
    bal_col = positions((BAL_ROWS, MOVE_ROWS), 0)
    win_col = positions((BAL_ROWS, MOVE_ROWS), 1)
    hit = bal_col == win_col + (kept + incoming - MOVE_ROWS)
    hit = hit & (win_col >= MOVE_ROWS - incoming)
    return jnp.where(hit, 1.0, 0.0).astype(bf16)


def start(sems, *pairs):
    copies = [pltpu.make_async_copy(a, b, sems.at[i]) for i, (a, b) in enumerate(pairs)]
    for copy in copies:
        copy.start()
    return copies


def wait(copies):
    for copy in copies:
        copy.wait()


def project_kernel(
    frames_hbm, partner_hbm, moved_hbm,
    attended_hbm, residual_hbm, grad_hbm, weight_hbm, scale_hbm,
    projected_hbm, layer_hbm, window_hbm,
    frames_ref, partner_ref, moved_ref,
    attended_ref, residual_ref, grad_ref, weight_ref, scale_ref,
    projected_ref, layer_ref, window_ref,
    small_sems, attended_sems, weight_sems, out_sems,
):
    small = start(
        small_sems,
        (frames_hbm, frames_ref),
        (partner_hbm, partner_ref),
        (moved_hbm, moved_ref),
        (scale_hbm, scale_ref),
        (grad_hbm, grad_ref),
        (residual_hbm, residual_ref),
    )
    cuts = [pl.ds(first, CHUNK) for first in range(0, A, CHUNK)]
    attended = start(
        attended_sems, *[(attended_hbm.at[cut, :], attended_ref.at[cut, :]) for cut in cuts]
    )
    weight = start(
        weight_sems, *[(weight_hbm.at[:, cut], weight_ref.at[:, cut]) for cut in cuts]
    )
    wait(small[:5])
    kept, incoming, holds_two = my_counts(frames_ref, partner_ref, moved_ref)
    gains = to_column(scale_ref[...])
    grad_win = dot(grad_ref[...], light_places(kept, incoming))
    window_ref[pl.ds(ROWS, PAD_ROWS - ROWS), :] = jnp.zeros(
        (PAD_ROWS - ROWS, MOVE_ROWS), bf16
    )
    projected = None
    for index, cut in enumerate(cuts):
        attended[index].wait()
        weight[index].wait()
        part = dot(weight_ref[:, cut], attended_ref[cut, :])
        projected = part if projected is None else projected + part
    small[5].wait()
    layer = (residual_ref[...].astype(f32) + gains * projected).astype(bf16)
    layer_win = layer[:, MOVE_ROWS:].astype(f32)
    window_ref[pl.ds(0, ROWS), :] = jnp.where(holds_two == 1, layer_win, grad_win).astype(bf16)
    out = start(out_sems, (window_ref, window_hbm))
    projected_ref[...] = projected
    layer_ref[...] = layer
    out += start(
        out_sems.at[pl.ds(1, 2)], (projected_ref, projected_hbm), (layer_ref, layer_hbm)
    )
    wait(out)


def weight_grad_kernel(
    frames_ref, partner_ref, moved_ref, slot_ref,
    attended_ref, grad_ref, scale_ref, got_ref, projected_hbm,
    scaled_hbm, pieces_hbm,
    head_of, wide, projected_ref, scaled_ref, pieces_ref, sems,
):
    (fetch,) = start(sems, (projected_hbm, projected_ref))
    kept, incoming, holds_two = my_counts(frames_ref, partner_ref, moved_ref)
    for head in range(HEADS):
        head_of[slot_ref[head]] = head
    own = grad_ref[...].astype(f32)
    own = jnp.concatenate([own, jnp.zeros((ROWS, CAP_ROWS - BAL_ROWS), f32)], axis=1)
    got = got_ref[pl.ds(0, ROWS), :].astype(f32)
    got = jnp.where(holds_two == 1, got, 0.0)
    got = jnp.concatenate([jnp.zeros((ROWS, CAP_ROWS - MOVE_ROWS), f32), got], axis=1)
    grad = jnp.where(positions((ROWS, CAP_ROWS), 1) < kept, own, got)
    scaled = (grad * to_column(scale_ref[...])).astype(bf16)
    scaled_ref[...] = scaled
    (store,) = start(sems.at[pl.ds(1, 1)], (scaled_ref, scaled_hbm))
    for slot in range(HEADS):
        first = pl.multiple_of(head_of[slot] * HD, HD)
        wide[:, pl.ds(slot * ROWS, ROWS)] = dot(
            attended_ref[pl.ds(first, HD), :], scaled, COLS_BY_COLS
        )
    fetch.wait()
    part = jnp.sum(grad * projected_ref[...], axis=1, keepdims=True) * INVERSE_ROOT
    part = to_row(part)
    high = part.astype(bf16).astype(f32)
    low = part - high
    zeros = jnp.zeros((1, 2 * HD - ROWS), f32)
    lines = [
        high[:, :HD],
        jnp.concatenate([high[:, HD:], zeros], axis=1),
        low[:, :HD],
        jnp.concatenate([low[:, HD:], zeros], axis=1),
    ]
    wide[:, pl.ds(D, HD)] = jnp.concatenate(lines * N_DP, axis=0)
    stores = [store]
    for z in range(NZ):
        for x in range(NX):
            pieces_ref[z * NX + x] = wide[pl.ds((x * NZ + z) * SHARE, SHARE), :].astype(bf16)
        cut = pl.ds(z * NX, NX)
        stores += start(sems.at[pl.ds(2 + z, 1)], (pieces_ref.at[cut], pieces_hbm.at[cut]))
    wait(stores)


def input_kernel(
    frames_ref, partner_ref, moved_ref,
    weight_ref, got_ref, scaled_hbm, layer_hbm,
    even_ref, odd_ref, layer_out_ref,
    scaled_ref, layer_ref, sems,
):
    fetch = start(sems, (scaled_hbm, scaled_ref), (layer_hbm, layer_ref))
    kept, incoming, holds_two = my_counts(frames_ref, partner_ref, moved_ref)
    block = lax.axis_index("y") * NC + lax.axis_index("c")
    fetch[0].wait()
    scaled = scaled_ref[...]
    for index, other in enumerate(EVEN):
        for ref, partner in ((even_ref, other), (odd_ref, other + 1)):
            first = pl.multiple_of((block ^ partner) * HD, HD)
            part = dot(weight_ref[:, pl.ds(first, HD)], scaled, ROWS_BY_COLS)
            ref[pl.ds(index * HD, HD), :] = part.astype(bf16)
    fetch[1].wait()
    received = dot(got_ref[pl.ds(0, ROWS), :], light_places(kept, incoming), COLS_BY_COLS)
    own = layer_ref[:, pl.ds(0, BAL_ROWS)].astype(f32)
    keep = positions((ROWS, BAL_ROWS), 1) < kept
    layer_out_ref[...] = jnp.where(keep, own, received).astype(bf16)


def slots_kernel(pieces_ref, copies_hbm, scale_grad_ref, by_slot, sems):
    total = pieces_ref[0].astype(f32)
    for piece in range(1, N_DP):
        total = total + pieces_ref[piece].astype(f32)
    for slot in range(HEADS):
        by_slot[slot] = total[:, slot * ROWS : (slot + 1) * ROWS].astype(bf16)
    copies = [
        (by_slot, copies_hbm.at[pl.ds(z * HEADS, HEADS)]) for z in range(NZ)
    ]
    copies = start(sems, *copies)
    lines = total[0:2, D:] + total[2:4, D:]
    scale_grad_ref[...] = jnp.concatenate([lines[0:1, :], lines[1:2, : ROWS - HD]], axis=1)
    wait(copies)


def join_kernel(owned_ref, copies_hbm, joined, whole, sems):
    for z in range(NZ):
        for block in range(N_FSDP):
            joined[pl.ds(z * SHARE, SHARE), pl.ds(block * ROWS, ROWS)] = owned_ref[
                z * N_FSDP + block
            ].astype(f32)
    whole[...] = joined[...].astype(bf16)
    wait(start(sems, *[(whole, copies_hbm.at[x]) for x in range(NX)]))


def ortho_kernel(grad_ref, out_ref):
    def mul(a, b):
        return jnp.dot(a, b, precision=lax.Precision.HIGHEST, preferred_element_type=f32)

    grad = grad_ref[...]
    gram = dot(grad, grad, COLS_BY_COLS)
    eye = jnp.where(same(HD), 1.0, 0.0).astype(f32)
    squares = jnp.sum(jnp.sum(gram * eye, axis=1, keepdims=True), axis=0, keepdims=True)
    norm = jnp.sqrt(squares) + EPSILON
    gram = gram / norm / norm
    total = None
    for sweep in range(ITERS):
        step = coeff_linear * eye + coeff_square * gram + coeff_cubic * mul(gram, gram)
        total = step if total is None else mul(total, step)
        if sweep < ITERS - 1:
            gram = mul(mul(step, gram), step)
    total = total * (0.2 * math.sqrt(D) / norm)
    high = total.astype(bf16)
    low = (total - high.astype(f32)).astype(bf16)
    out = dot(grad, high, ROWS_BY_COLS) + dot(grad, low, ROWS_BY_COLS)
    out_ref[...] = out.astype(bf16)


S, V, H = pltpu.SMEM, pltpu.VMEM, pltpu.HBM
FREE = pl.CostEstimate(flops=0, bytes_accessed=0, transcendentals=0)


def call(kernel, name, places, arrays, outs, scratch=(), cost=None):
    arrays = [
        pltpu.with_memory_space_constraint(array, H) if place is H else array
        for array, place in zip(arrays, places)
    ]
    return pl.pallas_call(
        kernel,
        out_shape=[
            H(shape, dtype) if place is H else jax.ShapeDtypeStruct(shape, dtype)
            for shape, dtype, place in outs
        ],
        in_specs=[pl.BlockSpec(memory_space=place) for place in places],
        out_specs=[pl.BlockSpec(memory_space=place) for shape, dtype, place in outs],
        scratch_shapes=list(scratch),
        compiler_params=pltpu.CompilerParams(vmem_limit_bytes=32 * 1024 * 1024),
        name=name,
        cost_estimate=cost,
    )(*arrays)


def exchange(pieces, axes):
    return lax.all_to_all(pieces, axes, split_axis=0, concat_axis=0, tiled=True)


def crossed(array, axis, size, bit):
    return lax.ppermute(array, axis, [(i, i ^ bit) for i in range(size)])


EVEN = (0, 8, 4, 12, 2, 10, 6, 14)


def add_kernel(left_ref, other_ref, *out_refs):
    rows = left_ref.shape[0] // len(out_refs)
    for index, out_ref in enumerate(out_refs):
        cut = pl.ds(index * rows, rows)
        total = left_ref[cut, :].astype(f32) + other_ref[cut, :].astype(f32)
        out_ref[...] = total.astype(bf16)


def add(left, other, parts):
    rows = left.shape[0] // parts
    return call(
        add_kernel, "add", [V] * 2, (left, other),
        [((rows, CAP_ROWS), bf16, V)] * parts, cost=FREE,
    )


def body(
    attended, residual, grad_out, out_weight, layer_scale, frames, partner, moved_tiles, owner_slot
):
    scale_row = layer_scale[None, :]
    ints = pltpu.SMEM((N_DP,), jnp.int32)
    dma = pltpu.SemaphoreType.DMA

    projected, layer_own, window = call(
        project_kernel, "project", [H] * 8,
        (frames, partner, moved_tiles, attended, residual, grad_out, out_weight, scale_row),
        [((ROWS, CAP_ROWS), f32, H), ((ROWS, CAP_ROWS), bf16, H), ((PAD_ROWS, MOVE_ROWS), bf16, H)],
        [
            ints, ints, ints,
            V((A, CAP_ROWS), bf16), V((ROWS, CAP_ROWS), bf16), V((ROWS, BAL_ROWS), bf16),
            V((ROWS, A), bf16), V((1, ROWS), f32),
            V((ROWS, CAP_ROWS), f32), V((ROWS, CAP_ROWS), bf16), V((PAD_ROWS, MOVE_ROWS), bf16),
            dma((6,)), dma((A // CHUNK,)), dma((A // CHUNK,)), dma((3,)),
        ],
    )
    pieces = exchange(window.reshape(N_DP, PAD_ROWS // N_DP, MOVE_ROWS), ("z", "x"))
    pieces = exchange(jnp.take(pieces, partner, axis=0), ("z", "x"))
    got = pieces.reshape(PAD_ROWS, MOVE_ROWS)

    scaled, pieces = call(
        weight_grad_kernel, "weight_grad", [S] * 4 + [V] * 4 + [H],
        (frames, partner, moved_tiles, owner_slot, attended, grad_out, scale_row, got, projected),
        [((ROWS, CAP_ROWS), bf16, H), ((N_DP, SHARE, WIDE), bf16, H)],
        [
            pltpu.SMEM((HEADS,), jnp.int32), V((HD, WIDE), f32),
            V((ROWS, CAP_ROWS), f32), V((ROWS, CAP_ROWS), bf16),
            V((N_DP, SHARE, WIDE), bf16), dma((2 + NZ,)),
        ],
    )
    summed = exchange(pieces, ("z", "x"))

    half = ((A // 2, CAP_ROWS), bf16, V)
    even, odd, layer_out = call(
        input_kernel, "input_grad", [S] * 3 + [V] * 2 + [H] * 2,
        (frames, partner, moved_tiles, out_weight, got, scaled, layer_own),
        [half, half, ((ROWS, BAL_ROWS), bf16, V)],
        [V((ROWS, CAP_ROWS), bf16), V((ROWS, CAP_ROWS), bf16), dma((2,))],
        FREE,
    )
    left, other = add(even, crossed(odd, "c", NC, 1), 2)
    summed, _ = lax.optimization_barrier((summed, left))
    copies, scale_grad = call(
        slots_kernel, "slots", [V], (summed,),
        [((NZ * HEADS, SHARE, ROWS), bf16, H), ((1, ROWS), f32, V)],
        [V((HEADS, SHARE, ROWS), bf16), dma((NZ,))],
    )
    owned = exchange(copies, ("z", "y", "c"))
    left, other = add(left, crossed(other, "y", NY, 1), 2)
    left, other = add(left, crossed(other, "y", NY, 2), 2)
    owned, _ = lax.optimization_barrier((owned, left))
    (copies,) = call(
        join_kernel, "join", [V], (owned,),
        [((NX, BY_X, D), bf16, H)],
        [V((BY_X, D), f32), V((BY_X, D), bf16), dma((NX,))],
    )
    other = crossed(other, "y", NY, 4)
    whole = exchange(copies, "x").reshape(HD, D)
    (ortho_update,) = call(ortho_kernel, "ortho", [V], (whole,), [((D, HD), bf16, V)])
    left, other, ortho_update = lax.optimization_barrier((left, other, ortho_update))
    (input_grad,) = add(left, other, 1)
    return (layer_out, input_grad, scale_grad.reshape(ROWS), ortho_update[:, None, :])


def solution(mesh):
    chips = Mesh(mesh.devices.reshape(NZ, NX, NY, NC), ("z", "x", "y", "c"))
    dp, fsdp = ("z", "x"), ("y", "c")
    placed = (
        P(None, dp),
        P(fsdp, dp),
        P(fsdp, dp),
        P(fsdp, None),
        P(fsdp),
        P(),
        P(),
        P(),
        P(),
    )
    return jax.shard_map(
        body,
        mesh=chips,
        in_specs=placed,
        out_specs=(P(fsdp, dp), P(fsdp, dp), P(fsdp), P(None, fsdp, None)),
        check_vma=False,
    )
```

```python
import functools
import math

import jax
import jax.numpy as jnp
from jax import lax
from jax.experimental import pallas as pl
from jax.experimental.pallas import tpu as pltpu
from jax.sharding import Mesh, PartitionSpec as P

D = 3200
HEADS = 16
HD = 128
FRAME = 256
TILE = 16
ITERS = 5
A = 2048
CAP_ROWS = 512
MOVE_ROWS = 256
BAL_ROWS = 384
N_DP = 32
N_FSDP = 16

NZ, NX, NY, NC = 8, 4, 8, 2
ROWS = D // N_FSDP
BY_X = HD // NX
SHARE = HD // N_DP
HALF = D // NC
WIDE = 14 * HD
PAD_ROWS = 256
CHUNK = 512

coeff_linear = 3.4445
coeff_square = -4.775
coeff_cubic = 2.0315
EPSILON = 1e-07
INVERSE_ROOT = 1.0 / math.sqrt(N_DP * BAL_ROWS)

bf16 = jnp.bfloat16
f32 = jnp.float32

ROWS_BY_COLS = (((0,), (0,)), ((), ()))
COLS_BY_COLS = (((1,), (1,)), ((), ()))


def positions(shape, dimension):
    return lax.broadcasted_iota(jnp.int32, shape, dimension)


def dot(a, b, dims=(((1,), (0,)), ((), ()))):
    return lax.dot_general(a, b, dims, preferred_element_type=f32)


def same(size):
    return positions((size, size), 0) == positions((size, size), 1)


def to_column(row):
    size = row.shape[1]
    return jnp.sum(jnp.where(same(size), row, 0.0), axis=1, keepdims=True)


def to_row(column):
    size = column.shape[0]
    return jnp.sum(jnp.where(same(size), column, 0.0), axis=0, keepdims=True)


def my_counts(frames_ref, partner_ref, moved_ref):
    replica = lax.axis_index("z") * NX + lax.axis_index("x")
    mate = partner_ref[replica]
    kept = frames_ref[replica] * FRAME - moved_ref[replica] * TILE
    incoming = moved_ref[mate] * TILE
    holds_two = (frames_ref[replica] > frames_ref[mate]).astype(jnp.int32)
    return kept, incoming, holds_two


def light_places(kept, incoming):
    bal_col = positions((BAL_ROWS, MOVE_ROWS), 0)
    win_col = positions((BAL_ROWS, MOVE_ROWS), 1)
    hit = bal_col == win_col + (kept + incoming - MOVE_ROWS)
    hit = hit & (win_col >= MOVE_ROWS - incoming)
    return jnp.where(hit, 1.0, 0.0).astype(bf16)


def start(sems, *pairs):
    copies = [pltpu.make_async_copy(a, b, sems.at[i]) for i, (a, b) in enumerate(pairs)]
    for copy in copies:
        copy.start()
    return copies


def wait(copies):
    for copy in copies:
        copy.wait()


def project_kernel(
    frames_hbm, partner_hbm, moved_hbm,
    attended_hbm, residual_hbm, grad_hbm, weight_hbm, scale_hbm,
    projected_hbm, layer_hbm, window_hbm,
    frames_ref, partner_ref, moved_ref,
    attended_ref, residual_ref, grad_ref, weight_ref, scale_ref,
    projected_ref, layer_ref, window_ref,
    small_sems, attended_sems, weight_sems, out_sems,
):
    small = start(
        small_sems,
        (frames_hbm, frames_ref),
        (partner_hbm, partner_ref),
        (moved_hbm, moved_ref),
        (scale_hbm, scale_ref),
        (grad_hbm, grad_ref),
        (residual_hbm, residual_ref),
    )
    cuts = [pl.ds(first, CHUNK) for first in range(0, A, CHUNK)]
    attended = start(
        attended_sems, *[(attended_hbm.at[cut, :], attended_ref.at[cut, :]) for cut in cuts]
    )
    weight = start(
        weight_sems, *[(weight_hbm.at[:, cut], weight_ref.at[:, cut]) for cut in cuts]
    )
    wait(small[:5])
    kept, incoming, holds_two = my_counts(frames_ref, partner_ref, moved_ref)
    gains = to_column(scale_ref[...])
    grad_win = dot(grad_ref[...], light_places(kept, incoming))
    window_ref[pl.ds(ROWS, PAD_ROWS - ROWS), :] = jnp.zeros(
        (PAD_ROWS - ROWS, MOVE_ROWS), bf16
    )
    projected = None
    for index, cut in enumerate(cuts):
        attended[index].wait()
        weight[index].wait()
        part = dot(weight_ref[:, cut], attended_ref[cut, :])
        projected = part if projected is None else projected + part
    small[5].wait()
    layer = (residual_ref[...].astype(f32) + gains * projected).astype(bf16)
    layer_win = layer[:, MOVE_ROWS:].astype(f32)
    window_ref[pl.ds(0, ROWS), :] = jnp.where(holds_two == 1, layer_win, grad_win).astype(bf16)
    out = start(out_sems, (window_ref, window_hbm))
    projected_ref[...] = projected
    layer_ref[...] = layer
    out += start(
        out_sems.at[pl.ds(1, 2)], (projected_ref, projected_hbm), (layer_ref, layer_hbm)
    )
    wait(out)


def weight_grad_kernel(
    frames_ref, partner_ref, moved_ref, slot_ref,
    attended_ref, grad_ref, scale_ref, got_ref, projected_hbm,
    scaled_hbm, pieces_hbm,
    head_of, wide, projected_ref, scaled_ref, pieces_ref, sems,
):
    (fetch,) = start(sems, (projected_hbm, projected_ref))
    kept, incoming, holds_two = my_counts(frames_ref, partner_ref, moved_ref)
    for head in range(HEADS):
        head_of[slot_ref[head]] = head
    own = grad_ref[...].astype(f32)
    own = jnp.concatenate([own, jnp.zeros((ROWS, CAP_ROWS - BAL_ROWS), f32)], axis=1)
    got = got_ref[pl.ds(0, ROWS), :].astype(f32)
    got = jnp.where(holds_two == 1, got, 0.0)
    got = jnp.concatenate([jnp.zeros((ROWS, CAP_ROWS - MOVE_ROWS), f32), got], axis=1)
    grad = jnp.where(positions((ROWS, CAP_ROWS), 1) < kept, own, got)
    scaled = (grad * to_column(scale_ref[...])).astype(bf16)
    scaled_ref[...] = scaled
    (store,) = start(sems.at[pl.ds(1, 1)], (scaled_ref, scaled_hbm))
    for y in range(NY):
        for c in range(NC):
            first = pl.multiple_of(head_of[y * NC + c] * HD, HD)
            wide[c, :, pl.ds(y * ROWS, ROWS)] = dot(
                attended_ref[pl.ds(first, HD), :], scaled, COLS_BY_COLS
            )
    fetch.wait()
    part = jnp.sum(grad * projected_ref[...], axis=1, keepdims=True) * INVERSE_ROOT
    part = to_row(part)
    high = part.astype(bf16).astype(f32)
    low = part - high
    zeros = jnp.zeros((1, 2 * HD - ROWS), f32)
    lines = [
        high[:, :HD],
        jnp.concatenate([high[:, HD:], zeros], axis=1),
        low[:, :HD],
        jnp.concatenate([low[:, HD:], zeros], axis=1),
    ]
    lines = jnp.concatenate(lines * N_DP, axis=0)
    for c in range(NC):
        wide[c, :, pl.ds(HALF, WIDE - HD - HALF)] = jnp.zeros((HD, WIDE - HD - HALF), f32)
        wide[c, :, pl.ds(WIDE - HD, HD)] = lines
    stores = [store]
    for z in range(NZ):
        for x in range(NX):
            cut = pl.ds((x * NZ + z) * SHARE, SHARE)
            for c in range(NC):
                pieces_ref[(z * NX + x) * NC + c] = wide[c, cut, :].astype(bf16)
        cut = pl.ds(z * NX * NC, NX * NC)
        stores += start(sems.at[pl.ds(2 + z, 1)], (pieces_ref.at[cut], pieces_hbm.at[cut]))
    wait(stores)


def input_kernel(
    frames_ref, partner_ref, moved_ref,
    weight_ref, got_ref, scaled_hbm, layer_hbm,
    even_ref, odd_ref, layer_out_ref,
    scaled_ref, layer_ref, sems,
):
    fetch = start(sems, (scaled_hbm, scaled_ref), (layer_hbm, layer_ref))
    kept, incoming, holds_two = my_counts(frames_ref, partner_ref, moved_ref)
    block = lax.axis_index("y") * NC + lax.axis_index("c")
    fetch[0].wait()
    scaled = scaled_ref[...]
    for index, other in enumerate(EVEN):
        for ref, partner in ((even_ref, other), (odd_ref, other + 1)):
            first = pl.multiple_of((block ^ partner) * HD, HD)
            part = dot(weight_ref[:, pl.ds(first, HD)], scaled, ROWS_BY_COLS)
            ref[pl.ds(index * HD, HD), :] = part.astype(bf16)
    fetch[1].wait()
    received = dot(got_ref[pl.ds(0, ROWS), :], light_places(kept, incoming), COLS_BY_COLS)
    own = layer_ref[:, pl.ds(0, BAL_ROWS)].astype(f32)
    keep = positions((ROWS, BAL_ROWS), 1) < kept
    layer_out_ref[...] = jnp.where(keep, own, received).astype(bf16)


def slots_kernel(pieces_ref, copies_hbm, scale_grad_ref, by_slot, sems):
    totals = []
    for c in range(NC):
        total = pieces_ref[c].astype(f32)
        for replica in range(1, N_DP):
            total = total + pieces_ref[replica * NC + c].astype(f32)
        totals.append(total)
    for y in range(NY):
        both = [total[:, y * ROWS : (y + 1) * ROWS] for total in totals]
        by_slot[y] = jnp.concatenate(both, axis=1).astype(bf16)
    copies = [(by_slot, copies_hbm.at[pl.ds(z * NY, NY)]) for z in range(NZ)]
    copies = start(sems, *copies)
    lines = [total[0:2, WIDE - HD :] + total[2:4, WIDE - HD :] for total in totals]
    lines = jnp.where(lax.axis_index("c") == 0, lines[0], lines[1])
    scale_grad_ref[...] = jnp.concatenate([lines[0:1, :], lines[1:2, : ROWS - HD]], axis=1)
    wait(copies)


def join_kernel(owned_ref, copies_hbm, joined, whole, sems):
    for z in range(NZ):
        for y in range(NY):
            joined[pl.ds(z * SHARE, SHARE), pl.ds(y * NC * ROWS, NC * ROWS)] = owned_ref[
                z * NY + y
            ].astype(f32)
    whole[...] = joined[...].astype(bf16)
    wait(start(sems, *[(whole, copies_hbm.at[x]) for x in range(NX)]))


def ortho_kernel(grad_ref, out_ref):
    def mul(a, b):
        return jnp.dot(a, b, precision=lax.Precision.HIGHEST, preferred_element_type=f32)

    grad = grad_ref[...]
    gram = dot(grad, grad, COLS_BY_COLS)
    eye = jnp.where(same(HD), 1.0, 0.0).astype(f32)
    squares = jnp.sum(jnp.sum(gram * eye, axis=1, keepdims=True), axis=0, keepdims=True)
    norm = jnp.sqrt(squares) + EPSILON
    gram = gram / norm / norm
    total = None
    for sweep in range(ITERS):
        step = coeff_linear * eye + coeff_square * gram + coeff_cubic * mul(gram, gram)
        total = step if total is None else mul(total, step)
        if sweep < ITERS - 1:
            gram = mul(mul(step, gram), step)
    total = total * (0.2 * math.sqrt(D) / norm)
    high = total.astype(bf16)
    low = (total - high.astype(f32)).astype(bf16)
    out = dot(grad, high, ROWS_BY_COLS) + dot(grad, low, ROWS_BY_COLS)
    out_ref[...] = out.astype(bf16)


S, V, H = pltpu.SMEM, pltpu.VMEM, pltpu.HBM
FREE = pl.CostEstimate(flops=0, bytes_accessed=0, transcendentals=0)


def call(kernel, name, places, arrays, outs, scratch=(), cost=None):
    arrays = [
        pltpu.with_memory_space_constraint(array, H) if place is H else array
        for array, place in zip(arrays, places)
    ]
    return pl.pallas_call(
        kernel,
        out_shape=[
            H(shape, dtype) if place is H else jax.ShapeDtypeStruct(shape, dtype)
            for shape, dtype, place in outs
        ],
        in_specs=[pl.BlockSpec(memory_space=place) for place in places],
        out_specs=[pl.BlockSpec(memory_space=place) for shape, dtype, place in outs],
        scratch_shapes=list(scratch),
        compiler_params=pltpu.CompilerParams(vmem_limit_bytes=32 * 1024 * 1024),
        name=name,
        cost_estimate=cost,
    )(*arrays)


def exchange(pieces, axes):
    return lax.all_to_all(pieces, axes, split_axis=0, concat_axis=0, tiled=True)


def crossed(array, axis, size, bit):
    return lax.ppermute(array, axis, [(i, i ^ bit) for i in range(size)])


EVEN = (0, 8, 4, 12, 2, 10, 6, 14)


def add_kernel(*refs, parts):
    in_refs, out_refs = refs[:-parts], refs[-parts:]
    rows = in_refs[0].shape[0] // parts
    for index, out_ref in enumerate(out_refs):
        cut = pl.ds(index * rows, rows)
        total = in_refs[0][cut, :].astype(f32)
        for ref in in_refs[1:]:
            total = total + ref[cut, :].astype(f32)
        out_ref[...] = total.astype(bf16)


def add(arrays, parts):
    rows = arrays[0].shape[0] // parts
    return call(
        functools.partial(add_kernel, parts=parts), "add", [V] * len(arrays), arrays,
        [((rows, CAP_ROWS), bf16, V)] * parts, cost=FREE,
    )


def body(
    attended, residual, grad_out, out_weight, layer_scale, frames, partner, moved_tiles, owner_slot
):
    scale_row = layer_scale[None, :]
    ints = pltpu.SMEM((N_DP,), jnp.int32)
    dma = pltpu.SemaphoreType.DMA

    projected, layer_own, window = call(
        project_kernel, "project", [H] * 8,
        (frames, partner, moved_tiles, attended, residual, grad_out, out_weight, scale_row),
        [((ROWS, CAP_ROWS), f32, H), ((ROWS, CAP_ROWS), bf16, H), ((PAD_ROWS, MOVE_ROWS), bf16, H)],
        [
            ints, ints, ints,
            V((A, CAP_ROWS), bf16), V((ROWS, CAP_ROWS), bf16), V((ROWS, BAL_ROWS), bf16),
            V((ROWS, A), bf16), V((1, ROWS), f32),
            V((ROWS, CAP_ROWS), f32), V((ROWS, CAP_ROWS), bf16), V((PAD_ROWS, MOVE_ROWS), bf16),
            dma((6,)), dma((A // CHUNK,)), dma((A // CHUNK,)), dma((3,)),
        ],
    )
    pieces = exchange(window.reshape(N_DP, PAD_ROWS // N_DP, MOVE_ROWS), ("z", "x"))
    pieces = exchange(jnp.take(pieces, partner, axis=0), ("z", "x"))
    got = pieces.reshape(PAD_ROWS, MOVE_ROWS)

    scaled, pieces = call(
        weight_grad_kernel, "weight_grad", [S] * 4 + [V] * 4 + [H],
        (frames, partner, moved_tiles, owner_slot, attended, grad_out, scale_row, got, projected),
        [((ROWS, CAP_ROWS), bf16, H), ((N_DP * NC, SHARE, WIDE), bf16, H)],
        [
            pltpu.SMEM((HEADS,), jnp.int32), V((NC, HD, WIDE), f32),
            V((ROWS, CAP_ROWS), f32), V((ROWS, CAP_ROWS), bf16),
            V((N_DP * NC, SHARE, WIDE), bf16), dma((2 + NZ,)),
        ],
    )
    summed = exchange(pieces, ("z", "x", "c"))

    half = ((A // 2, CAP_ROWS), bf16, V)
    even, odd, layer_out = call(
        input_kernel, "input_grad", [S] * 3 + [V] * 2 + [H] * 2,
        (frames, partner, moved_tiles, out_weight, got, scaled, layer_own),
        [half, half, ((ROWS, BAL_ROWS), bf16, V)],
        [V((ROWS, CAP_ROWS), bf16), V((ROWS, CAP_ROWS), bf16), dma((2,))],
        FREE,
    )
    left, other = add((even, crossed(odd, "c", NC, 1)), 2)
    summed, _ = lax.optimization_barrier((summed, left))
    copies, scale_grad = call(
        slots_kernel, "slots", [V], (summed,),
        [((NZ * NY, SHARE, NC * ROWS), bf16, H), ((1, ROWS), f32, V)],
        [V((NY, SHARE, NC * ROWS), bf16), dma((NZ,))],
    )
    owned = exchange(copies, ("z", "y"))
    left, *others = add((left, crossed(other, "y", NY, 1)), 4)
    owned, _ = lax.optimization_barrier((owned, left))
    others = [crossed(other, "y", NY, step) for other, step in zip(others, (4, 2, 6))]
    (copies,) = call(
        join_kernel, "join", [V], (owned,),
        [((NX, BY_X, D), bf16, H)],
        [V((BY_X, D), f32), V((BY_X, D), bf16), dma((NX,))],
    )
    whole = exchange(copies, "x").reshape(HD, D)
    (ortho_update,) = call(ortho_kernel, "ortho", [V], (whole,), [((D, HD), bf16, V)])
    left, others, ortho_update = lax.optimization_barrier((left, others, ortho_update))
    (input_grad,) = add((left, *others), 1)
    return (layer_out, input_grad, scale_grad.reshape(ROWS), ortho_update[:, None, :])


def solution(mesh):
    chips = Mesh(mesh.devices.reshape(NZ, NX, NY, NC), ("z", "x", "y", "c"))
    dp, fsdp = ("z", "x"), ("y", "c")
    placed = (
        P(None, dp),
        P(fsdp, dp),
        P(fsdp, dp),
        P(fsdp, None),
        P(fsdp),
        P(),
        P(),
        P(),
        P(),
    )
    return jax.shard_map(
        body,
        mesh=chips,
        in_specs=placed,
        out_specs=(P(fsdp, dp), P(fsdp, dp), P(fsdp), P(None, fsdp, None)),
        check_vma=False,
    )
```

```python
import functools
import math

import jax
import jax.numpy as jnp
from jax import lax
from jax.experimental import pallas as pl
from jax.experimental.pallas import tpu as pltpu
from jax.sharding import Mesh, PartitionSpec as P

D = 3200
HEADS = 16
HD = 128
FRAME = 256
TILE = 16
ITERS = 5
A = 2048
CAP_ROWS = 512
MOVE_ROWS = 256
BAL_ROWS = 384
N_DP = 32
N_FSDP = 16

NZ, NX, NY, NC = 8, 4, 8, 2
ROWS = D // N_FSDP
BY_X = HD // NX
SHARE = HD // N_DP
WIDE = D + HD
PAD_ROWS = 256
CHUNK = 512
PARTS = 5

coeff_linear = 3.4445
coeff_square = -4.775
coeff_cubic = 2.0315
EPSILON = 1e-07
INVERSE_ROOT = 1.0 / math.sqrt(N_DP * BAL_ROWS)

bf16 = jnp.bfloat16
f32 = jnp.float32

ROWS_BY_COLS = (((0,), (0,)), ((), ()))
COLS_BY_COLS = (((1,), (1,)), ((), ()))


def positions(shape, dimension):
    return lax.broadcasted_iota(jnp.int32, shape, dimension)


def dot(a, b, dims=(((1,), (0,)), ((), ()))):
    return lax.dot_general(a, b, dims, preferred_element_type=f32)


def same(size):
    return positions((size, size), 0) == positions((size, size), 1)


def to_column(row):
    size = row.shape[1]
    return jnp.sum(jnp.where(same(size), row, 0.0), axis=1, keepdims=True)


def to_row(column):
    size = column.shape[0]
    return jnp.sum(jnp.where(same(size), column, 0.0), axis=0, keepdims=True)


def my_counts(frames_ref, partner_ref, moved_ref):
    replica = lax.axis_index("z") * NX + lax.axis_index("x")
    mate = partner_ref[replica]
    kept = frames_ref[replica] * FRAME - moved_ref[replica] * TILE
    incoming = moved_ref[mate] * TILE
    holds_two = (frames_ref[replica] > frames_ref[mate]).astype(jnp.int32)
    return kept, incoming, holds_two


def light_places(kept, incoming):
    bal_col = positions((BAL_ROWS, MOVE_ROWS), 0)
    win_col = positions((BAL_ROWS, MOVE_ROWS), 1)
    hit = bal_col == win_col + (kept + incoming - MOVE_ROWS)
    hit = hit & (win_col >= MOVE_ROWS - incoming)
    return jnp.where(hit, 1.0, 0.0).astype(bf16)


def start(sems, *pairs):
    copies = [pltpu.make_async_copy(a, b, sems.at[i]) for i, (a, b) in enumerate(pairs)]
    for copy in copies:
        copy.start()
    return copies


def wait(copies):
    for copy in copies:
        copy.wait()


def project_kernel(
    frames_hbm, partner_hbm, moved_hbm,
    attended_hbm, residual_hbm, grad_hbm, weight_hbm, scale_hbm,
    projected_hbm, layer_hbm, window_hbm,
    frames_ref, partner_ref, moved_ref,
    attended_ref, residual_ref, grad_ref, weight_ref, scale_ref,
    projected_ref, layer_ref, window_ref,
    small_sems, attended_sems, weight_sems, out_sems,
):
    small = start(
        small_sems,
        (frames_hbm, frames_ref),
        (partner_hbm, partner_ref),
        (moved_hbm, moved_ref),
        (scale_hbm, scale_ref),
        (grad_hbm, grad_ref),
        (residual_hbm, residual_ref),
    )
    cuts = [pl.ds(first, CHUNK) for first in range(0, A, CHUNK)]
    attended = start(
        attended_sems, *[(attended_hbm.at[cut, :], attended_ref.at[cut, :]) for cut in cuts]
    )
    weight = start(
        weight_sems, *[(weight_hbm.at[:, cut], weight_ref.at[:, cut]) for cut in cuts]
    )
    wait(small[:5])
    kept, incoming, holds_two = my_counts(frames_ref, partner_ref, moved_ref)
    gains = to_column(scale_ref[...])
    grad_win = dot(grad_ref[...], light_places(kept, incoming))
    window_ref[pl.ds(ROWS, PAD_ROWS - ROWS), :] = jnp.zeros(
        (PAD_ROWS - ROWS, MOVE_ROWS), bf16
    )
    projected = None
    for index, cut in enumerate(cuts):
        attended[index].wait()
        weight[index].wait()
        part = dot(weight_ref[:, cut], attended_ref[cut, :])
        projected = part if projected is None else projected + part
    small[5].wait()
    layer = (residual_ref[...].astype(f32) + gains * projected).astype(bf16)
    layer_win = layer[:, MOVE_ROWS:].astype(f32)
    window_ref[pl.ds(0, ROWS), :] = jnp.where(holds_two == 1, layer_win, grad_win).astype(bf16)
    out = start(out_sems, (window_ref, window_hbm))
    projected_ref[...] = projected
    layer_ref[...] = layer
    out += start(
        out_sems.at[pl.ds(1, 2)], (projected_ref, projected_hbm), (layer_ref, layer_hbm)
    )
    wait(out)


def weight_grad_kernel(
    frames_ref, partner_ref, moved_ref, slot_ref,
    attended_ref, grad_ref, scale_ref, got_ref, projected_hbm,
    scaled_hbm, pieces_hbm,
    head_of, product, wide, projected_ref, scaled_ref, pieces_ref, sems,
):
    (fetch,) = start(sems, (projected_hbm, projected_ref))
    kept, incoming, holds_two = my_counts(frames_ref, partner_ref, moved_ref)
    for head in range(HEADS):
        head_of[slot_ref[head]] = head
    own = grad_ref[...].astype(f32)
    own = jnp.concatenate([own, jnp.zeros((ROWS, CAP_ROWS - BAL_ROWS), f32)], axis=1)
    got = got_ref[pl.ds(0, ROWS), :].astype(f32)
    got = jnp.where(holds_two == 1, got, 0.0)
    got = jnp.concatenate([jnp.zeros((ROWS, CAP_ROWS - MOVE_ROWS), f32), got], axis=1)
    grad = jnp.where(positions((ROWS, CAP_ROWS), 1) < kept, own, got)
    scaled = (grad * to_column(scale_ref[...])).astype(bf16)
    scaled_ref[...] = scaled
    (store,) = start(sems.at[pl.ds(1, 1)], (scaled_ref, scaled_hbm))
    product[...] = dot(attended_ref[...], scaled, COLS_BY_COLS)
    for slot in range(HEADS):
        first = pl.multiple_of(head_of[slot] * HD, HD)
        wide[:, pl.ds(slot * ROWS, ROWS)] = product[pl.ds(first, HD), :]
    fetch.wait()
    part = jnp.sum(grad * projected_ref[...], axis=1, keepdims=True) * INVERSE_ROOT
    part = to_row(part)
    high = part.astype(bf16).astype(f32)
    low = part - high
    zeros = jnp.zeros((1, 2 * HD - ROWS), f32)
    lines = [
        high[:, :HD],
        jnp.concatenate([high[:, HD:], zeros], axis=1),
        low[:, :HD],
        jnp.concatenate([low[:, HD:], zeros], axis=1),
    ]
    wide[:, pl.ds(D, HD)] = jnp.concatenate(lines * N_DP, axis=0)
    stores = [store]
    for z in range(NZ):
        for x in range(NX):
            pieces_ref[z * NX + x] = wide[pl.ds((x * NZ + z) * SHARE, SHARE), :].astype(bf16)
        cut = pl.ds(z * NX, NX)
        stores += start(sems.at[pl.ds(2 + z, 1)], (pieces_ref.at[cut], pieces_hbm.at[cut]))
    wait(stores)


def input_kernel(
    frames_ref, partner_ref, moved_ref,
    weight_ref, got_ref, scaled_hbm, layer_hbm,
    even_ref, odd_ref, layer_out_ref,
    scaled_ref, layer_ref, sems,
):
    fetch = start(sems, (scaled_hbm, scaled_ref), (layer_hbm, layer_ref))
    kept, incoming, holds_two = my_counts(frames_ref, partner_ref, moved_ref)
    block = lax.axis_index("y") * NC + lax.axis_index("c")
    fetch[0].wait()
    scaled = scaled_ref[...]
    for index, other in enumerate(EVEN):
        for ref, partner in ((even_ref, other), (odd_ref, other + 1)):
            first = pl.multiple_of((block ^ partner) * HD, HD)
            part = dot(weight_ref[:, pl.ds(first, HD)], scaled, ROWS_BY_COLS)
            ref[pl.ds(index * HD, HD), :] = part.astype(bf16)
    fetch[1].wait()
    received = dot(got_ref[pl.ds(0, ROWS), :], light_places(kept, incoming), COLS_BY_COLS)
    own = layer_ref[:, pl.ds(0, BAL_ROWS)].astype(f32)
    keep = positions((ROWS, BAL_ROWS), 1) < kept
    layer_out_ref[...] = jnp.where(keep, own, received).astype(bf16)


def slots_kernel(pieces_ref, copies_hbm, scale_grad_ref, by_slot, sems):
    total = pieces_ref[0].astype(f32)
    for piece in range(1, N_DP):
        total = total + pieces_ref[piece].astype(f32)
    for slot in range(HEADS):
        by_slot[slot] = total[:, slot * ROWS : (slot + 1) * ROWS].astype(bf16)
    copies = [
        (by_slot, copies_hbm.at[pl.ds(z * HEADS, HEADS)]) for z in range(NZ)
    ]
    copies = start(sems, *copies)
    lines = total[0:2, D:] + total[2:4, D:]
    scale_grad_ref[...] = jnp.concatenate([lines[0:1, :], lines[1:2, : ROWS - HD]], axis=1)
    wait(copies)


def join_kernel(owned_ref, copies_hbm, joined, whole, sems):
    for z in range(NZ):
        for block in range(N_FSDP):
            joined[pl.ds(z * SHARE, SHARE), pl.ds(block * ROWS, ROWS)] = owned_ref[
                z * N_FSDP + block
            ].astype(f32)
    whole[...] = joined[...].astype(bf16)
    wait(start(sems, *[(whole, copies_hbm.at[x]) for x in range(NX)]))


def split(values):
    high = values.astype(bf16)
    return high, (values - high.astype(f32)).astype(bf16)


def mul(a, b):
    a_high, a_low = split(a)
    b_high, b_low = split(b)
    return dot(
        jnp.concatenate([a_high, a_high, a_low], axis=1),
        jnp.concatenate([b_high, b_low, b_high], axis=0),
    )


def ortho_kernel(grad_ref, out_hbm, out_ref, sems):
    grad = grad_ref[...]
    gram = dot(grad, grad, COLS_BY_COLS)
    eye = jnp.where(same(HD), 1.0, 0.0).astype(f32)
    squares = jnp.sum(jnp.sum(gram * eye, axis=1, keepdims=True), axis=0, keepdims=True)
    norm = jnp.sqrt(squares) + EPSILON
    gram = gram / norm / norm
    total = None
    for sweep in range(ITERS):
        step = coeff_linear * eye + coeff_square * gram + coeff_cubic * mul(gram, gram)
        total = step if total is None else mul(total, step)
        if sweep < ITERS - 1:
            gram = mul(mul(step, gram), step)
    total = jnp.concatenate(split(total * (0.2 * math.sqrt(D) / norm)), axis=1)
    stores = []
    for index, first in enumerate(range(0, D, D // PARTS)):
        cut = pl.ds(first, D // PARTS)
        out = dot(grad_ref[:, cut], total, ROWS_BY_COLS)
        out_ref[cut, :] = (out[:, :HD] + out[:, HD:]).astype(bf16)
        stores += start(sems.at[pl.ds(index, 1)], (out_ref.at[cut, :], out_hbm.at[cut, :]))
    wait(stores)


S, V, H = pltpu.SMEM, pltpu.VMEM, pltpu.HBM
FREE = pl.CostEstimate(flops=0, bytes_accessed=0, transcendentals=0)


def call(kernel, name, places, arrays, outs, scratch=(), cost=None):
    arrays = [
        pltpu.with_memory_space_constraint(array, H) if place is H else array
        for array, place in zip(arrays, places)
    ]
    return pl.pallas_call(
        kernel,
        out_shape=[
            H(shape, dtype) if place is H else jax.ShapeDtypeStruct(shape, dtype)
            for shape, dtype, place in outs
        ],
        in_specs=[pl.BlockSpec(memory_space=place) for place in places],
        out_specs=[pl.BlockSpec(memory_space=place) for shape, dtype, place in outs],
        scratch_shapes=list(scratch),
        compiler_params=pltpu.CompilerParams(vmem_limit_bytes=32 * 1024 * 1024),
        name=name,
        cost_estimate=cost,
    )(*arrays)


def exchange(pieces, axes):
    return lax.all_to_all(pieces, axes, split_axis=0, concat_axis=0, tiled=True)


def crossed(array, axis, size, bit):
    return lax.ppermute(array, axis, [(i, i ^ bit) for i in range(size)])


EVEN = (0, 8, 4, 12, 2, 10, 6, 14)


def add_kernel(*refs, parts):
    in_refs, out_refs = refs[:-parts], refs[-parts:]
    rows = in_refs[0].shape[0] // parts
    for index, out_ref in enumerate(out_refs):
        cut = pl.ds(index * rows, rows)
        total = in_refs[0][cut, :].astype(f32)
        for ref in in_refs[1:]:
            total = total + ref[cut, :].astype(f32)
        out_ref[...] = total.astype(bf16)


def add(arrays, parts):
    rows = arrays[0].shape[0] // parts
    return call(
        functools.partial(add_kernel, parts=parts), "add", [V] * len(arrays), arrays,
        [((rows, CAP_ROWS), bf16, V)] * parts, cost=FREE,
    )


def body(
    attended, residual, grad_out, out_weight, layer_scale, frames, partner, moved_tiles, owner_slot
):
    scale_row = layer_scale[None, :]
    ints = pltpu.SMEM((N_DP,), jnp.int32)
    dma = pltpu.SemaphoreType.DMA

    projected, layer_own, window = call(
        project_kernel, "project", [H] * 8,
        (frames, partner, moved_tiles, attended, residual, grad_out, out_weight, scale_row),
        [((ROWS, CAP_ROWS), f32, H), ((ROWS, CAP_ROWS), bf16, H), ((PAD_ROWS, MOVE_ROWS), bf16, H)],
        [
            ints, ints, ints,
            V((A, CAP_ROWS), bf16), V((ROWS, CAP_ROWS), bf16), V((ROWS, BAL_ROWS), bf16),
            V((ROWS, A), bf16), V((1, ROWS), f32),
            V((ROWS, CAP_ROWS), f32), V((ROWS, CAP_ROWS), bf16), V((PAD_ROWS, MOVE_ROWS), bf16),
            dma((6,)), dma((A // CHUNK,)), dma((A // CHUNK,)), dma((3,)),
        ],
    )
    pieces = exchange(window.reshape(N_DP, PAD_ROWS // N_DP, MOVE_ROWS), ("z", "x"))
    pieces = exchange(jnp.take(pieces, partner, axis=0), ("z", "x"))
    got = pieces.reshape(PAD_ROWS, MOVE_ROWS)

    scaled, pieces = call(
        weight_grad_kernel, "weight_grad", [S] * 4 + [V] * 4 + [H],
        (frames, partner, moved_tiles, owner_slot, attended, grad_out, scale_row, got, projected),
        [((ROWS, CAP_ROWS), bf16, H), ((N_DP, SHARE, WIDE), bf16, H)],
        [
            pltpu.SMEM((HEADS,), jnp.int32), V((A, ROWS), f32), V((HD, WIDE), f32),
            V((ROWS, CAP_ROWS), f32), V((ROWS, CAP_ROWS), bf16),
            V((N_DP, SHARE, WIDE), bf16), dma((2 + NZ,)),
        ],
    )
    summed = exchange(pieces, ("z", "x"))

    half = ((A // 2, CAP_ROWS), bf16, V)
    even, odd, layer_out = call(
        input_kernel, "input_grad", [S] * 3 + [V] * 2 + [H] * 2,
        (frames, partner, moved_tiles, out_weight, got, scaled, layer_own),
        [half, half, ((ROWS, BAL_ROWS), bf16, V)],
        [V((ROWS, CAP_ROWS), bf16), V((ROWS, CAP_ROWS), bf16), dma((2,))],
        FREE,
    )
    left, other = add((even, crossed(odd, "c", NC, 1)), 2)
    summed, _ = lax.optimization_barrier((summed, left))
    copies, scale_grad = call(
        slots_kernel, "slots", [V], (summed,),
        [((NZ * HEADS, SHARE, ROWS), bf16, H), ((1, ROWS), f32, V)],
        [V((HEADS, SHARE, ROWS), bf16), dma((NZ,))],
    )
    owned = exchange(copies, ("z", "y", "c"))
    left, *others = add((left, crossed(other, "y", NY, 1)), 4)
    owned, _ = lax.optimization_barrier((owned, left))
    others = [crossed(other, "y", NY, step) for other, step in zip(others, (4, 2, 6))]
    (copies,) = call(
        join_kernel, "join", [V], (owned,),
        [((NX, BY_X, D), bf16, H)],
        [V((BY_X, D), f32), V((BY_X, D), bf16), dma((NX,))],
    )
    whole = exchange(copies, "x").reshape(HD, D)
    (ortho_update,) = call(
        ortho_kernel, "ortho", [V], (whole,), [((D, HD), bf16, H)],
        [V((D, HD), bf16), dma((PARTS,))],
    )
    left, others, ortho_update = lax.optimization_barrier((left, others, ortho_update))
    (input_grad,) = add((left, *others), 1)
    return (layer_out, input_grad, scale_grad.reshape(ROWS), ortho_update[:, None, :])


def solution(mesh):
    chips = Mesh(mesh.devices.reshape(NZ, NX, NY, NC), ("z", "x", "y", "c"))
    dp, fsdp = ("z", "x"), ("y", "c")
    placed = (
        P(None, dp),
        P(fsdp, dp),
        P(fsdp, dp),
        P(fsdp, None),
        P(fsdp),
        P(),
        P(),
        P(),
        P(),
    )
    return jax.shard_map(
        body,
        mesh=chips,
        in_specs=placed,
        out_specs=(P(fsdp, dp), P(fsdp, dp), P(fsdp), P(None, fsdp, None)),
        check_vma=False,
    )
```

```python
import functools
import math

import jax
import jax.numpy as jnp
from jax import lax
from jax.experimental import pallas as pl
from jax.experimental.pallas import tpu as pltpu
from jax.sharding import Mesh, PartitionSpec as P

D = 3200
HEADS = 16
HD = 128
FRAME = 256
TILE = 16
ITERS = 5
A = 2048
CAP_ROWS = 512
MOVE_ROWS = 256
BAL_ROWS = 384
N_DP = 32
N_FSDP = 16

NZ, NX, NY, NC = 8, 4, 8, 2
ROWS = D // N_FSDP
BY_X = HD // NX
SHARE = HD // N_DP
WIDE = D + HD
PAD_ROWS = 256
EARLY = CAP_ROWS - MOVE_ROWS
LATE = MOVE_ROWS
CHUNK = 512
PARTS = 5

coeff_linear = 3.4445
coeff_square = -4.775
coeff_cubic = 2.0315
EPSILON = 1e-07
INVERSE_ROOT = 1.0 / math.sqrt(N_DP * BAL_ROWS)

bf16 = jnp.bfloat16
f32 = jnp.float32

ROWS_BY_COLS = (((0,), (0,)), ((), ()))
COLS_BY_COLS = (((1,), (1,)), ((), ()))


def positions(shape, dimension):
    return lax.broadcasted_iota(jnp.int32, shape, dimension)


def dot(a, b, dims=(((1,), (0,)), ((), ()))):
    return lax.dot_general(a, b, dims, preferred_element_type=f32)


def same(size):
    return positions((size, size), 0) == positions((size, size), 1)


def to_column(row):
    size = row.shape[1]
    return jnp.sum(jnp.where(same(size), row, 0.0), axis=1, keepdims=True)


def to_row(column):
    size = column.shape[0]
    return jnp.sum(jnp.where(same(size), column, 0.0), axis=0, keepdims=True)


def my_counts(frames_ref, partner_ref, moved_ref):
    replica = lax.axis_index("z") * NX + lax.axis_index("x")
    mate = partner_ref[replica]
    kept = frames_ref[replica] * FRAME - moved_ref[replica] * TILE
    incoming = moved_ref[mate] * TILE
    holds_two = (frames_ref[replica] > frames_ref[mate]).astype(jnp.int32)
    return kept, incoming, holds_two


def light_places(kept, incoming):
    bal_col = positions((BAL_ROWS, MOVE_ROWS), 0)
    win_col = positions((BAL_ROWS, MOVE_ROWS), 1)
    hit = bal_col == win_col + (kept + incoming - MOVE_ROWS)
    hit = hit & (win_col >= MOVE_ROWS - incoming)
    return jnp.where(hit, 1.0, 0.0).astype(bf16)


def start(sems, *pairs):
    copies = [pltpu.make_async_copy(a, b, sems.at[i]) for i, (a, b) in enumerate(pairs)]
    for copy in copies:
        copy.start()
    return copies


def wait(copies):
    for copy in copies:
        copy.wait()


def window_kernel(
    frames_hbm, partner_hbm, moved_hbm,
    attended_hbm, residual_hbm, grad_hbm, weight_hbm, scale_hbm,
    projected_hbm, layer_hbm, window_hbm,
    frames_ref, partner_ref, moved_ref,
    attended_ref, residual_ref, grad_ref, weight_ref, scale_ref,
    projected_ref, layer_ref, window_ref,
    small_sems, attended_sems, weight_sems, out_sems,
):
    late = pl.ds(EARLY, LATE)
    cuts = [pl.ds(first, CHUNK) for first in range(0, A, CHUNK)]
    attended = start(
        attended_sems, *[(attended_hbm.at[cut, late], attended_ref.at[cut, :]) for cut in cuts]
    )
    weight = start(
        weight_sems, *[(weight_hbm.at[:, cut], weight_ref.at[:, cut]) for cut in cuts]
    )
    small = start(
        small_sems,
        (frames_hbm, frames_ref),
        (partner_hbm, partner_ref),
        (moved_hbm, moved_ref),
        (scale_hbm, scale_ref),
        (grad_hbm, grad_ref),
        (residual_hbm.at[:, late], residual_ref),
    )
    wait(small[:5])
    kept, incoming, holds_two = my_counts(frames_ref, partner_ref, moved_ref)
    gains = to_column(scale_ref[...])
    grad_win = dot(grad_ref[...], light_places(kept, incoming))
    window_ref[pl.ds(ROWS, PAD_ROWS - ROWS), :] = jnp.zeros(
        (PAD_ROWS - ROWS, MOVE_ROWS), bf16
    )
    projected = None
    for index, cut in enumerate(cuts):
        attended[index].wait()
        weight[index].wait()
        part = dot(weight_ref[:, cut], attended_ref[cut, :])
        projected = part if projected is None else projected + part
    small[5].wait()
    layer = (residual_ref[...].astype(f32) + gains * projected).astype(bf16)
    window = jnp.where(holds_two == 1, layer.astype(f32), grad_win)
    window_ref[pl.ds(0, ROWS), :] = window.astype(bf16)
    out = start(out_sems, (window_ref, window_hbm))
    projected_ref[...] = projected
    layer_ref[...] = layer
    out += start(
        out_sems.at[pl.ds(1, 2)], (projected_ref, projected_hbm), (layer_ref, layer_hbm)
    )
    wait(out)


def by_slots(attended_ref, columns, scaled, slot_ref, head_of, wide):
    for head in range(HEADS):
        head_of[slot_ref[head]] = head
    for slot in range(HEADS):
        first = pl.multiple_of(head_of[slot] * HD, HD)
        wide[:, pl.ds(slot * ROWS, ROWS)] = dot(
            attended_ref[pl.ds(first, HD), columns], scaled, COLS_BY_COLS
        )


def early_kernel(
    frames_ref, partner_ref, moved_ref, slot_ref,
    attended_ref, residual_ref, grad_ref, weight_ref, scale_ref,
    layer_hbm, scaled_hbm, wide_hbm, part_ref,
    head_of, layer_ref, scaled_ref, wide_ref, sems,
):
    early = pl.ds(0, EARLY)
    kept, incoming, holds_two = my_counts(frames_ref, partner_ref, moved_ref)
    gains = to_column(scale_ref[...])
    projected = dot(weight_ref[...], attended_ref[:, early])
    layer_ref[...] = (residual_ref[:, early].astype(f32) + gains * projected).astype(bf16)
    stores = start(sems, (layer_ref, layer_hbm))
    keep = positions((ROWS, EARLY), 1) < kept
    grad = jnp.where(keep, grad_ref[:, early].astype(f32), 0.0)
    scaled = (grad * gains).astype(bf16)
    scaled_ref[...] = scaled
    stores += start(sems.at[pl.ds(1, 1)], (scaled_ref, scaled_hbm))
    by_slots(attended_ref, early, scaled, slot_ref, head_of, wide_ref)
    stores += start(sems.at[pl.ds(2, 1)], (wide_ref, wide_hbm))
    part_ref[...] = to_row(jnp.sum(grad * projected, axis=1, keepdims=True))
    wait(stores)


def weight_grad_kernel(
    frames_ref, partner_ref, moved_ref, slot_ref,
    attended_ref, grad_ref, scale_ref, got_ref, part_ref, early_hbm, projected_hbm,
    scaled_hbm, pieces_hbm,
    head_of, wide, early_ref, projected_ref, scaled_ref, pieces_ref, sems,
):
    fetch = start(
        sems.at[pl.ds(1 + NZ, 2)], (early_hbm, early_ref), (projected_hbm, projected_ref)
    )
    kept, incoming, holds_two = my_counts(frames_ref, partner_ref, moved_ref)
    own = grad_ref[:, pl.ds(EARLY, BAL_ROWS - EARLY)].astype(f32)
    own = jnp.concatenate([own, jnp.zeros((ROWS, CAP_ROWS - BAL_ROWS), f32)], axis=1)
    got = got_ref[pl.ds(0, ROWS), :].astype(f32)
    got = jnp.where(holds_two == 1, got, 0.0)
    grad = jnp.where(positions((ROWS, LATE), 1) < kept - EARLY, own, got)
    scaled = (grad * to_column(scale_ref[...])).astype(bf16)
    scaled_ref[...] = scaled
    stores = start(sems, (scaled_ref, scaled_hbm))
    by_slots(attended_ref, pl.ds(EARLY, LATE), scaled, slot_ref, head_of, wide)
    wait(fetch)
    part = to_row(jnp.sum(grad * projected_ref[...], axis=1, keepdims=True))
    part = (part + part_ref[...]) * INVERSE_ROOT
    high = part.astype(bf16).astype(f32)
    low = part - high
    zeros = jnp.zeros((1, 2 * HD - ROWS), f32)
    lines = [
        high[:, :HD],
        jnp.concatenate([high[:, HD:], zeros], axis=1),
        low[:, :HD],
        jnp.concatenate([low[:, HD:], zeros], axis=1),
    ]
    lines = jnp.concatenate(lines, axis=0).astype(bf16)
    for z in range(NZ):
        for x in range(NX):
            cut = pl.ds((x * NZ + z) * SHARE, SHARE)
            pieces_ref[z * NX + x, :, pl.ds(0, D)] = (wide[cut, :] + early_ref[cut, :]).astype(bf16)
            pieces_ref[z * NX + x, :, pl.ds(D, HD)] = lines
        cut = pl.ds(z * NX, NX)
        stores += start(sems.at[pl.ds(1 + z, 1)], (pieces_ref.at[cut], pieces_hbm.at[cut]))
    wait(stores)


def input_kernel(
    frames_ref, partner_ref, moved_ref,
    weight_ref, got_ref, scaled_early_hbm, scaled_late_hbm, layer_early_hbm, layer_late_hbm,
    even_ref, odd_ref, layer_out_ref,
    scaled_ref, layer_ref, sems,
):
    early, late = pl.ds(0, EARLY), pl.ds(EARLY, LATE)
    fetch = start(
        sems,
        (scaled_early_hbm, scaled_ref.at[:, early]),
        (scaled_late_hbm, scaled_ref.at[:, late]),
        (layer_early_hbm, layer_ref.at[:, early]),
        (layer_late_hbm, layer_ref.at[:, late]),
    )
    kept, incoming, holds_two = my_counts(frames_ref, partner_ref, moved_ref)
    block = lax.axis_index("y") * NC + lax.axis_index("c")
    wait(fetch[:2])
    scaled = scaled_ref[...]
    for index, other in enumerate(EVEN):
        for ref, partner in ((even_ref, other), (odd_ref, other + 1)):
            first = pl.multiple_of((block ^ partner) * HD, HD)
            part = dot(weight_ref[:, pl.ds(first, HD)], scaled, ROWS_BY_COLS)
            ref[pl.ds(index * HD, HD), :] = part.astype(bf16)
    wait(fetch[2:])
    received = dot(got_ref[pl.ds(0, ROWS), :], light_places(kept, incoming), COLS_BY_COLS)
    own = layer_ref[:, pl.ds(0, BAL_ROWS)].astype(f32)
    keep = positions((ROWS, BAL_ROWS), 1) < kept
    layer_out_ref[...] = jnp.where(keep, own, received).astype(bf16)


def slots_kernel(pieces_ref, copies_hbm, scale_grad_ref, by_slot, sems):
    total = pieces_ref[0].astype(f32)
    for piece in range(1, N_DP):
        total = total + pieces_ref[piece].astype(f32)
    for slot in range(HEADS):
        by_slot[slot] = total[:, slot * ROWS : (slot + 1) * ROWS].astype(bf16)
    copies = [
        (by_slot, copies_hbm.at[pl.ds(z * HEADS, HEADS)]) for z in range(NZ)
    ]
    copies = start(sems, *copies)
    lines = total[0:2, D:] + total[2:4, D:]
    scale_grad_ref[...] = jnp.concatenate([lines[0:1, :], lines[1:2, : ROWS - HD]], axis=1)
    wait(copies)


def join_kernel(owned_ref, copies_hbm, joined, whole, sems):
    for z in range(NZ):
        for block in range(N_FSDP):
            joined[pl.ds(z * SHARE, SHARE), pl.ds(block * ROWS, ROWS)] = owned_ref[
                z * N_FSDP + block
            ].astype(f32)
    whole[...] = joined[...].astype(bf16)
    wait(start(sems, *[(whole, copies_hbm.at[x]) for x in range(NX)]))


def split(values):
    high = values.astype(bf16)
    return high, (values - high.astype(f32)).astype(bf16)


def mul(a, b):
    a_high, a_low = split(a)
    b_high, b_low = split(b)
    return dot(
        jnp.concatenate([a_high, a_high, a_low], axis=1),
        jnp.concatenate([b_high, b_low, b_high], axis=0),
    )


def ortho_kernel(grad_ref, out_hbm, out_ref, sems):
    grad = grad_ref[...]
    gram = dot(grad, grad, COLS_BY_COLS)
    eye = jnp.where(same(HD), 1.0, 0.0).astype(f32)
    squares = jnp.sum(jnp.sum(gram * eye, axis=1, keepdims=True), axis=0, keepdims=True)
    norm = jnp.sqrt(squares) + EPSILON
    gram = gram / norm / norm
    total = None
    for sweep in range(ITERS):
        step = coeff_linear * eye + coeff_square * gram + coeff_cubic * mul(gram, gram)
        total = step if total is None else mul(total, step)
        if sweep < ITERS - 1:
            gram = mul(mul(step, gram), step)
    total = jnp.concatenate(split(total * (0.2 * math.sqrt(D) / norm)), axis=1)
    stores = []
    for index, first in enumerate(range(0, D, D // PARTS)):
        cut = pl.ds(first, D // PARTS)
        out = dot(grad_ref[:, cut], total, ROWS_BY_COLS)
        out_ref[cut, :] = (out[:, :HD] + out[:, HD:]).astype(bf16)
        stores += start(sems.at[pl.ds(index, 1)], (out_ref.at[cut, :], out_hbm.at[cut, :]))
    wait(stores)


S, V, H = pltpu.SMEM, pltpu.VMEM, pltpu.HBM
FREE = pl.CostEstimate(flops=0, bytes_accessed=0, transcendentals=0)


def call(kernel, name, places, arrays, outs, scratch=(), cost=None):
    arrays = [
        pltpu.with_memory_space_constraint(array, H) if place is H else array
        for array, place in zip(arrays, places)
    ]
    return pl.pallas_call(
        kernel,
        out_shape=[
            H(shape, dtype) if place is H else jax.ShapeDtypeStruct(shape, dtype)
            for shape, dtype, place in outs
        ],
        in_specs=[pl.BlockSpec(memory_space=place) for place in places],
        out_specs=[pl.BlockSpec(memory_space=place) for shape, dtype, place in outs],
        scratch_shapes=list(scratch),
        compiler_params=pltpu.CompilerParams(vmem_limit_bytes=32 * 1024 * 1024),
        name=name,
        cost_estimate=cost,
    )(*arrays)


def exchange(pieces, axes):
    return lax.all_to_all(pieces, axes, split_axis=0, concat_axis=0, tiled=True)


def crossed(array, axis, size, bit):
    return lax.ppermute(array, axis, [(i, i ^ bit) for i in range(size)])


EVEN = (0, 8, 4, 12, 2, 10, 6, 14)


def add_kernel(*refs, parts):
    in_refs, out_refs = refs[:-parts], refs[-parts:]
    rows = in_refs[0].shape[0] // parts
    for index, out_ref in enumerate(out_refs):
        cut = pl.ds(index * rows, rows)
        total = in_refs[0][cut, :].astype(f32)
        for ref in in_refs[1:]:
            total = total + ref[cut, :].astype(f32)
        out_ref[...] = total.astype(bf16)


def add(arrays, parts):
    rows = arrays[0].shape[0] // parts
    return call(
        functools.partial(add_kernel, parts=parts), "add", [V] * len(arrays), arrays,
        [((rows, CAP_ROWS), bf16, V)] * parts, cost=FREE,
    )


def body(
    attended, residual, grad_out, out_weight, layer_scale, frames, partner, moved_tiles, owner_slot
):
    scale_row = layer_scale[None, :]
    ints = pltpu.SMEM((N_DP,), jnp.int32)
    dma = pltpu.SemaphoreType.DMA

    late = (ROWS, LATE)
    projected, layer_late, window = call(
        window_kernel, "window", [H] * 8,
        (frames, partner, moved_tiles, attended, residual, grad_out, out_weight, scale_row),
        [(late, f32, H), (late, bf16, H), ((PAD_ROWS, MOVE_ROWS), bf16, H)],
        [
            ints, ints, ints,
            V((A, LATE), bf16), V(late, bf16), V((ROWS, BAL_ROWS), bf16),
            V((ROWS, A), bf16), V((1, ROWS), f32),
            V(late, f32), V(late, bf16), V((PAD_ROWS, MOVE_ROWS), bf16),
            dma((6,)), dma((A // CHUNK,)), dma((A // CHUNK,)), dma((3,)),
        ],
    )
    pieces = exchange(window.reshape(N_DP, PAD_ROWS // N_DP, MOVE_ROWS), ("z", "x"))
    pieces = exchange(jnp.take(pieces, partner, axis=0), ("z", "x"))
    got = pieces.reshape(PAD_ROWS, MOVE_ROWS)

    early = (ROWS, EARLY)
    heads = pltpu.SMEM((HEADS,), jnp.int32)
    layer_early, scaled_early, wide, part = call(
        early_kernel, "early", [S] * 4 + [V] * 5,
        (frames, partner, moved_tiles, owner_slot, attended, residual, grad_out, out_weight, scale_row),
        [(early, bf16, H), (early, bf16, H), ((HD, D), f32, H), ((1, ROWS), f32, V)],
        [heads, V(early, bf16), V(early, bf16), V((HD, D), f32), dma((3,))],
        FREE,
    )
    scaled_late, pieces = call(
        weight_grad_kernel, "weight_grad", [S] * 4 + [V] * 5 + [H] * 2,
        (
            frames, partner, moved_tiles, owner_slot,
            attended, grad_out, scale_row, got, part, wide, projected,
        ),
        [(late, bf16, H), ((N_DP, SHARE, WIDE), bf16, H)],
        [
            heads, V((HD, D), f32), V((HD, D), f32), V(late, f32), V(late, bf16),
            V((N_DP, SHARE, WIDE), bf16), dma((3 + NZ,)),
        ],
    )
    summed = exchange(pieces, ("z", "x"))

    half = ((A // 2, CAP_ROWS), bf16, V)
    even, odd, layer_out = call(
        input_kernel, "input_grad", [S] * 3 + [V] * 2 + [H] * 4,
        (
            frames, partner, moved_tiles, out_weight, got,
            scaled_early, scaled_late, layer_early, layer_late,
        ),
        [half, half, ((ROWS, BAL_ROWS), bf16, V)],
        [V((ROWS, CAP_ROWS), bf16), V((ROWS, CAP_ROWS), bf16), dma((4,))],
        FREE,
    )
    left, other = add((even, crossed(odd, "c", NC, 1)), 2)
    summed, _ = lax.optimization_barrier((summed, left))
    copies, scale_grad = call(
        slots_kernel, "slots", [V], (summed,),
        [((NZ * HEADS, SHARE, ROWS), bf16, H), ((1, ROWS), f32, V)],
        [V((HEADS, SHARE, ROWS), bf16), dma((NZ,))],
    )
    owned = exchange(copies, ("z", "y", "c"))
    left, *others = add((left, crossed(other, "y", NY, 1)), 4)
    others = [crossed(other, "y", NY, step) for other, step in zip(others, (4, 2, 6))]
    owned, _ = lax.optimization_barrier((owned, others[:2]))
    (copies,) = call(
        join_kernel, "join", [V], (owned,),
        [((NX, BY_X, D), bf16, H)],
        [V((BY_X, D), f32), V((BY_X, D), bf16), dma((NX,))],
    )
    whole = exchange(copies, "x").reshape(HD, D)
    (input_grad,) = add((left, *others), 1)
    whole, _ = lax.optimization_barrier((whole, input_grad))
    (ortho_update,) = call(
        ortho_kernel, "ortho", [V], (whole,), [((D, HD), bf16, H)],
        [V((D, HD), bf16), dma((PARTS,))],
    )
    return (layer_out, input_grad, scale_grad.reshape(ROWS), ortho_update[:, None, :])


def solution(mesh):
    chips = Mesh(mesh.devices.reshape(NZ, NX, NY, NC), ("z", "x", "y", "c"))
    dp, fsdp = ("z", "x"), ("y", "c")
    placed = (
        P(None, dp),
        P(fsdp, dp),
        P(fsdp, dp),
        P(fsdp, None),
        P(fsdp),
        P(),
        P(),
        P(),
        P(),
    )
    return jax.shard_map(
        body,
        mesh=chips,
        in_specs=placed,
        out_specs=(P(fsdp, dp), P(fsdp, dp), P(fsdp), P(None, fsdp, None)),
        check_vma=False,
    )
```

```python
import functools
import math

import jax
import jax.numpy as jnp
from jax import lax
from jax.experimental import pallas as pl
from jax.experimental.pallas import tpu as pltpu
from jax.sharding import Mesh, PartitionSpec as P

D = 3200
HEADS = 16
HD = 128
FRAME = 256
TILE = 16
ITERS = 5
A = 2048
CAP_ROWS = 512
MOVE_ROWS = 256
BAL_ROWS = 384
N_DP = 32
N_FSDP = 16

NZ, NX, NY, NC = 8, 4, 8, 2
ROWS = D // N_FSDP
BY_X = HD // NX
SHARE = HD // N_DP
WIDE = D + HD
PAD_ROWS = 256
CHUNK = 512
PARTS = 5

coeff_linear = 3.4445
coeff_square = -4.775
coeff_cubic = 2.0315
EPSILON = 1e-07
INVERSE_ROOT = 1.0 / math.sqrt(N_DP * BAL_ROWS)

bf16 = jnp.bfloat16
f32 = jnp.float32

ROWS_BY_COLS = (((0,), (0,)), ((), ()))
COLS_BY_COLS = (((1,), (1,)), ((), ()))


def positions(shape, dimension):
    return lax.broadcasted_iota(jnp.int32, shape, dimension)


def dot(a, b, dims=(((1,), (0,)), ((), ()))):
    return lax.dot_general(a, b, dims, preferred_element_type=f32)


def same(size):
    return positions((size, size), 0) == positions((size, size), 1)


def to_column(row):
    size = row.shape[1]
    return jnp.sum(jnp.where(same(size), row, 0.0), axis=1, keepdims=True)


def to_row(column):
    size = column.shape[0]
    return jnp.sum(jnp.where(same(size), column, 0.0), axis=0, keepdims=True)


def my_counts(frames_ref, partner_ref, moved_ref):
    replica = lax.axis_index("z") * NX + lax.axis_index("x")
    mate = partner_ref[replica]
    kept = frames_ref[replica] * FRAME - moved_ref[replica] * TILE
    incoming = moved_ref[mate] * TILE
    holds_two = (frames_ref[replica] > frames_ref[mate]).astype(jnp.int32)
    return kept, incoming, holds_two


def light_places(kept, incoming):
    bal_col = positions((BAL_ROWS, MOVE_ROWS), 0)
    win_col = positions((BAL_ROWS, MOVE_ROWS), 1)
    hit = bal_col == win_col + (kept + incoming - MOVE_ROWS)
    hit = hit & (win_col >= MOVE_ROWS - incoming)
    return jnp.where(hit, 1.0, 0.0).astype(bf16)


def start(sems, *pairs):
    copies = [pltpu.make_async_copy(a, b, sems.at[i]) for i, (a, b) in enumerate(pairs)]
    for copy in copies:
        copy.start()
    return copies


def wait(copies):
    for copy in copies:
        copy.wait()


def project_kernel(
    frames_hbm, partner_hbm, moved_hbm,
    attended_hbm, residual_hbm, grad_hbm, weight_hbm, scale_hbm,
    projected_hbm, layer_hbm, window_ref,
    frames_ref, partner_ref, moved_ref,
    attended_ref, residual_ref, grad_ref, weight_ref, scale_ref,
    projected_ref, layer_ref,
    small_sems, attended_sems, weight_sems, out_sems,
):
    small = start(
        small_sems,
        (frames_hbm, frames_ref),
        (partner_hbm, partner_ref),
        (moved_hbm, moved_ref),
        (scale_hbm, scale_ref),
        (grad_hbm, grad_ref),
        (residual_hbm, residual_ref),
    )
    cuts = [pl.ds(first, CHUNK) for first in range(0, A, CHUNK)]
    attended = start(
        attended_sems, *[(attended_hbm.at[cut, :], attended_ref.at[cut, :]) for cut in cuts]
    )
    weight = start(
        weight_sems, *[(weight_hbm.at[:, cut], weight_ref.at[:, cut]) for cut in cuts]
    )
    wait(small[:5])
    kept, incoming, holds_two = my_counts(frames_ref, partner_ref, moved_ref)
    gains = to_column(scale_ref[...])
    grad_win = dot(grad_ref[...], light_places(kept, incoming))
    window_ref[pl.ds(ROWS, PAD_ROWS - ROWS), :] = jnp.zeros(
        (PAD_ROWS - ROWS, MOVE_ROWS), bf16
    )
    projected = None
    for index, cut in enumerate(cuts):
        attended[index].wait()
        weight[index].wait()
        part = dot(weight_ref[:, cut], attended_ref[cut, :])
        projected = part if projected is None else projected + part
    projected_ref[...] = projected
    out = start(out_sems, (projected_ref, projected_hbm))
    small[5].wait()
    layer = (residual_ref[...].astype(f32) + gains * projected).astype(bf16)
    layer_ref[...] = layer
    out += start(out_sems.at[pl.ds(1, 1)], (layer_ref, layer_hbm))
    layer_win = layer[:, MOVE_ROWS:].astype(f32)
    window_ref[pl.ds(0, ROWS), :] = jnp.where(holds_two == 1, layer_win, grad_win).astype(bf16)
    wait(out)


def forward_kernel(partner_ref, pieces_ref, out_ref):
    for replica in range(N_DP):
        out_ref[replica] = pieces_ref[partner_ref[replica]]


def send_lanes(first, last, value, pieces_ref, pieces_hbm, sems):
    lanes = pl.ds(first, last - first)
    for piece in range(N_DP):
        pieces_ref[piece, :, lanes] = value(piece, lanes)
    return start(sems, (pieces_ref.at[:, :, lanes], pieces_hbm.at[:, :, lanes]))


def weight_grad_kernel(
    frames_ref, partner_ref, moved_ref, slot_ref,
    attended_ref, grad_ref, scale_ref, got_ref, projected_hbm,
    scaled_hbm, pieces_hbm,
    head_of, wide, projected_ref, scaled_ref, pieces_ref, sems,
):
    (fetch,) = start(sems, (projected_hbm, projected_ref))
    kept, incoming, holds_two = my_counts(frames_ref, partner_ref, moved_ref)
    for head in range(HEADS):
        head_of[slot_ref[head]] = head
    own = grad_ref[...].astype(f32)
    own = jnp.concatenate([own, jnp.zeros((ROWS, CAP_ROWS - BAL_ROWS), f32)], axis=1)
    got = got_ref[pl.ds(0, ROWS), :].astype(f32)
    got = jnp.where(holds_two == 1, got, 0.0)
    got = jnp.concatenate([jnp.zeros((ROWS, CAP_ROWS - MOVE_ROWS), f32), got], axis=1)
    grad = jnp.where(positions((ROWS, CAP_ROWS), 1) < kept, own, got)
    scaled = (grad * to_column(scale_ref[...])).astype(bf16)
    scaled_ref[...] = scaled
    (store,) = start(sems.at[pl.ds(1, 1)], (scaled_ref, scaled_hbm))
    stores, done = [store], 0
    for slot in range(HEADS):
        first = pl.multiple_of(head_of[slot] * HD, HD)
        wide[:, pl.ds(slot * ROWS, ROWS)] = dot(
            attended_ref[pl.ds(first, HD), :], scaled, COLS_BY_COLS
        )
        if (slot + 1) % 4 == 0:
            full = (slot + 1) * ROWS // HD * HD
            stores += send_lanes(done, full, lambda piece, lanes: wide[
                pl.ds((piece % NX * NZ + piece // NX) * SHARE, SHARE), lanes
            ].astype(bf16), pieces_ref, pieces_hbm, sems.at[pl.ds(2 + slot // 4, 1)])
            done = full
    fetch.wait()
    part = jnp.sum(grad * projected_ref[...], axis=1, keepdims=True) * INVERSE_ROOT
    part = to_row(part)
    high = part.astype(bf16).astype(f32)
    low = part - high
    zeros = jnp.zeros((1, 2 * HD - ROWS), f32)
    lines = [
        high[:, :HD],
        jnp.concatenate([high[:, HD:], zeros], axis=1),
        low[:, :HD],
        jnp.concatenate([low[:, HD:], zeros], axis=1),
    ]
    lines = jnp.concatenate(lines, axis=0).astype(bf16)
    stores += send_lanes(
        D, WIDE, lambda piece, lanes: lines, pieces_ref, pieces_hbm, sems.at[pl.ds(6, 1)]
    )
    wait(stores)


def input_kernel(
    frames_ref, partner_ref, moved_ref,
    weight_ref, got_ref, scaled_hbm, layer_hbm,
    even_ref, odd_ref, layer_out_ref,
    scaled_ref, layer_ref, sems,
):
    fetch = start(sems, (scaled_hbm, scaled_ref), (layer_hbm, layer_ref))
    kept, incoming, holds_two = my_counts(frames_ref, partner_ref, moved_ref)
    block = lax.axis_index("y") * NC + lax.axis_index("c")
    fetch[0].wait()
    scaled = scaled_ref[...]
    for index, other in enumerate(EVEN):
        for ref, partner in ((even_ref, other), (odd_ref, other + 1)):
            first = pl.multiple_of((block ^ partner) * HD, HD)
            part = dot(weight_ref[:, pl.ds(first, HD)], scaled, ROWS_BY_COLS)
            ref[pl.ds(index * HD, HD), :] = part.astype(bf16)
    fetch[1].wait()
    received = dot(got_ref[pl.ds(0, ROWS), :], light_places(kept, incoming), COLS_BY_COLS)
    own = layer_ref[:, pl.ds(0, BAL_ROWS)].astype(f32)
    keep = positions((ROWS, BAL_ROWS), 1) < kept
    layer_out_ref[...] = jnp.where(keep, own, received).astype(bf16)


def slots_kernel(pieces_ref, copies_hbm, scale_grad_ref, by_slot, sems):
    total = pieces_ref[0].astype(f32)
    for piece in range(1, N_DP):
        total = total + pieces_ref[piece].astype(f32)
    for slot in range(HEADS):
        by_slot[slot] = total[:, slot * ROWS : (slot + 1) * ROWS].astype(bf16)
    copies = [
        (by_slot, copies_hbm.at[pl.ds(z * HEADS, HEADS)]) for z in range(NZ)
    ]
    copies = start(sems, *copies)
    lines = total[0:2, D:] + total[2:4, D:]
    scale_grad_ref[...] = jnp.concatenate([lines[0:1, :], lines[1:2, : ROWS - HD]], axis=1)
    wait(copies)


def join_kernel(owned_ref, copies_hbm, joined, whole, sems):
    for z in range(NZ):
        for block in range(N_FSDP):
            joined[pl.ds(z * SHARE, SHARE), pl.ds(block * ROWS, ROWS)] = owned_ref[
                z * N_FSDP + block
            ].astype(f32)
    whole[...] = joined[...].astype(bf16)
    wait(start(sems, *[(whole, copies_hbm.at[x]) for x in range(NX)]))


def split(values):
    high = values.astype(bf16)
    return high, (values - high.astype(f32)).astype(bf16)


def mul(a, b):
    a_high, a_low = split(a)
    b_high, b_low = split(b)
    return dot(
        jnp.concatenate([a_high, a_high, a_low], axis=1),
        jnp.concatenate([b_high, b_low, b_high], axis=0),
    )


def ortho_kernel(grad_ref, out_hbm, out_ref, sems):
    grad = grad_ref[...]
    gram = dot(grad, grad, COLS_BY_COLS)
    eye = jnp.where(same(HD), 1.0, 0.0).astype(f32)
    squares = jnp.sum(jnp.sum(gram * eye, axis=1, keepdims=True), axis=0, keepdims=True)
    norm = jnp.sqrt(squares) + EPSILON
    gram = gram / norm / norm
    total = None
    for sweep in range(ITERS):
        step = coeff_linear * eye + coeff_square * gram + coeff_cubic * mul(gram, gram)
        total = step if total is None else mul(total, step)
        if sweep < ITERS - 1:
            gram = mul(mul(step, gram), step)
    total = jnp.concatenate(split(total * (0.2 * math.sqrt(D) / norm)), axis=1)
    stores = []
    for index, first in enumerate(range(0, D, D // PARTS)):
        cut = pl.ds(first, D // PARTS)
        out = dot(grad_ref[:, cut], total, ROWS_BY_COLS)
        out_ref[cut, :] = (out[:, :HD] + out[:, HD:]).astype(bf16)
        stores += start(sems.at[pl.ds(index, 1)], (out_ref.at[cut, :], out_hbm.at[cut, :]))
    wait(stores)


S, V, H = pltpu.SMEM, pltpu.VMEM, pltpu.HBM
FREE = pl.CostEstimate(flops=0, bytes_accessed=0, transcendentals=0)


def call(kernel, name, places, arrays, outs, scratch=(), cost=None):
    arrays = [
        pltpu.with_memory_space_constraint(array, H) if place is H else array
        for array, place in zip(arrays, places)
    ]
    return pl.pallas_call(
        kernel,
        out_shape=[
            H(shape, dtype) if place is H else jax.ShapeDtypeStruct(shape, dtype)
            for shape, dtype, place in outs
        ],
        in_specs=[pl.BlockSpec(memory_space=place) for place in places],
        out_specs=[pl.BlockSpec(memory_space=place) for shape, dtype, place in outs],
        scratch_shapes=list(scratch),
        compiler_params=pltpu.CompilerParams(vmem_limit_bytes=32 * 1024 * 1024),
        name=name,
        cost_estimate=cost,
    )(*arrays)


def exchange(pieces, axes):
    return lax.all_to_all(pieces, axes, split_axis=0, concat_axis=0, tiled=True)


def crossed(array, axis, size, bit):
    return lax.ppermute(array, axis, [(i, i ^ bit) for i in range(size)])


EVEN = (0, 8, 4, 12, 2, 10, 6, 14)


def add_kernel(*refs, parts):
    in_refs, out_refs = refs[:-parts], refs[-parts:]
    rows = in_refs[0].shape[0] // parts
    for index, out_ref in enumerate(out_refs):
        cut = pl.ds(index * rows, rows)
        total = in_refs[0][cut, :].astype(f32)
        for ref in in_refs[1:]:
            total = total + ref[cut, :].astype(f32)
        out_ref[...] = total.astype(bf16)


def add(arrays, parts):
    rows = arrays[0].shape[0] // parts
    return call(
        functools.partial(add_kernel, parts=parts), "add", [V] * len(arrays), arrays,
        [((rows, CAP_ROWS), bf16, V)] * parts, cost=FREE,
    )


def body(
    attended, residual, grad_out, out_weight, layer_scale, frames, partner, moved_tiles, owner_slot
):
    scale_row = layer_scale[None, :]
    ints = pltpu.SMEM((N_DP,), jnp.int32)
    dma = pltpu.SemaphoreType.DMA

    projected, layer_own, window = call(
        project_kernel, "project", [H] * 8,
        (frames, partner, moved_tiles, attended, residual, grad_out, out_weight, scale_row),
        [((ROWS, CAP_ROWS), f32, H), ((ROWS, CAP_ROWS), bf16, H), ((PAD_ROWS, MOVE_ROWS), bf16, V)],
        [
            ints, ints, ints,
            V((A, CAP_ROWS), bf16), V((ROWS, CAP_ROWS), bf16), V((ROWS, BAL_ROWS), bf16),
            V((ROWS, A), bf16), V((1, ROWS), f32),
            V((ROWS, CAP_ROWS), f32), V((ROWS, CAP_ROWS), bf16),
            dma((6,)), dma((A // CHUNK,)), dma((A // CHUNK,)), dma((2,)),
        ],
    )
    pieces = exchange(window.reshape(N_DP, PAD_ROWS // N_DP, MOVE_ROWS), ("z", "x"))
    (pieces,) = call(
        forward_kernel, "forward", [S, V], (partner, pieces),
        [((N_DP, PAD_ROWS // N_DP, MOVE_ROWS), bf16, V)],
    )
    pieces = exchange(pieces, ("z", "x"))
    got = pieces.reshape(PAD_ROWS, MOVE_ROWS)

    scaled, pieces = call(
        weight_grad_kernel, "weight_grad", [S] * 4 + [V] * 4 + [H],
        (frames, partner, moved_tiles, owner_slot, attended, grad_out, scale_row, got, projected),
        [((ROWS, CAP_ROWS), bf16, H), ((N_DP, SHARE, WIDE), bf16, H)],
        [
            pltpu.SMEM((HEADS,), jnp.int32), V((HD, D), f32),
            V((ROWS, CAP_ROWS), f32), V((ROWS, CAP_ROWS), bf16),
            V((N_DP, SHARE, WIDE), bf16), dma((7,)),
        ],
    )
    summed = exchange(pieces, ("z", "x"))

    half = ((A // 2, CAP_ROWS), bf16, V)
    even, odd, layer_out = call(
        input_kernel, "input_grad", [S] * 3 + [V] * 2 + [H] * 2,
        (frames, partner, moved_tiles, out_weight, got, scaled, layer_own),
        [half, half, ((ROWS, BAL_ROWS), bf16, V)],
        [V((ROWS, CAP_ROWS), bf16), V((ROWS, CAP_ROWS), bf16), dma((2,))],
        FREE,
    )
    left, other = add((even, crossed(odd, "c", NC, 1)), 2)
    summed, _ = lax.optimization_barrier((summed, left))
    copies, scale_grad = call(
        slots_kernel, "slots", [V], (summed,),
        [((NZ * HEADS, SHARE, ROWS), bf16, H), ((1, ROWS), f32, V)],
        [V((HEADS, SHARE, ROWS), bf16), dma((NZ,))],
    )
    owned = exchange(copies, ("z", "y", "c"))
    left, *others = add((left, crossed(other, "y", NY, 1)), 4)
    owned, _ = lax.optimization_barrier((owned, left))
    others = [crossed(other, "y", NY, step) for other, step in zip(others, (4, 2, 6))]
    (copies,) = call(
        join_kernel, "join", [V], (owned,),
        [((NX, BY_X, D), bf16, H)],
        [V((BY_X, D), f32), V((BY_X, D), bf16), dma((NX,))],
    )
    whole = exchange(copies, "x").reshape(HD, D)
    (ortho_update,) = call(
        ortho_kernel, "ortho", [V], (whole,), [((D, HD), bf16, H)],
        [V((D, HD), bf16), dma((PARTS,))],
    )
    left, others, ortho_update = lax.optimization_barrier((left, others, ortho_update))
    (input_grad,) = add((left, *others), 1)
    return (layer_out, input_grad, scale_grad.reshape(ROWS), ortho_update[:, None, :])


def solution(mesh):
    chips = Mesh(mesh.devices.reshape(NZ, NX, NY, NC), ("z", "x", "y", "c"))
    dp, fsdp = ("z", "x"), ("y", "c")
    placed = (
        P(None, dp),
        P(fsdp, dp),
        P(fsdp, dp),
        P(fsdp, None),
        P(fsdp),
        P(),
        P(),
        P(),
        P(),
    )
    return jax.shard_map(
        body,
        mesh=chips,
        in_specs=placed,
        out_specs=(P(fsdp, dp), P(fsdp, dp), P(fsdp), P(None, fsdp, None)),
        check_vma=False,
    )
```

```python
import functools
import math

import jax
import jax.numpy as jnp
from jax import lax
from jax.experimental import pallas as pl
from jax.experimental.pallas import tpu as pltpu
from jax.sharding import Mesh, PartitionSpec as P

D = 3200
HEADS = 16
HD = 128
FRAME = 256
TILE = 16
ITERS = 5
A = 2048
CAP_ROWS = 512
MOVE_ROWS = 256
BAL_ROWS = 384
N_DP = 32
N_FSDP = 16

NZ, NX, NY, NC = 8, 4, 8, 2
ROWS = D // N_FSDP
BY_X = HD // NX
SHARE = HD // N_DP
WIDE = D + HD
PAD_ROWS = 256
CHUNK = 512
PARTS = 5

coeff_linear = 3.4445
coeff_square = -4.775
coeff_cubic = 2.0315
EPSILON = 1e-07
INVERSE_ROOT = 1.0 / math.sqrt(N_DP * BAL_ROWS)

bf16 = jnp.bfloat16
f32 = jnp.float32

ROWS_BY_COLS = (((0,), (0,)), ((), ()))
COLS_BY_COLS = (((1,), (1,)), ((), ()))


def positions(shape, dimension):
    return lax.broadcasted_iota(jnp.int32, shape, dimension)


def dot(a, b, dims=(((1,), (0,)), ((), ()))):
    return lax.dot_general(a, b, dims, preferred_element_type=f32)


def same(size):
    return positions((size, size), 0) == positions((size, size), 1)


def to_column(row):
    size = row.shape[1]
    return jnp.sum(jnp.where(same(size), row, 0.0), axis=1, keepdims=True)


def to_row(column):
    size = column.shape[0]
    return jnp.sum(jnp.where(same(size), column, 0.0), axis=0, keepdims=True)


def my_counts(frames_ref, partner_ref, moved_ref):
    replica = lax.axis_index("z") * NX + lax.axis_index("x")
    mate = partner_ref[replica]
    kept = frames_ref[replica] * FRAME - moved_ref[replica] * TILE
    incoming = moved_ref[mate] * TILE
    holds_two = (frames_ref[replica] > frames_ref[mate]).astype(jnp.int32)
    return kept, incoming, holds_two


def light_places(kept, incoming):
    bal_col = positions((BAL_ROWS, MOVE_ROWS), 0)
    win_col = positions((BAL_ROWS, MOVE_ROWS), 1)
    hit = bal_col == win_col + (kept + incoming - MOVE_ROWS)
    hit = hit & (win_col >= MOVE_ROWS - incoming)
    return jnp.where(hit, 1.0, 0.0).astype(bf16)


def start(sems, *pairs):
    copies = [pltpu.make_async_copy(a, b, sems.at[i]) for i, (a, b) in enumerate(pairs)]
    for copy in copies:
        copy.start()
    return copies


def wait(copies):
    for copy in copies:
        copy.wait()


def project_kernel(
    frames_hbm, partner_hbm, moved_hbm,
    attended_hbm, residual_hbm, grad_hbm, weight_hbm, scale_hbm,
    projected_hbm, layer_hbm, window_ref,
    frames_ref, partner_ref, moved_ref,
    attended_ref, residual_ref, grad_ref, weight_ref, scale_ref,
    projected_ref, layer_ref,
    small_sems, attended_sems, weight_sems, out_sems,
):
    small = start(
        small_sems,
        (frames_hbm, frames_ref),
        (partner_hbm, partner_ref),
        (moved_hbm, moved_ref),
        (scale_hbm, scale_ref),
        (grad_hbm, grad_ref),
        (residual_hbm, residual_ref),
    )
    cuts = [pl.ds(first, CHUNK) for first in range(0, A, CHUNK)]
    attended = start(
        attended_sems, *[(attended_hbm.at[cut, :], attended_ref.at[cut, :]) for cut in cuts]
    )
    weight = start(
        weight_sems, *[(weight_hbm.at[:, cut], weight_ref.at[:, cut]) for cut in cuts]
    )
    wait(small[:5])
    kept, incoming, holds_two = my_counts(frames_ref, partner_ref, moved_ref)
    gains = to_column(scale_ref[...])
    grad_win = dot(grad_ref[...], light_places(kept, incoming))
    window_ref[pl.ds(ROWS, PAD_ROWS - ROWS), :] = jnp.zeros(
        (PAD_ROWS - ROWS, MOVE_ROWS), bf16
    )
    projected = None
    for index, cut in enumerate(cuts):
        attended[index].wait()
        weight[index].wait()
        part = dot(weight_ref[:, cut], attended_ref[cut, :])
        projected = part if projected is None else projected + part
    projected_ref[...] = projected
    out = start(out_sems, (projected_ref, projected_hbm))
    small[5].wait()
    layer = (residual_ref[...].astype(f32) + gains * projected).astype(bf16)
    layer_ref[...] = layer
    out += start(out_sems.at[pl.ds(1, 1)], (layer_ref, layer_hbm))
    layer_win = layer[:, MOVE_ROWS:].astype(f32)
    window_ref[pl.ds(0, ROWS), :] = jnp.where(holds_two == 1, layer_win, grad_win).astype(bf16)
    wait(out)


def forward_kernel(partner_ref, pieces_ref, out_ref):
    for replica in range(N_DP):
        out_ref[replica] = pieces_ref[partner_ref[replica]]


def send_lanes(first, last, value, pieces_ref, pieces_hbm, sems):
    lanes = pl.ds(first, last - first)
    for piece in range(N_DP):
        pieces_ref[piece, :, lanes] = value(piece, lanes)
    return start(sems, (pieces_ref.at[:, :, lanes], pieces_hbm.at[:, :, lanes]))


def weight_grad_kernel(
    frames_ref, partner_ref, moved_ref, slot_ref,
    attended_ref, grad_ref, scale_ref, got_ref, projected_hbm,
    scaled_hbm, pieces_hbm,
    head_of, wide, projected_ref, scaled_ref, pieces_ref, sems,
):
    (fetch,) = start(sems, (projected_hbm, projected_ref))
    kept, incoming, holds_two = my_counts(frames_ref, partner_ref, moved_ref)
    for head in range(HEADS):
        head_of[slot_ref[head]] = head
    own = grad_ref[...].astype(f32)
    own = jnp.concatenate([own, jnp.zeros((ROWS, CAP_ROWS - BAL_ROWS), f32)], axis=1)
    got = got_ref[pl.ds(0, ROWS), :].astype(f32)
    got = jnp.where(holds_two == 1, got, 0.0)
    got = jnp.concatenate([jnp.zeros((ROWS, CAP_ROWS - MOVE_ROWS), f32), got], axis=1)
    grad = jnp.where(positions((ROWS, CAP_ROWS), 1) < kept, own, got)
    scaled = (grad * to_column(scale_ref[...])).astype(bf16)
    scaled_ref[...] = scaled
    (store,) = start(sems.at[pl.ds(1, 1)], (scaled_ref, scaled_hbm))
    stores, done = [store], 0
    for slot in range(HEADS):
        first = pl.multiple_of(head_of[slot] * HD, HD)
        wide[:, pl.ds(slot * ROWS, ROWS)] = dot(
            attended_ref[pl.ds(first, HD), :], scaled, COLS_BY_COLS
        )
        if (slot + 1) % 4 == 0:
            full = (slot + 1) * ROWS // HD * HD
            stores += send_lanes(done, full, lambda piece, lanes: wide[
                pl.ds((piece % NX * NZ + piece // NX) * SHARE, SHARE), lanes
            ].astype(bf16), pieces_ref, pieces_hbm, sems.at[pl.ds(2 + slot // 4, 1)])
            done = full
    fetch.wait()
    part = jnp.sum(grad * projected_ref[...], axis=1, keepdims=True) * INVERSE_ROOT
    part = to_row(part)
    high = part.astype(bf16).astype(f32)
    low = part - high
    zeros = jnp.zeros((1, 2 * HD - ROWS), f32)
    lines = [
        high[:, :HD],
        jnp.concatenate([high[:, HD:], zeros], axis=1),
        low[:, :HD],
        jnp.concatenate([low[:, HD:], zeros], axis=1),
    ]
    lines = jnp.concatenate(lines, axis=0).astype(bf16)
    stores += send_lanes(
        D, WIDE, lambda piece, lanes: lines, pieces_ref, pieces_hbm, sems.at[pl.ds(6, 1)]
    )
    wait(stores)


def input_kernel(
    frames_ref, partner_ref, moved_ref,
    weight_ref, got_ref, scaled_hbm, layer_hbm,
    even_ref, odd_ref, layer_out_ref,
    scaled_ref, layer_ref, sems,
):
    fetch = start(sems, (scaled_hbm, scaled_ref), (layer_hbm, layer_ref))
    kept, incoming, holds_two = my_counts(frames_ref, partner_ref, moved_ref)
    block = lax.axis_index("y") * NC + lax.axis_index("c")
    fetch[0].wait()
    scaled = scaled_ref[...]
    for index, other in enumerate(EVEN):
        for ref, partner in ((even_ref, other), (odd_ref, other + 1)):
            first = pl.multiple_of((block ^ partner) * HD, HD)
            part = dot(weight_ref[:, pl.ds(first, HD)], scaled, ROWS_BY_COLS)
            ref[pl.ds(index * HD, HD), :] = part.astype(bf16)
    fetch[1].wait()
    received = dot(got_ref[pl.ds(0, ROWS), :], light_places(kept, incoming), COLS_BY_COLS)
    own = layer_ref[:, pl.ds(0, BAL_ROWS)].astype(f32)
    keep = positions((ROWS, BAL_ROWS), 1) < kept
    layer_out_ref[...] = jnp.where(keep, own, received).astype(bf16)


def slots_kernel(pieces_ref, copies_ref, scale_grad_ref):
    total = pieces_ref[0].astype(f32)
    for piece in range(1, N_DP):
        total = total + pieces_ref[piece].astype(f32)
    for slot in range(HEADS):
        part = total[:, slot * ROWS : (slot + 1) * ROWS].astype(bf16)
        for z in range(NZ):
            copies_ref[z * HEADS + slot] = part
    lines = total[0:2, D:] + total[2:4, D:]
    scale_grad_ref[...] = jnp.concatenate([lines[0:1, :], lines[1:2, : ROWS - HD]], axis=1)


def join_kernel(owned_ref, copies_hbm, joined, whole, sems):
    for z in range(NZ):
        for block in range(N_FSDP):
            joined[pl.ds(z * SHARE, SHARE), pl.ds(block * ROWS, ROWS)] = owned_ref[
                z * N_FSDP + block
            ].astype(f32)
    whole[...] = joined[...].astype(bf16)
    wait(start(sems, *[(whole, copies_hbm.at[x]) for x in range(NX)]))


def split(values):
    high = values.astype(bf16)
    return high, (values - high.astype(f32)).astype(bf16)


def mul(a, b):
    a_high, a_low = split(a)
    b_high, b_low = split(b)
    return dot(
        jnp.concatenate([a_high, a_high, a_low], axis=1),
        jnp.concatenate([b_high, b_low, b_high], axis=0),
    )


def ortho_kernel(grad_ref, out_hbm, out_ref, sems):
    grad = grad_ref[...]
    gram = dot(grad, grad, COLS_BY_COLS)
    eye = jnp.where(same(HD), 1.0, 0.0).astype(f32)
    squares = jnp.sum(jnp.sum(gram * eye, axis=1, keepdims=True), axis=0, keepdims=True)
    norm = jnp.sqrt(squares) + EPSILON
    gram = gram / norm / norm
    total = None
    for sweep in range(ITERS):
        step = coeff_linear * eye + coeff_square * gram + coeff_cubic * mul(gram, gram)
        total = step if total is None else mul(total, step)
        if sweep < ITERS - 1:
            gram = mul(mul(step, gram), step)
    total = jnp.concatenate(split(total * (0.2 * math.sqrt(D) / norm)), axis=1)
    stores = []
    for index, first in enumerate(range(0, D, D // PARTS)):
        cut = pl.ds(first, D // PARTS)
        out = dot(grad_ref[:, cut], total, ROWS_BY_COLS)
        out_ref[cut, :] = (out[:, :HD] + out[:, HD:]).astype(bf16)
        stores += start(sems.at[pl.ds(index, 1)], (out_ref.at[cut, :], out_hbm.at[cut, :]))
    wait(stores)


S, V, H = pltpu.SMEM, pltpu.VMEM, pltpu.HBM
FREE = pl.CostEstimate(flops=0, bytes_accessed=0, transcendentals=0)


def call(kernel, name, places, arrays, outs, scratch=(), cost=None):
    arrays = [
        pltpu.with_memory_space_constraint(array, H) if place is H else array
        for array, place in zip(arrays, places)
    ]
    return pl.pallas_call(
        kernel,
        out_shape=[
            H(shape, dtype) if place is H else jax.ShapeDtypeStruct(shape, dtype)
            for shape, dtype, place in outs
        ],
        in_specs=[pl.BlockSpec(memory_space=place) for place in places],
        out_specs=[pl.BlockSpec(memory_space=place) for shape, dtype, place in outs],
        scratch_shapes=list(scratch),
        compiler_params=pltpu.CompilerParams(vmem_limit_bytes=32 * 1024 * 1024),
        name=name,
        cost_estimate=cost,
    )(*arrays)


def exchange(pieces, axes):
    return lax.all_to_all(pieces, axes, split_axis=0, concat_axis=0, tiled=True)


def crossed(array, axis, size, bit):
    return lax.ppermute(array, axis, [(i, i ^ bit) for i in range(size)])


EVEN = (0, 4, 8, 2, 6, 10, 12, 14)


def add_kernel(*refs, blocks):
    count = len(blocks)
    in_refs, out_refs = refs[:-count], refs[-count:]
    first = 0
    for out_ref, size in zip(out_refs, blocks):
        cut = pl.ds(first * HD, size * HD)
        total = in_refs[0][cut, :].astype(f32)
        for ref in in_refs[1:]:
            total = total + ref[cut, :].astype(f32)
        out_ref[...] = total.astype(bf16)
        first += size


def add(arrays, *blocks):
    return call(
        functools.partial(add_kernel, blocks=blocks), "add", [V] * len(arrays), arrays,
        [((size * HD, CAP_ROWS), bf16, V) for size in blocks], cost=FREE,
    )


def body(
    attended, residual, grad_out, out_weight, layer_scale, frames, partner, moved_tiles, owner_slot
):
    scale_row = layer_scale[None, :]
    ints = pltpu.SMEM((N_DP,), jnp.int32)
    dma = pltpu.SemaphoreType.DMA

    projected, layer_own, window = call(
        project_kernel, "project", [H] * 8,
        (frames, partner, moved_tiles, attended, residual, grad_out, out_weight, scale_row),
        [((ROWS, CAP_ROWS), f32, H), ((ROWS, CAP_ROWS), bf16, H), ((PAD_ROWS, MOVE_ROWS), bf16, V)],
        [
            ints, ints, ints,
            V((A, CAP_ROWS), bf16), V((ROWS, CAP_ROWS), bf16), V((ROWS, BAL_ROWS), bf16),
            V((ROWS, A), bf16), V((1, ROWS), f32),
            V((ROWS, CAP_ROWS), f32), V((ROWS, CAP_ROWS), bf16),
            dma((6,)), dma((A // CHUNK,)), dma((A // CHUNK,)), dma((2,)),
        ],
    )
    pieces = exchange(window.reshape(N_DP, PAD_ROWS // N_DP, MOVE_ROWS), ("z", "x"))
    (pieces,) = call(
        forward_kernel, "forward", [S, V], (partner, pieces),
        [((N_DP, PAD_ROWS // N_DP, MOVE_ROWS), bf16, V)],
    )
    pieces = exchange(pieces, ("z", "x"))
    got = pieces.reshape(PAD_ROWS, MOVE_ROWS)

    scaled, pieces = call(
        weight_grad_kernel, "weight_grad", [S] * 4 + [V] * 4 + [H],
        (frames, partner, moved_tiles, owner_slot, attended, grad_out, scale_row, got, projected),
        [((ROWS, CAP_ROWS), bf16, H), ((N_DP, SHARE, WIDE), bf16, H)],
        [
            pltpu.SMEM((HEADS,), jnp.int32), V((HD, D), f32),
            V((ROWS, CAP_ROWS), f32), V((ROWS, CAP_ROWS), bf16),
            V((N_DP, SHARE, WIDE), bf16), dma((7,)),
        ],
    )
    summed = exchange(pieces, ("z", "x"))

    half = ((A // 2, CAP_ROWS), bf16, V)
    even, odd, layer_out = call(
        input_kernel, "input_grad", [S] * 3 + [V] * 2 + [H] * 2,
        (frames, partner, moved_tiles, out_weight, got, scaled, layer_own),
        [half, half, ((ROWS, BAL_ROWS), bf16, V)],
        [V((ROWS, CAP_ROWS), bf16), V((ROWS, CAP_ROWS), bf16), dma((2,))],
        FREE,
    )
    left, near, *far = add((even, crossed(odd, "c", NC, 1)), 3, 3, 1, 1)
    far = [crossed(other, "y", NY, step) for other, step in zip(far, (6, 7))]
    left, *others = add((left, crossed(near, "y", NY, 1)), 1, 1, 1)
    summed, _ = lax.optimization_barrier((summed, (left, far)))
    copies, scale_grad = call(
        slots_kernel, "slots", [V], (summed,),
        [((NZ * HEADS, SHARE, ROWS), bf16, V), ((1, ROWS), f32, V)],
    )
    owned = exchange(copies, ("z", "y", "c"))
    far += [crossed(other, "y", NY, step) for other, step in zip(others, (2, 4))]
    (copies,) = call(
        join_kernel, "join", [V], (owned,),
        [((NX, BY_X, D), bf16, H)],
        [V((BY_X, D), f32), V((BY_X, D), bf16), dma((NX,))],
    )
    whole = exchange(copies, "x").reshape(HD, D)
    (ortho_update,) = call(
        ortho_kernel, "ortho", [V], (whole,), [((D, HD), bf16, H)],
        [V((D, HD), bf16), dma((PARTS,))],
    )
    left, far, ortho_update = lax.optimization_barrier((left, far, ortho_update))
    (input_grad,) = add((left, *far), 1)
    return (layer_out, input_grad, scale_grad.reshape(ROWS), ortho_update[:, None, :])


def solution(mesh):
    chips = Mesh(mesh.devices.reshape(NZ, NX, NY, NC), ("z", "x", "y", "c"))
    dp, fsdp = ("z", "x"), ("y", "c")
    placed = (
        P(None, dp),
        P(fsdp, dp),
        P(fsdp, dp),
        P(fsdp, None),
        P(fsdp),
        P(),
        P(),
        P(),
        P(),
    )
    return jax.shard_map(
        body,
        mesh=chips,
        in_specs=placed,
        out_specs=(P(fsdp, dp), P(fsdp, dp), P(fsdp), P(None, fsdp, None)),
        check_vma=False,
    )
```

```python
import functools
import math

import jax
import jax.numpy as jnp
from jax import lax
from jax.experimental import pallas as pl
from jax.experimental.pallas import tpu as pltpu
from jax.sharding import Mesh, PartitionSpec as P

D = 3200
HEADS = 16
HD = 128
FRAME = 256
TILE = 16
ITERS = 5
A = 2048
CAP_ROWS = 512
MOVE_ROWS = 256
BAL_ROWS = 384
N_DP = 32
N_FSDP = 16

NZ, NX, NY, NC = 8, 4, 8, 2
ROWS = D // N_FSDP
BY_X = HD // NX
SHARE = HD // N_DP
WIDE = D + HD
PAD_ROWS = 256
CHUNK = 512
PARTS = 5

coeff_linear = 3.4445
coeff_square = -4.775
coeff_cubic = 2.0315
EPSILON = 1e-07
INVERSE_ROOT = 1.0 / math.sqrt(N_DP * BAL_ROWS)

bf16 = jnp.bfloat16
f32 = jnp.float32

ROWS_BY_COLS = (((0,), (0,)), ((), ()))
COLS_BY_COLS = (((1,), (1,)), ((), ()))


def positions(shape, dimension):
    return lax.broadcasted_iota(jnp.int32, shape, dimension)


def dot(a, b, dims=(((1,), (0,)), ((), ()))):
    return lax.dot_general(a, b, dims, preferred_element_type=f32)


def same(size):
    return positions((size, size), 0) == positions((size, size), 1)


def to_column(row):
    size = row.shape[1]
    return jnp.sum(jnp.where(same(size), row, 0.0), axis=1, keepdims=True)


def to_row(column):
    size = column.shape[0]
    return jnp.sum(jnp.where(same(size), column, 0.0), axis=0, keepdims=True)


def my_counts(frames_ref, partner_ref, moved_ref):
    replica = lax.axis_index("z") * NX + lax.axis_index("x")
    mate = partner_ref[replica]
    kept = frames_ref[replica] * FRAME - moved_ref[replica] * TILE
    incoming = moved_ref[mate] * TILE
    holds_two = (frames_ref[replica] > frames_ref[mate]).astype(jnp.int32)
    return kept, incoming, holds_two


def light_places(kept, incoming):
    bal_col = positions((BAL_ROWS, MOVE_ROWS), 0)
    win_col = positions((BAL_ROWS, MOVE_ROWS), 1)
    hit = bal_col == win_col + (kept + incoming - MOVE_ROWS)
    hit = hit & (win_col >= MOVE_ROWS - incoming)
    return jnp.where(hit, 1.0, 0.0).astype(bf16)


def start(sems, *pairs):
    copies = [pltpu.make_async_copy(a, b, sems.at[i]) for i, (a, b) in enumerate(pairs)]
    for copy in copies:
        copy.start()
    return copies


def wait(copies):
    for copy in copies:
        copy.wait()


def project_kernel(
    frames_hbm, partner_hbm, moved_hbm,
    attended_hbm, residual_hbm, grad_hbm, weight_hbm, scale_hbm,
    projected_hbm, layer_hbm, window_ref,
    frames_ref, partner_ref, moved_ref,
    attended_ref, residual_ref, grad_ref, weight_ref, scale_ref,
    projected_ref, layer_ref,
    small_sems, attended_sems, weight_sems, out_sems,
):
    small = start(
        small_sems,
        (frames_hbm, frames_ref),
        (partner_hbm, partner_ref),
        (moved_hbm, moved_ref),
        (scale_hbm, scale_ref),
        (grad_hbm, grad_ref),
        (residual_hbm, residual_ref),
    )
    cuts = [pl.ds(first, CHUNK) for first in range(0, A, CHUNK)]
    attended = start(
        attended_sems, *[(attended_hbm.at[cut, :], attended_ref.at[cut, :]) for cut in cuts]
    )
    weight = start(
        weight_sems, *[(weight_hbm.at[:, cut], weight_ref.at[:, cut]) for cut in cuts]
    )
    wait(small[:5])
    kept, incoming, holds_two = my_counts(frames_ref, partner_ref, moved_ref)
    gains = to_column(scale_ref[...])
    grad_win = dot(grad_ref[...], light_places(kept, incoming))
    window_ref[pl.ds(ROWS, PAD_ROWS - ROWS), :] = jnp.zeros(
        (PAD_ROWS - ROWS, MOVE_ROWS), bf16
    )
    projected = None
    for index, cut in enumerate(cuts):
        attended[index].wait()
        weight[index].wait()
        part = dot(weight_ref[:, cut], attended_ref[cut, :])
        projected = part if projected is None else projected + part
    projected_ref[...] = projected
    out = start(out_sems, (projected_ref, projected_hbm))
    small[5].wait()
    layer = (residual_ref[...].astype(f32) + gains * projected).astype(bf16)
    layer_ref[...] = layer
    out += start(out_sems.at[pl.ds(1, 1)], (layer_ref, layer_hbm))
    layer_win = layer[:, MOVE_ROWS:].astype(f32)
    window_ref[pl.ds(0, ROWS), :] = jnp.where(holds_two == 1, layer_win, grad_win).astype(bf16)
    wait(out)


def forward_kernel(partner_ref, pieces_ref, out_ref):
    for replica in range(N_DP):
        out_ref[replica] = pieces_ref[partner_ref[replica]]


def send_lanes(first, last, value, pieces_ref, pieces_hbm, sems):
    lanes = pl.ds(first, last - first)
    for piece in range(N_DP):
        pieces_ref[piece, :, lanes] = value(piece, lanes)
    return start(sems, (pieces_ref.at[:, :, lanes], pieces_hbm.at[:, :, lanes]))


def weight_grad_kernel(
    frames_ref, partner_ref, moved_ref, slot_ref,
    attended_ref, grad_ref, scale_ref, got_ref, projected_hbm,
    scaled_hbm, pieces_hbm,
    head_of, wide, projected_ref, scaled_ref, pieces_ref, sems,
):
    (fetch,) = start(sems, (projected_hbm, projected_ref))
    kept, incoming, holds_two = my_counts(frames_ref, partner_ref, moved_ref)
    for head in range(HEADS):
        head_of[slot_ref[head]] = head
    own = grad_ref[...].astype(f32)
    own = jnp.concatenate([own, jnp.zeros((ROWS, CAP_ROWS - BAL_ROWS), f32)], axis=1)
    got = got_ref[pl.ds(0, ROWS), :].astype(f32)
    got = jnp.where(holds_two == 1, got, 0.0)
    got = jnp.concatenate([jnp.zeros((ROWS, CAP_ROWS - MOVE_ROWS), f32), got], axis=1)
    grad = jnp.where(positions((ROWS, CAP_ROWS), 1) < kept, own, got)
    scaled = (grad * to_column(scale_ref[...])).astype(bf16)
    scaled_ref[...] = scaled
    (store,) = start(sems.at[pl.ds(1, 1)], (scaled_ref, scaled_hbm))
    stores, done = [store], 0
    for slot in range(HEADS):
        first = pl.multiple_of(head_of[slot] * HD, HD)
        wide[:, pl.ds(slot * ROWS, ROWS)] = dot(
            attended_ref[pl.ds(first, HD), :], scaled, COLS_BY_COLS
        )
        if (slot + 1) % 4 == 0:
            full = (slot + 1) * ROWS // HD * HD
            stores += send_lanes(done, full, lambda piece, lanes: wide[
                pl.ds((piece % NX * NZ + piece // NX) * SHARE, SHARE), lanes
            ].astype(bf16), pieces_ref, pieces_hbm, sems.at[pl.ds(2 + slot // 4, 1)])
            done = full
    fetch.wait()
    part = jnp.sum(grad * projected_ref[...], axis=1, keepdims=True) * INVERSE_ROOT
    part = to_row(part)
    high = part.astype(bf16).astype(f32)
    low = part - high
    zeros = jnp.zeros((1, 2 * HD - ROWS), f32)
    lines = [
        high[:, :HD],
        jnp.concatenate([high[:, HD:], zeros], axis=1),
        low[:, :HD],
        jnp.concatenate([low[:, HD:], zeros], axis=1),
    ]
    lines = jnp.concatenate(lines, axis=0).astype(bf16)
    stores += send_lanes(
        D, WIDE, lambda piece, lanes: lines, pieces_ref, pieces_hbm, sems.at[pl.ds(6, 1)]
    )
    wait(stores)


def input_kernel(
    frames_ref, partner_ref, moved_ref,
    weight_ref, got_ref, scaled_hbm, layer_hbm,
    even_ref, odd_ref, layer_out_ref,
    scaled_ref, layer_ref, sems,
):
    fetch = start(sems, (scaled_hbm, scaled_ref), (layer_hbm, layer_ref))
    kept, incoming, holds_two = my_counts(frames_ref, partner_ref, moved_ref)
    y, c = lax.axis_index("y"), lax.axis_index("c")
    fetch[0].wait()
    scaled = scaled_ref[...]
    for index, step in enumerate(STEPS):
        for ref, core in ((even_ref, c), (odd_ref, 1 - c)):
            first = pl.multiple_of((lax.rem(y + step + NY, NY) * NC + core) * HD, HD)
            part = dot(weight_ref[:, pl.ds(first, HD)], scaled, ROWS_BY_COLS)
            ref[pl.ds(index * HD, HD), :] = part.astype(bf16)
    fetch[1].wait()
    received = dot(got_ref[pl.ds(0, ROWS), :], light_places(kept, incoming), COLS_BY_COLS)
    own = layer_ref[:, pl.ds(0, BAL_ROWS)].astype(f32)
    keep = positions((ROWS, BAL_ROWS), 1) < kept
    layer_out_ref[...] = jnp.where(keep, own, received).astype(bf16)


def slots_kernel(pieces_ref, copies_ref, scale_grad_ref):
    total = pieces_ref[0].astype(f32)
    for piece in range(1, N_DP):
        total = total + pieces_ref[piece].astype(f32)
    for slot in range(HEADS):
        part = total[:, slot * ROWS : (slot + 1) * ROWS].astype(bf16)
        for z in range(NZ):
            copies_ref[z * HEADS + slot] = part
    lines = total[0:2, D:] + total[2:4, D:]
    scale_grad_ref[...] = jnp.concatenate([lines[0:1, :], lines[1:2, : ROWS - HD]], axis=1)


def join_kernel(owned_ref, copies_hbm, joined, whole, sems):
    for z in range(NZ):
        for block in range(N_FSDP):
            joined[pl.ds(z * SHARE, SHARE), pl.ds(block * ROWS, ROWS)] = owned_ref[
                z * N_FSDP + block
            ].astype(f32)
    whole[...] = joined[...].astype(bf16)
    wait(start(sems, *[(whole, copies_hbm.at[x]) for x in range(NX)]))


def split(values):
    high = values.astype(bf16)
    return high, (values - high.astype(f32)).astype(bf16)


def mul(a, b):
    a_high, a_low = split(a)
    b_high, b_low = split(b)
    return dot(
        jnp.concatenate([a_high, a_high, a_low], axis=1),
        jnp.concatenate([b_high, b_low, b_high], axis=0),
    )


def ortho_kernel(grad_ref, out_hbm, out_ref, sems):
    grad = grad_ref[...]
    gram = dot(grad, grad, COLS_BY_COLS)
    eye = jnp.where(same(HD), 1.0, 0.0).astype(f32)
    squares = jnp.sum(jnp.sum(gram * eye, axis=1, keepdims=True), axis=0, keepdims=True)
    norm = jnp.sqrt(squares) + EPSILON
    gram = gram / norm / norm
    total = None
    for sweep in range(ITERS):
        step = coeff_linear * eye + coeff_square * gram + coeff_cubic * mul(gram, gram)
        total = step if total is None else mul(total, step)
        if sweep < ITERS - 1:
            gram = mul(mul(step, gram), step)
    total = jnp.concatenate(split(total * (0.2 * math.sqrt(D) / norm)), axis=1)
    stores = []
    for index, first in enumerate(range(0, D, D // PARTS)):
        cut = pl.ds(first, D // PARTS)
        out = dot(grad_ref[:, cut], total, ROWS_BY_COLS)
        out_ref[cut, :] = (out[:, :HD] + out[:, HD:]).astype(bf16)
        stores += start(sems.at[pl.ds(index, 1)], (out_ref.at[cut, :], out_hbm.at[cut, :]))
    wait(stores)


S, V, H = pltpu.SMEM, pltpu.VMEM, pltpu.HBM
FREE = pl.CostEstimate(flops=0, bytes_accessed=0, transcendentals=0)


def call(kernel, name, places, arrays, outs, scratch=(), cost=None):
    arrays = [
        pltpu.with_memory_space_constraint(array, H) if place is H else array
        for array, place in zip(arrays, places)
    ]
    return pl.pallas_call(
        kernel,
        out_shape=[
            H(shape, dtype) if place is H else jax.ShapeDtypeStruct(shape, dtype)
            for shape, dtype, place in outs
        ],
        in_specs=[pl.BlockSpec(memory_space=place) for place in places],
        out_specs=[pl.BlockSpec(memory_space=place) for shape, dtype, place in outs],
        scratch_shapes=list(scratch),
        compiler_params=pltpu.CompilerParams(vmem_limit_bytes=32 * 1024 * 1024),
        name=name,
        cost_estimate=cost,
    )(*arrays)


def exchange(pieces, axes):
    return lax.all_to_all(pieces, axes, split_axis=0, concat_axis=0, tiled=True)


def shifted(array, axis, size, step):
    return lax.ppermute(array, axis, [(i, (i + step) % size) for i in range(size)])


STEPS = (0, -3, 3, -1, -4, 2, 1, -2)


def add_kernel(*refs, blocks):
    count = len(blocks)
    in_refs, out_refs = refs[:-count], refs[-count:]
    first = 0
    for out_ref, size in zip(out_refs, blocks):
        cut = pl.ds(first * HD, size * HD)
        total = in_refs[0][cut, :].astype(f32)
        first += size
        for ref in in_refs[1:]:
            if ref.shape[0] >= first * HD:
                total = total + ref[cut, :].astype(f32)
        out_ref[...] = total.astype(bf16)


def add(arrays, *blocks):
    return call(
        functools.partial(add_kernel, blocks=blocks), "add", [V] * len(arrays), arrays,
        [((size * HD, CAP_ROWS), bf16, V) for size in blocks], cost=FREE,
    )


def body(
    attended, residual, grad_out, out_weight, layer_scale, frames, partner, moved_tiles, owner_slot
):
    scale_row = layer_scale[None, :]
    ints = pltpu.SMEM((N_DP,), jnp.int32)
    dma = pltpu.SemaphoreType.DMA

    projected, layer_own, window = call(
        project_kernel, "project", [H] * 8,
        (frames, partner, moved_tiles, attended, residual, grad_out, out_weight, scale_row),
        [((ROWS, CAP_ROWS), f32, H), ((ROWS, CAP_ROWS), bf16, H), ((PAD_ROWS, MOVE_ROWS), bf16, V)],
        [
            ints, ints, ints,
            V((A, CAP_ROWS), bf16), V((ROWS, CAP_ROWS), bf16), V((ROWS, BAL_ROWS), bf16),
            V((ROWS, A), bf16), V((1, ROWS), f32),
            V((ROWS, CAP_ROWS), f32), V((ROWS, CAP_ROWS), bf16),
            dma((6,)), dma((A // CHUNK,)), dma((A // CHUNK,)), dma((2,)),
        ],
    )
    pieces = exchange(window.reshape(N_DP, PAD_ROWS // N_DP, MOVE_ROWS), ("z", "x"))
    (pieces,) = call(
        forward_kernel, "forward", [S, V], (partner, pieces),
        [((N_DP, PAD_ROWS // N_DP, MOVE_ROWS), bf16, V)],
    )
    pieces = exchange(pieces, ("z", "x"))
    got = pieces.reshape(PAD_ROWS, MOVE_ROWS)

    scaled, pieces = call(
        weight_grad_kernel, "weight_grad", [S] * 4 + [V] * 4 + [H],
        (frames, partner, moved_tiles, owner_slot, attended, grad_out, scale_row, got, projected),
        [((ROWS, CAP_ROWS), bf16, H), ((N_DP, SHARE, WIDE), bf16, H)],
        [
            pltpu.SMEM((HEADS,), jnp.int32), V((HD, D), f32),
            V((ROWS, CAP_ROWS), f32), V((ROWS, CAP_ROWS), bf16),
            V((N_DP, SHARE, WIDE), bf16), dma((7,)),
        ],
    )
    summed = exchange(pieces, ("z", "x"))

    half = ((A // 2, CAP_ROWS), bf16, V)
    even, odd, layer_out = call(
        input_kernel, "input_grad", [S] * 3 + [V] * 2 + [H] * 2,
        (frames, partner, moved_tiles, out_weight, got, scaled, layer_own),
        [half, half, ((ROWS, BAL_ROWS), bf16, V)],
        [V((ROWS, CAP_ROWS), bf16), V((ROWS, CAP_ROWS), bf16), dma((2,))],
        FREE,
    )
    keep, below, above = add((even, shifted(odd, "c", NC, 1)), 3, 3, 2)
    below, above = shifted(below, "y", NY, -1), shifted(above, "y", NY, 1)
    keep, below, above = add((keep, below, above), 1, 1, 1)
    summed, _ = lax.optimization_barrier((summed, keep))
    copies, scale_grad = call(
        slots_kernel, "slots", [V], (summed,),
        [((NZ * HEADS, SHARE, ROWS), bf16, V), ((1, ROWS), f32, V)],
    )
    owned = exchange(copies, ("z", "y", "c"))
    (copies,) = call(
        join_kernel, "join", [V], (owned,),
        [((NX, BY_X, D), bf16, H)],
        [V((BY_X, D), f32), V((BY_X, D), bf16), dma((NX,))],
    )
    below, above = shifted(below, "y", NY, -3), shifted(above, "y", NY, 3)
    whole = exchange(copies, "x").reshape(HD, D)
    (ortho_update,) = call(
        ortho_kernel, "ortho", [V], (whole,), [((D, HD), bf16, H)],
        [V((D, HD), bf16), dma((PARTS,))],
    )
    keep, below, above, ortho_update = lax.optimization_barrier((keep, below, above, ortho_update))
    (input_grad,) = add((keep, below, above), 1)
    return (layer_out, input_grad, scale_grad.reshape(ROWS), ortho_update[:, None, :])


def solution(mesh):
    chips = Mesh(mesh.devices.reshape(NZ, NX, NY, NC), ("z", "x", "y", "c"))
    dp, fsdp = ("z", "x"), ("y", "c")
    placed = (
        P(None, dp),
        P(fsdp, dp),
        P(fsdp, dp),
        P(fsdp, None),
        P(fsdp),
        P(),
        P(),
        P(),
        P(),
    )
    return jax.shard_map(
        body,
        mesh=chips,
        in_specs=placed,
        out_specs=(P(fsdp, dp), P(fsdp, dp), P(fsdp), P(None, fsdp, None)),
        check_vma=False,
    )
```

```python
import functools
import math

import jax
import jax.numpy as jnp
from jax import lax
from jax.experimental import pallas as pl
from jax.experimental.pallas import tpu as pltpu
from jax.sharding import Mesh, PartitionSpec as P

D = 3200
HEADS = 16
HD = 128
FRAME = 256
TILE = 16
ITERS = 5
A = 2048
CAP_ROWS = 512
MOVE_ROWS = 256
BAL_ROWS = 384
N_DP = 32
N_FSDP = 16

NZ, NX, NY, NC = 8, 4, 8, 2
ROWS = D // N_FSDP
BY_X = HD // NX
SHARE = HD // N_DP
WIDE = D + HD
PAD_ROWS = 256
CHUNK = 512
PARTS = 5

coeff_linear = 3.4445
coeff_square = -4.775
coeff_cubic = 2.0315
EPSILON = 1e-07
INVERSE_ROOT = 1.0 / math.sqrt(N_DP * BAL_ROWS)

bf16 = jnp.bfloat16
f32 = jnp.float32

ROWS_BY_COLS = (((0,), (0,)), ((), ()))
COLS_BY_COLS = (((1,), (1,)), ((), ()))


def positions(shape, dimension):
    return lax.broadcasted_iota(jnp.int32, shape, dimension)


def dot(a, b, dims=(((1,), (0,)), ((), ()))):
    return lax.dot_general(a, b, dims, preferred_element_type=f32)


def same(size):
    return positions((size, size), 0) == positions((size, size), 1)


def to_column(row):
    size = row.shape[1]
    return jnp.sum(jnp.where(same(size), row, 0.0), axis=1, keepdims=True)


def to_row(column):
    size = column.shape[0]
    return jnp.sum(jnp.where(same(size), column, 0.0), axis=0, keepdims=True)


def my_counts(frames_ref, partner_ref, moved_ref):
    replica = lax.axis_index("z") * NX + lax.axis_index("x")
    mate = partner_ref[replica]
    kept = frames_ref[replica] * FRAME - moved_ref[replica] * TILE
    incoming = moved_ref[mate] * TILE
    holds_two = (frames_ref[replica] > frames_ref[mate]).astype(jnp.int32)
    return kept, incoming, holds_two


def light_places(kept, incoming):
    bal_col = positions((BAL_ROWS, MOVE_ROWS), 0)
    win_col = positions((BAL_ROWS, MOVE_ROWS), 1)
    hit = bal_col == win_col + (kept + incoming - MOVE_ROWS)
    hit = hit & (win_col >= MOVE_ROWS - incoming)
    return jnp.where(hit, 1.0, 0.0).astype(bf16)


def start(sems, *pairs):
    copies = [pltpu.make_async_copy(a, b, sems.at[i]) for i, (a, b) in enumerate(pairs)]
    for copy in copies:
        copy.start()
    return copies


def wait(copies):
    for copy in copies:
        copy.wait()


def project_kernel(
    frames_hbm, partner_hbm, moved_hbm,
    attended_hbm, residual_hbm, grad_hbm, weight_hbm, scale_hbm,
    projected_hbm, layer_hbm, window_ref,
    frames_ref, partner_ref, moved_ref,
    attended_ref, residual_ref, grad_ref, weight_ref, scale_ref,
    projected_ref, layer_ref,
    small_sems, attended_sems, weight_sems, out_sems,
):
    small = start(
        small_sems,
        (frames_hbm, frames_ref),
        (partner_hbm, partner_ref),
        (moved_hbm, moved_ref),
        (scale_hbm, scale_ref),
        (grad_hbm, grad_ref),
        (residual_hbm, residual_ref),
    )
    cuts = [pl.ds(first, CHUNK) for first in range(0, A, CHUNK)]
    attended = start(
        attended_sems, *[(attended_hbm.at[cut, :], attended_ref.at[cut, :]) for cut in cuts]
    )
    weight = start(
        weight_sems, *[(weight_hbm.at[:, cut], weight_ref.at[:, cut]) for cut in cuts]
    )
    wait(small[:5])
    kept, incoming, holds_two = my_counts(frames_ref, partner_ref, moved_ref)
    gains = to_column(scale_ref[...])
    grad_win = dot(grad_ref[...], light_places(kept, incoming))
    window_ref[pl.ds(ROWS, PAD_ROWS - ROWS), :] = jnp.zeros(
        (PAD_ROWS - ROWS, MOVE_ROWS), bf16
    )
    projected = None
    for index, cut in enumerate(cuts):
        attended[index].wait()
        weight[index].wait()
        part = dot(weight_ref[:, cut], attended_ref[cut, :])
        projected = part if projected is None else projected + part
    projected_ref[...] = projected
    out = start(out_sems, (projected_ref, projected_hbm))
    small[5].wait()
    layer = (residual_ref[...].astype(f32) + gains * projected).astype(bf16)
    layer_ref[...] = layer
    out += start(out_sems.at[pl.ds(1, 1)], (layer_ref, layer_hbm))
    layer_win = layer[:, MOVE_ROWS:].astype(f32)
    window_ref[pl.ds(0, ROWS), :] = jnp.where(holds_two == 1, layer_win, grad_win).astype(bf16)
    wait(out)


def forward_kernel(partner_ref, pieces_ref, out_ref):
    for replica in range(N_DP):
        out_ref[replica] = pieces_ref[partner_ref[replica]]


def send_lanes(first, last, value, pieces_ref, pieces_hbm, sems):
    lanes = pl.ds(first, last - first)
    for piece in range(N_DP):
        pieces_ref[piece, :, lanes] = value(piece, lanes)
    return start(sems, (pieces_ref.at[:, :, lanes], pieces_hbm.at[:, :, lanes]))


def weight_grad_kernel(
    frames_ref, partner_ref, moved_ref, slot_ref,
    attended_ref, grad_ref, scale_ref, got_ref, projected_hbm,
    scaled_hbm, pieces_hbm,
    head_of, wide, projected_ref, scaled_ref, pieces_ref, sems,
):
    (fetch,) = start(sems, (projected_hbm, projected_ref))
    kept, incoming, holds_two = my_counts(frames_ref, partner_ref, moved_ref)
    for head in range(HEADS):
        head_of[slot_ref[head]] = head
    own = grad_ref[...].astype(f32)
    own = jnp.concatenate([own, jnp.zeros((ROWS, CAP_ROWS - BAL_ROWS), f32)], axis=1)
    got = got_ref[pl.ds(0, ROWS), :].astype(f32)
    got = jnp.where(holds_two == 1, got, 0.0)
    got = jnp.concatenate([jnp.zeros((ROWS, CAP_ROWS - MOVE_ROWS), f32), got], axis=1)
    grad = jnp.where(positions((ROWS, CAP_ROWS), 1) < kept, own, got)
    scaled = (grad * to_column(scale_ref[...])).astype(bf16)
    scaled_ref[...] = scaled
    (store,) = start(sems.at[pl.ds(1, 1)], (scaled_ref, scaled_hbm))
    stores, done = [store], 0
    for slot in range(HEADS):
        first = pl.multiple_of(head_of[slot] * HD, HD)
        wide[:, pl.ds(slot * ROWS, ROWS)] = dot(
            attended_ref[pl.ds(first, HD), :], scaled, COLS_BY_COLS
        )
        if (slot + 1) % 4 == 0:
            full = (slot + 1) * ROWS // HD * HD
            stores += send_lanes(done, full, lambda piece, lanes: wide[
                pl.ds((piece % NX * NZ + piece // NX) * SHARE, SHARE), lanes
            ].astype(bf16), pieces_ref, pieces_hbm, sems.at[pl.ds(2 + slot // 4, 1)])
            done = full
    fetch.wait()
    part = jnp.sum(grad * projected_ref[...], axis=1, keepdims=True) * INVERSE_ROOT
    part = to_row(part)
    high = part.astype(bf16).astype(f32)
    low = part - high
    zeros = jnp.zeros((1, 2 * HD - ROWS), f32)
    lines = [
        high[:, :HD],
        jnp.concatenate([high[:, HD:], zeros], axis=1),
        low[:, :HD],
        jnp.concatenate([low[:, HD:], zeros], axis=1),
    ]
    lines = jnp.concatenate(lines, axis=0).astype(bf16)
    stores += send_lanes(
        D, WIDE, lambda piece, lanes: lines, pieces_ref, pieces_hbm, sems.at[pl.ds(6, 1)]
    )
    wait(stores)


def input_kernel(
    frames_ref, partner_ref, moved_ref,
    weight_ref, got_ref, scaled_hbm, layer_hbm,
    even_ref, odd_ref, layer_out_ref,
    scaled_ref, layer_ref, sems,
):
    fetch = start(sems, (scaled_hbm, scaled_ref), (layer_hbm, layer_ref))
    kept, incoming, holds_two = my_counts(frames_ref, partner_ref, moved_ref)
    block = lax.axis_index("y") * NC + lax.axis_index("c")
    fetch[0].wait()
    scaled = scaled_ref[...]
    for index, other in enumerate(EVEN):
        for ref, partner in ((even_ref, other), (odd_ref, other + 1)):
            first = pl.multiple_of((block ^ partner) * HD, HD)
            part = dot(weight_ref[:, pl.ds(first, HD)], scaled, ROWS_BY_COLS)
            ref[pl.ds(index * HD, HD), :] = part.astype(bf16)
    fetch[1].wait()
    received = dot(got_ref[pl.ds(0, ROWS), :], light_places(kept, incoming), COLS_BY_COLS)
    own = layer_ref[:, pl.ds(0, BAL_ROWS)].astype(f32)
    keep = positions((ROWS, BAL_ROWS), 1) < kept
    layer_out_ref[...] = jnp.where(keep, own, received).astype(bf16)


def slots_kernel(pieces_ref, copies_hbm, scale_grad_ref, by_slot, sems):
    total = pieces_ref[0].astype(f32)
    for piece in range(1, N_DP):
        total = total + pieces_ref[piece].astype(f32)
    for slot in range(HEADS):
        by_slot[slot] = total[:, slot * ROWS : (slot + 1) * ROWS].astype(bf16)
    copies = [
        (by_slot, copies_hbm.at[pl.ds(z * HEADS, HEADS)]) for z in range(NZ)
    ]
    copies = start(sems, *copies)
    lines = total[0:2, D:] + total[2:4, D:]
    scale_grad_ref[...] = jnp.concatenate([lines[0:1, :], lines[1:2, : ROWS - HD]], axis=1)
    wait(copies)


def join_kernel(owned_ref, whole_ref, joined):
    for z in range(NZ):
        for block in range(N_FSDP):
            joined[pl.ds(z * SHARE, SHARE), pl.ds(block * ROWS, ROWS)] = owned_ref[
                z * N_FSDP + block
            ].astype(f32)
    whole_ref[...] = joined[...].astype(bf16)


def split(values):
    high = values.astype(bf16)
    return high, (values - high.astype(f32)).astype(bf16)


def mul(a, b):
    a_high, a_low = split(a)
    b_high, b_low = split(b)
    return dot(
        jnp.concatenate([a_high, a_high, a_low], axis=1),
        jnp.concatenate([b_high, b_low, b_high], axis=0),
    )


def ortho_kernel(grad_ref, out_hbm, out_ref, sems):
    grad = grad_ref[...]
    gram = dot(grad, grad, COLS_BY_COLS)
    eye = jnp.where(same(HD), 1.0, 0.0).astype(f32)
    squares = jnp.sum(jnp.sum(gram * eye, axis=1, keepdims=True), axis=0, keepdims=True)
    norm = jnp.sqrt(squares) + EPSILON
    gram = gram / norm / norm
    total = None
    for sweep in range(ITERS):
        step = coeff_linear * eye + coeff_square * gram + coeff_cubic * mul(gram, gram)
        total = step if total is None else mul(total, step)
        if sweep < ITERS - 1:
            gram = mul(mul(step, gram), step)
    total = jnp.concatenate(split(total * (0.2 * math.sqrt(D) / norm)), axis=1)
    stores = []
    for index, first in enumerate(range(0, D, D // PARTS)):
        cut = pl.ds(first, D // PARTS)
        out = dot(grad_ref[:, cut], total, ROWS_BY_COLS)
        out_ref[cut, :] = (out[:, :HD] + out[:, HD:]).astype(bf16)
        stores += start(sems.at[pl.ds(index, 1)], (out_ref.at[cut, :], out_hbm.at[cut, :]))
    wait(stores)


S, V, H = pltpu.SMEM, pltpu.VMEM, pltpu.HBM
FREE = pl.CostEstimate(flops=0, bytes_accessed=0, transcendentals=0)


def call(kernel, name, places, arrays, outs, scratch=(), cost=None):
    arrays = [
        pltpu.with_memory_space_constraint(array, H) if place is H else array
        for array, place in zip(arrays, places)
    ]
    return pl.pallas_call(
        kernel,
        out_shape=[
            H(shape, dtype) if place is H else jax.ShapeDtypeStruct(shape, dtype)
            for shape, dtype, place in outs
        ],
        in_specs=[pl.BlockSpec(memory_space=place) for place in places],
        out_specs=[pl.BlockSpec(memory_space=place) for shape, dtype, place in outs],
        scratch_shapes=list(scratch),
        compiler_params=pltpu.CompilerParams(vmem_limit_bytes=32 * 1024 * 1024),
        name=name,
        cost_estimate=cost,
    )(*arrays)


def exchange(pieces, axes):
    return lax.all_to_all(pieces, axes, split_axis=0, concat_axis=0, tiled=True)


def crossed(array, axis, size, bit):
    return lax.ppermute(array, axis, [(i, i ^ bit) for i in range(size)])


EVEN = (0, 8, 4, 12, 2, 10, 6, 14)


def add_kernel(*refs, parts):
    in_refs, out_refs = refs[:-parts], refs[-parts:]
    rows = in_refs[0].shape[0] // parts
    for index, out_ref in enumerate(out_refs):
        cut = pl.ds(index * rows, rows)
        total = in_refs[0][cut, :].astype(f32)
        for ref in in_refs[1:]:
            total = total + ref[cut, :].astype(f32)
        out_ref[...] = total.astype(bf16)


def add(arrays, parts):
    rows = arrays[0].shape[0] // parts
    return call(
        functools.partial(add_kernel, parts=parts), "add", [V] * len(arrays), arrays,
        [((rows, CAP_ROWS), bf16, V)] * parts, cost=FREE,
    )


def body(
    attended, residual, grad_out, out_weight, layer_scale, frames, partner, moved_tiles, owner_slot
):
    scale_row = layer_scale[None, :]
    ints = pltpu.SMEM((N_DP,), jnp.int32)
    dma = pltpu.SemaphoreType.DMA

    projected, layer_own, window = call(
        project_kernel, "project", [H] * 8,
        (frames, partner, moved_tiles, attended, residual, grad_out, out_weight, scale_row),
        [((ROWS, CAP_ROWS), f32, H), ((ROWS, CAP_ROWS), bf16, H), ((PAD_ROWS, MOVE_ROWS), bf16, V)],
        [
            ints, ints, ints,
            V((A, CAP_ROWS), bf16), V((ROWS, CAP_ROWS), bf16), V((ROWS, BAL_ROWS), bf16),
            V((ROWS, A), bf16), V((1, ROWS), f32),
            V((ROWS, CAP_ROWS), f32), V((ROWS, CAP_ROWS), bf16),
            dma((6,)), dma((A // CHUNK,)), dma((A // CHUNK,)), dma((2,)),
        ],
    )
    pieces = exchange(window.reshape(N_DP, PAD_ROWS // N_DP, MOVE_ROWS), ("z", "x"))
    (pieces,) = call(
        forward_kernel, "forward", [S, V], (partner, pieces),
        [((N_DP, PAD_ROWS // N_DP, MOVE_ROWS), bf16, V)],
    )
    pieces = exchange(pieces, ("z", "x"))
    got = pieces.reshape(PAD_ROWS, MOVE_ROWS)

    scaled, pieces = call(
        weight_grad_kernel, "weight_grad", [S] * 4 + [V] * 4 + [H],
        (frames, partner, moved_tiles, owner_slot, attended, grad_out, scale_row, got, projected),
        [((ROWS, CAP_ROWS), bf16, H), ((N_DP, SHARE, WIDE), bf16, H)],
        [
            pltpu.SMEM((HEADS,), jnp.int32), V((HD, D), f32),
            V((ROWS, CAP_ROWS), f32), V((ROWS, CAP_ROWS), bf16),
            V((N_DP, SHARE, WIDE), bf16), dma((7,)),
        ],
    )
    summed = exchange(pieces, ("z", "x"))

    half = ((A // 2, CAP_ROWS), bf16, V)
    even, odd, layer_out = call(
        input_kernel, "input_grad", [S] * 3 + [V] * 2 + [H] * 2,
        (frames, partner, moved_tiles, out_weight, got, scaled, layer_own),
        [half, half, ((ROWS, BAL_ROWS), bf16, V)],
        [V((ROWS, CAP_ROWS), bf16), V((ROWS, CAP_ROWS), bf16), dma((2,))],
        FREE,
    )
    left, other = add((even, crossed(odd, "c", NC, 1)), 2)
    summed, _ = lax.optimization_barrier((summed, left))
    copies, scale_grad = call(
        slots_kernel, "slots", [V], (summed,),
        [((NZ * HEADS, SHARE, ROWS), bf16, H), ((1, ROWS), f32, V)],
        [V((HEADS, SHARE, ROWS), bf16), dma((NZ,))],
    )
    owned = exchange(copies, ("z", "y", "c"))
    left, *others = add((left, crossed(other, "y", NY, 1)), 4)
    owned, _ = lax.optimization_barrier((owned, left))
    others = [crossed(other, "y", NY, step) for other, step in zip(others, (4, 2, 6))]
    (copies,) = call(
        join_kernel, "join", [V], (owned,),
        [((BY_X, D), bf16, V)],
        [V((BY_X, D), f32)],
    )
    whole = lax.all_gather(copies, "x", axis=0, tiled=True)
    (ortho_update,) = call(
        ortho_kernel, "ortho", [V], (whole,), [((D, HD), bf16, H)],
        [V((D, HD), bf16), dma((PARTS,))],
    )
    left, others, ortho_update = lax.optimization_barrier((left, others, ortho_update))
    (input_grad,) = add((left, *others), 1)
    return (layer_out, input_grad, scale_grad.reshape(ROWS), ortho_update[:, None, :])


def solution(mesh):
    chips = Mesh(mesh.devices.reshape(NZ, NX, NY, NC), ("z", "x", "y", "c"))
    dp, fsdp = ("z", "x"), ("y", "c")
    placed = (
        P(None, dp),
        P(fsdp, dp),
        P(fsdp, dp),
        P(fsdp, None),
        P(fsdp),
        P(),
        P(),
        P(),
        P(),
    )
    return jax.shard_map(
        body,
        mesh=chips,
        in_specs=placed,
        out_specs=(P(fsdp, dp), P(fsdp, dp), P(fsdp), P(None, fsdp, None)),
        check_vma=False,
    )
```

```python
import functools
import math

import jax
import jax.numpy as jnp
from jax import lax
from jax.experimental import pallas as pl
from jax.experimental.pallas import tpu as pltpu
from jax.sharding import Mesh, PartitionSpec as P

D = 3200
HEADS = 16
HD = 128
FRAME = 256
TILE = 16
ITERS = 5
A = 2048
CAP_ROWS = 512
MOVE_ROWS = 256
BAL_ROWS = 384
N_DP = 32
N_FSDP = 16

NZ, NX, NY, NC = 8, 4, 8, 2
ROWS = D // N_FSDP
BY_X = HD // NX
SHARE = HD // N_DP
WIDE = D + HD
PAD_ROWS = 256
CHUNK = 512
PARTS = 5

coeff_linear = 3.4445
coeff_square = -4.775
coeff_cubic = 2.0315
EPSILON = 1e-07
INVERSE_ROOT = 1.0 / math.sqrt(N_DP * BAL_ROWS)

bf16 = jnp.bfloat16
f32 = jnp.float32

ROWS_BY_COLS = (((0,), (0,)), ((), ()))
COLS_BY_COLS = (((1,), (1,)), ((), ()))


def positions(shape, dimension):
    return lax.broadcasted_iota(jnp.int32, shape, dimension)


def dot(a, b, dims=(((1,), (0,)), ((), ()))):
    return lax.dot_general(a, b, dims, preferred_element_type=f32)


def same(size):
    return positions((size, size), 0) == positions((size, size), 1)


def to_column(row):
    size = row.shape[1]
    return jnp.sum(jnp.where(same(size), row, 0.0), axis=1, keepdims=True)


def to_row(column):
    size = column.shape[0]
    return jnp.sum(jnp.where(same(size), column, 0.0), axis=0, keepdims=True)


def my_counts(frames_ref, partner_ref, moved_ref):
    replica = lax.axis_index("z") * NX + lax.axis_index("x")
    mate = partner_ref[replica]
    kept = frames_ref[replica] * FRAME - moved_ref[replica] * TILE
    incoming = moved_ref[mate] * TILE
    holds_two = (frames_ref[replica] > frames_ref[mate]).astype(jnp.int32)
    return kept, incoming, holds_two


def light_places(kept, incoming):
    bal_col = positions((BAL_ROWS, MOVE_ROWS), 0)
    win_col = positions((BAL_ROWS, MOVE_ROWS), 1)
    hit = bal_col == win_col + (kept + incoming - MOVE_ROWS)
    hit = hit & (win_col >= MOVE_ROWS - incoming)
    return jnp.where(hit, 1.0, 0.0).astype(bf16)


def start(sems, *pairs):
    copies = [pltpu.make_async_copy(a, b, sems.at[i]) for i, (a, b) in enumerate(pairs)]
    for copy in copies:
        copy.start()
    return copies


def wait(copies):
    for copy in copies:
        copy.wait()


def project_kernel(
    frames_hbm, partner_hbm, moved_hbm,
    attended_hbm, residual_hbm, grad_hbm, weight_hbm, scale_hbm,
    window_ref,
    frames_ref, partner_ref, moved_ref,
    attended_ref, residual_ref, grad_ref, weight_ref, scale_ref,
    small_sems, attended_sems, weight_sems,
):
    late = pl.ds(CAP_ROWS - MOVE_ROWS, MOVE_ROWS)
    small = start(
        small_sems,
        (frames_hbm, frames_ref),
        (partner_hbm, partner_ref),
        (moved_hbm, moved_ref),
        (scale_hbm, scale_ref),
        (grad_hbm, grad_ref),
        (residual_hbm.at[:, late], residual_ref),
    )
    cuts = [pl.ds(first, CHUNK) for first in range(0, A, CHUNK)]
    attended = start(
        attended_sems, *[(attended_hbm.at[cut, late], attended_ref.at[cut, :]) for cut in cuts]
    )
    weight = start(
        weight_sems, *[(weight_hbm.at[:, cut], weight_ref.at[:, cut]) for cut in cuts]
    )
    wait(small[:5])
    kept, incoming, holds_two = my_counts(frames_ref, partner_ref, moved_ref)
    gains = to_column(scale_ref[...])
    grad_win = dot(grad_ref[...], light_places(kept, incoming))
    window_ref[pl.ds(ROWS, PAD_ROWS - ROWS), :] = jnp.zeros(
        (PAD_ROWS - ROWS, MOVE_ROWS), bf16
    )
    projected = None
    for index, cut in enumerate(cuts):
        attended[index].wait()
        weight[index].wait()
        part = dot(weight_ref[:, cut], attended_ref[cut, :])
        projected = part if projected is None else projected + part
    small[5].wait()
    layer = (residual_ref[...].astype(f32) + gains * projected).astype(bf16)
    layer_win = layer.astype(f32)
    window_ref[pl.ds(0, ROWS), :] = jnp.where(holds_two == 1, layer_win, grad_win).astype(bf16)


def forward_kernel(partner_ref, pieces_ref, out_ref):
    for replica in range(N_DP):
        out_ref[replica] = pieces_ref[partner_ref[replica]]


def send_lanes(first, last, value, pieces_ref, pieces_hbm, sems):
    lanes = pl.ds(first, last - first)
    for piece in range(N_DP):
        pieces_ref[piece, :, lanes] = value(piece, lanes)
    return start(sems, (pieces_ref.at[:, :, lanes], pieces_hbm.at[:, :, lanes]))


def weight_grad_kernel(
    frames_ref, partner_ref, moved_ref, slot_ref,
    attended_ref, grad_ref, weight_ref, scale_ref, got_ref,
    scaled_hbm, pieces_hbm,
    head_of, wide, scaled_ref, pieces_ref, sems,
):
    kept, incoming, holds_two = my_counts(frames_ref, partner_ref, moved_ref)
    for head in range(HEADS):
        head_of[slot_ref[head]] = head
    own = grad_ref[...].astype(f32)
    own = jnp.concatenate([own, jnp.zeros((ROWS, CAP_ROWS - BAL_ROWS), f32)], axis=1)
    got = got_ref[pl.ds(0, ROWS), :].astype(f32)
    got = jnp.where(holds_two == 1, got, 0.0)
    got = jnp.concatenate([jnp.zeros((ROWS, CAP_ROWS - MOVE_ROWS), f32), got], axis=1)
    grad = jnp.where(positions((ROWS, CAP_ROWS), 1) < kept, own, got)
    scaled = (grad * to_column(scale_ref[...])).astype(bf16)
    scaled_ref[...] = scaled
    (store,) = start(sems.at[pl.ds(1, 1)], (scaled_ref, scaled_hbm))
    stores, done = [store], 0
    for slot in range(HEADS):
        first = pl.multiple_of(head_of[slot] * HD, HD)
        wide[:, pl.ds(slot * ROWS, ROWS)] = dot(
            attended_ref[pl.ds(first, HD), :], scaled, COLS_BY_COLS
        )
        if (slot + 1) % 4 == 0:
            full = (slot + 1) * ROWS // HD * HD
            stores += send_lanes(done, full, lambda piece, lanes: wide[
                pl.ds((piece % NX * NZ + piece // NX) * SHARE, SHARE), lanes
            ].astype(bf16), pieces_ref, pieces_hbm, sems.at[pl.ds(2 + slot // 4, 1)])
            done = full
    projected = dot(weight_ref[...], attended_ref[...])
    part = jnp.sum(grad * projected, axis=1, keepdims=True) * INVERSE_ROOT
    part = to_row(part)
    high = part.astype(bf16).astype(f32)
    low = part - high
    zeros = jnp.zeros((1, 2 * HD - ROWS), f32)
    lines = [
        high[:, :HD],
        jnp.concatenate([high[:, HD:], zeros], axis=1),
        low[:, :HD],
        jnp.concatenate([low[:, HD:], zeros], axis=1),
    ]
    lines = jnp.concatenate(lines, axis=0).astype(bf16)
    stores += send_lanes(
        D, WIDE, lambda piece, lanes: lines, pieces_ref, pieces_hbm, sems.at[pl.ds(6, 1)]
    )
    wait(stores)


def input_kernel(
    frames_ref, partner_ref, moved_ref,
    weight_ref, scale_ref, got_ref, scaled_hbm, attended_hbm, residual_hbm,
    even_ref, odd_ref, layer_out_ref,
    scaled_ref, attended_ref, residual_ref, sems,
):
    balanced = pl.ds(0, BAL_ROWS)
    fetch = start(
        sems,
        (scaled_hbm, scaled_ref),
        (residual_hbm.at[:, balanced], residual_ref),
        (attended_hbm.at[:, balanced], attended_ref),
    )
    kept, incoming, holds_two = my_counts(frames_ref, partner_ref, moved_ref)
    block = lax.axis_index("y") * NC + lax.axis_index("c")
    fetch[0].wait()
    scaled = scaled_ref[...]
    for index, other in enumerate(EVEN):
        for ref, partner in ((even_ref, other), (odd_ref, other + 1)):
            first = pl.multiple_of((block ^ partner) * HD, HD)
            part = dot(weight_ref[:, pl.ds(first, HD)], scaled, ROWS_BY_COLS)
            ref[pl.ds(index * HD, HD), :] = part.astype(bf16)
    received = dot(got_ref[pl.ds(0, ROWS), :], light_places(kept, incoming), COLS_BY_COLS)
    wait(fetch[1:])
    own = to_column(scale_ref[...]) * dot(weight_ref[...], attended_ref[...])
    own = (residual_ref[...].astype(f32) + own).astype(bf16).astype(f32)
    keep = positions((ROWS, BAL_ROWS), 1) < kept
    layer_out_ref[...] = jnp.where(keep, own, received).astype(bf16)


def slots_kernel(pieces_ref, copies_hbm, scale_grad_ref, by_slot, sems):
    total = pieces_ref[0].astype(f32)
    for piece in range(1, N_DP):
        total = total + pieces_ref[piece].astype(f32)
    for slot in range(HEADS):
        by_slot[slot] = total[:, slot * ROWS : (slot + 1) * ROWS].astype(bf16)
    copies = [
        (by_slot, copies_hbm.at[pl.ds(z * HEADS, HEADS)]) for z in range(NZ)
    ]
    copies = start(sems, *copies)
    lines = total[0:2, D:] + total[2:4, D:]
    scale_grad_ref[...] = jnp.concatenate([lines[0:1, :], lines[1:2, : ROWS - HD]], axis=1)
    wait(copies)


def join_kernel(owned_ref, whole_ref, joined):
    for z in range(NZ):
        for block in range(N_FSDP):
            joined[pl.ds(z * SHARE, SHARE), pl.ds(block * ROWS, ROWS)] = owned_ref[
                z * N_FSDP + block
            ].astype(f32)
    whole_ref[...] = joined[...].astype(bf16)


def split(values):
    high = values.astype(bf16)
    return high, (values - high.astype(f32)).astype(bf16)


def mul(a, b):
    a_high, a_low = split(a)
    b_high, b_low = split(b)
    return dot(
        jnp.concatenate([a_high, a_high, a_low], axis=1),
        jnp.concatenate([b_high, b_low, b_high], axis=0),
    )


def ortho_kernel(
    grad_ref, left_ref, first_ref, second_ref, third_ref,
    out_hbm, input_grad_hbm,
    out_ref, input_grad_ref, sems,
):
    total = left_ref[...].astype(f32)
    for ref in (first_ref, second_ref, third_ref):
        total = total + ref[...].astype(f32)
    input_grad_ref[...] = total.astype(bf16)
    stores = start(sems.at[pl.ds(PARTS, 1)], (input_grad_ref, input_grad_hbm))
    grad = grad_ref[...]
    gram = dot(grad, grad, COLS_BY_COLS)
    eye = jnp.where(same(HD), 1.0, 0.0).astype(f32)
    squares = jnp.sum(jnp.sum(gram * eye, axis=1, keepdims=True), axis=0, keepdims=True)
    norm = jnp.sqrt(squares) + EPSILON
    gram = gram / norm / norm
    total = None
    for sweep in range(ITERS):
        step = coeff_linear * eye + coeff_square * gram + coeff_cubic * mul(gram, gram)
        total = step if total is None else mul(total, step)
        if sweep < ITERS - 1:
            gram = mul(mul(step, gram), step)
    total = jnp.concatenate(split(total * (0.2 * math.sqrt(D) / norm)), axis=1)
    for index, first in enumerate(range(0, D, D // PARTS)):
        cut = pl.ds(first, D // PARTS)
        out = dot(grad_ref[:, cut], total, ROWS_BY_COLS)
        out_ref[cut, :] = (out[:, :HD] + out[:, HD:]).astype(bf16)
        stores += start(sems.at[pl.ds(index, 1)], (out_ref.at[cut, :], out_hbm.at[cut, :]))
    wait(stores)


S, V, H = pltpu.SMEM, pltpu.VMEM, pltpu.HBM
FREE = pl.CostEstimate(flops=0, bytes_accessed=0, transcendentals=0)


def call(kernel, name, places, arrays, outs, scratch=(), cost=None):
    arrays = [
        pltpu.with_memory_space_constraint(array, H) if place is H else array
        for array, place in zip(arrays, places)
    ]
    return pl.pallas_call(
        kernel,
        out_shape=[
            H(shape, dtype) if place is H else jax.ShapeDtypeStruct(shape, dtype)
            for shape, dtype, place in outs
        ],
        in_specs=[pl.BlockSpec(memory_space=place) for place in places],
        out_specs=[pl.BlockSpec(memory_space=place) for shape, dtype, place in outs],
        scratch_shapes=list(scratch),
        compiler_params=pltpu.CompilerParams(vmem_limit_bytes=32 * 1024 * 1024),
        name=name,
        cost_estimate=cost,
    )(*arrays)


def exchange(pieces, axes):
    return lax.all_to_all(pieces, axes, split_axis=0, concat_axis=0, tiled=True)


def crossed(array, axis, size, bit):
    return lax.ppermute(array, axis, [(i, i ^ bit) for i in range(size)])


EVEN = (0, 8, 4, 12, 2, 10, 6, 14)


def add_kernel(*refs, parts):
    in_refs, out_refs = refs[:-parts], refs[-parts:]
    rows = in_refs[0].shape[0] // parts
    for index, out_ref in enumerate(out_refs):
        cut = pl.ds(index * rows, rows)
        total = in_refs[0][cut, :].astype(f32)
        for ref in in_refs[1:]:
            total = total + ref[cut, :].astype(f32)
        out_ref[...] = total.astype(bf16)


def add(arrays, parts):
    rows = arrays[0].shape[0] // parts
    return call(
        functools.partial(add_kernel, parts=parts), "add", [V] * len(arrays), arrays,
        [((rows, CAP_ROWS), bf16, V)] * parts, cost=FREE,
    )


def body(
    attended, residual, grad_out, out_weight, layer_scale, frames, partner, moved_tiles, owner_slot
):
    scale_row = layer_scale[None, :]
    ints = pltpu.SMEM((N_DP,), jnp.int32)
    dma = pltpu.SemaphoreType.DMA

    (window,) = call(
        project_kernel, "project", [H] * 8,
        (frames, partner, moved_tiles, attended, residual, grad_out, out_weight, scale_row),
        [((PAD_ROWS, MOVE_ROWS), bf16, V)],
        [
            ints, ints, ints,
            V((A, MOVE_ROWS), bf16), V((ROWS, MOVE_ROWS), bf16), V((ROWS, BAL_ROWS), bf16),
            V((ROWS, A), bf16), V((1, ROWS), f32),
            dma((6,)), dma((A // CHUNK,)), dma((A // CHUNK,)),
        ],
    )
    pieces = exchange(window.reshape(N_DP, PAD_ROWS // N_DP, MOVE_ROWS), ("z", "x"))
    (pieces,) = call(
        forward_kernel, "forward", [S, V], (partner, pieces),
        [((N_DP, PAD_ROWS // N_DP, MOVE_ROWS), bf16, V)],
    )
    pieces = exchange(pieces, ("z", "x"))
    got = pieces.reshape(PAD_ROWS, MOVE_ROWS)

    scaled, pieces = call(
        weight_grad_kernel, "weight_grad", [S] * 4 + [V] * 5,
        (
            frames, partner, moved_tiles, owner_slot,
            attended, grad_out, out_weight, scale_row, got,
        ),
        [((ROWS, CAP_ROWS), bf16, H), ((N_DP, SHARE, WIDE), bf16, H)],
        [
            pltpu.SMEM((HEADS,), jnp.int32), V((HD, D), f32),
            V((ROWS, CAP_ROWS), bf16), V((N_DP, SHARE, WIDE), bf16), dma((7,)),
        ],
    )
    summed = exchange(pieces, ("z", "x"))

    half = ((A // 2, CAP_ROWS), bf16, V)
    even, odd, layer_out = call(
        input_kernel, "input_grad", [S] * 3 + [V] * 3 + [H] * 3,
        (
            frames, partner, moved_tiles,
            out_weight, scale_row, got, scaled, attended, residual,
        ),
        [half, half, ((ROWS, BAL_ROWS), bf16, V)],
        [
            V((ROWS, CAP_ROWS), bf16), V((A, BAL_ROWS), bf16), V((ROWS, BAL_ROWS), bf16),
            dma((3,)),
        ],
        FREE,
    )
    left, other = add((even, crossed(odd, "c", NC, 1)), 2)
    summed, _ = lax.optimization_barrier((summed, left))
    copies, scale_grad = call(
        slots_kernel, "slots", [V], (summed,),
        [((NZ * HEADS, SHARE, ROWS), bf16, H), ((1, ROWS), f32, V)],
        [V((HEADS, SHARE, ROWS), bf16), dma((NZ,))],
    )
    owned = exchange(copies, ("z", "y", "c"))
    left, *others = add((left, crossed(other, "y", NY, 1)), 4)
    owned, _ = lax.optimization_barrier((owned, left))
    others = [crossed(other, "y", NY, step) for other, step in zip(others, (4, 2, 6))]
    (copies,) = call(
        join_kernel, "join", [V], (owned,),
        [((BY_X, D), bf16, V)],
        [V((BY_X, D), f32)],
    )
    whole = lax.all_gather(copies, "x", axis=0, tiled=True)
    ortho_update, input_grad = call(
        ortho_kernel, "ortho", [V] * 5, (whole, left, *others),
        [((D, HD), bf16, H), ((HD, CAP_ROWS), bf16, H)],
        [V((D, HD), bf16), V((HD, CAP_ROWS), bf16), dma((PARTS + 1,))],
    )
    return (layer_out, input_grad, scale_grad.reshape(ROWS), ortho_update[:, None, :])


def solution(mesh):
    chips = Mesh(mesh.devices.reshape(NZ, NX, NY, NC), ("z", "x", "y", "c"))
    dp, fsdp = ("z", "x"), ("y", "c")
    placed = (
        P(None, dp),
        P(fsdp, dp),
        P(fsdp, dp),
        P(fsdp, None),
        P(fsdp),
        P(),
        P(),
        P(),
        P(),
    )
    return jax.shard_map(
        body,
        mesh=chips,
        in_specs=placed,
        out_specs=(P(fsdp, dp), P(fsdp, dp), P(fsdp), P(None, fsdp, None)),
        check_vma=False,
    )
```

```python
import functools
import math

import jax
import jax.numpy as jnp
from jax import lax
from jax.experimental import pallas as pl
from jax.experimental.pallas import tpu as pltpu
from jax.sharding import Mesh, PartitionSpec as P

D = 3200
HEADS = 16
HD = 128
FRAME = 256
TILE = 16
ITERS = 5
A = 2048
CAP_ROWS = 512
MOVE_ROWS = 256
BAL_ROWS = 384
N_DP = 32
N_FSDP = 16

NZ, NX, NY, NC = 8, 4, 8, 2
ROWS = D // N_FSDP
BY_X = HD // NX
SHARE = HD // N_DP
WIDE = D + HD
PAD_ROWS = 256
CHUNK = 1024
PARTS = 5

coeff_linear = 3.4445
coeff_square = -4.775
coeff_cubic = 2.0315
EPSILON = 1e-07
INVERSE_ROOT = 1.0 / math.sqrt(N_DP * BAL_ROWS)

bf16 = jnp.bfloat16
f32 = jnp.float32

ROWS_BY_COLS = (((0,), (0,)), ((), ()))
COLS_BY_COLS = (((1,), (1,)), ((), ()))


def positions(shape, dimension):
    return lax.broadcasted_iota(jnp.int32, shape, dimension)


def dot(a, b, dims=(((1,), (0,)), ((), ()))):
    return lax.dot_general(a, b, dims, preferred_element_type=f32)


def same(size):
    return positions((size, size), 0) == positions((size, size), 1)


def to_column(row):
    size = row.shape[1]
    return jnp.sum(jnp.where(same(size), row, 0.0), axis=1, keepdims=True)


def to_row(column):
    size = column.shape[0]
    return jnp.sum(jnp.where(same(size), column, 0.0), axis=0, keepdims=True)


def my_counts(frames_ref, partner_ref, moved_ref):
    replica = lax.axis_index("z") * NX + lax.axis_index("x")
    mate = partner_ref[replica]
    kept = frames_ref[replica] * FRAME - moved_ref[replica] * TILE
    incoming = moved_ref[mate] * TILE
    holds_two = (frames_ref[replica] > frames_ref[mate]).astype(jnp.int32)
    return kept, incoming, holds_two


def light_places(kept, incoming):
    bal_col = positions((BAL_ROWS, MOVE_ROWS), 0)
    win_col = positions((BAL_ROWS, MOVE_ROWS), 1)
    hit = bal_col == win_col + (kept + incoming - MOVE_ROWS)
    hit = hit & (win_col >= MOVE_ROWS - incoming)
    return jnp.where(hit, 1.0, 0.0).astype(bf16)


def start(sems, *pairs):
    copies = [pltpu.make_async_copy(a, b, sems.at[i]) for i, (a, b) in enumerate(pairs)]
    for copy in copies:
        copy.start()
    return copies


def wait(copies):
    for copy in copies:
        copy.wait()


def project_kernel(
    frames_hbm, partner_hbm, moved_hbm,
    attended_hbm, residual_hbm, grad_hbm, weight_hbm, scale_hbm,
    window_ref,
    frames_ref, partner_ref, moved_ref,
    attended_ref, residual_ref, grad_ref, weight_ref, scale_ref,
    small_sems, attended_sems, weight_sems,
):
    late = pl.ds(CAP_ROWS - MOVE_ROWS, MOVE_ROWS)
    small = start(
        small_sems,
        (frames_hbm, frames_ref),
        (partner_hbm, partner_ref),
        (moved_hbm, moved_ref),
        (scale_hbm, scale_ref),
        (grad_hbm, grad_ref),
        (residual_hbm.at[:, late], residual_ref),
    )
    cuts = [pl.ds(first, CHUNK) for first in range(0, A, CHUNK)]
    attended = start(
        attended_sems, *[(attended_hbm.at[cut, late], attended_ref.at[cut, :]) for cut in cuts]
    )
    weight = start(
        weight_sems, *[(weight_hbm.at[:, cut], weight_ref.at[:, cut]) for cut in cuts]
    )
    wait(small[:5])
    kept, incoming, holds_two = my_counts(frames_ref, partner_ref, moved_ref)
    gains = to_column(scale_ref[...])
    grad_win = dot(grad_ref[...], light_places(kept, incoming))
    window_ref[pl.ds(ROWS, PAD_ROWS - ROWS), :] = jnp.zeros(
        (PAD_ROWS - ROWS, MOVE_ROWS), bf16
    )
    projected = None
    for index, cut in enumerate(cuts):
        attended[index].wait()
        weight[index].wait()
        part = dot(weight_ref[:, cut], attended_ref[cut, :])
        projected = part if projected is None else projected + part
    small[5].wait()
    layer = (residual_ref[...].astype(f32) + gains * projected).astype(bf16)
    layer_win = layer.astype(f32)
    window_ref[pl.ds(0, ROWS), :] = jnp.where(holds_two == 1, layer_win, grad_win).astype(bf16)


def forward_kernel(partner_ref, pieces_ref, out_ref):
    for replica in range(N_DP):
        out_ref[replica] = pieces_ref[partner_ref[replica]]


def send_lanes(first, last, value, pieces_ref, pieces_hbm, sems):
    lanes = pl.ds(first, last - first)
    for piece in range(N_DP):
        pieces_ref[piece, :, lanes] = value(piece, lanes)
    return start(sems, (pieces_ref.at[:, :, lanes], pieces_hbm.at[:, :, lanes]))


def weight_grad_kernel(
    frames_ref, partner_ref, moved_ref, slot_ref,
    attended_ref, grad_ref, weight_ref, scale_ref, got_ref,
    scaled_hbm, pieces_hbm,
    head_of, wide, scaled_ref, pieces_ref, sems,
):
    kept, incoming, holds_two = my_counts(frames_ref, partner_ref, moved_ref)
    for head in range(HEADS):
        head_of[slot_ref[head]] = head
    own = grad_ref[...].astype(f32)
    own = jnp.concatenate([own, jnp.zeros((ROWS, CAP_ROWS - BAL_ROWS), f32)], axis=1)
    got = got_ref[pl.ds(0, ROWS), :].astype(f32)
    got = jnp.where(holds_two == 1, got, 0.0)
    got = jnp.concatenate([jnp.zeros((ROWS, CAP_ROWS - MOVE_ROWS), f32), got], axis=1)
    grad = jnp.where(positions((ROWS, CAP_ROWS), 1) < kept, own, got)
    scaled = (grad * to_column(scale_ref[...])).astype(bf16)
    scaled_ref[...] = scaled
    (store,) = start(sems.at[pl.ds(1, 1)], (scaled_ref, scaled_hbm))
    projected = dot(weight_ref[...], attended_ref[...])
    part = jnp.sum(grad * projected, axis=1, keepdims=True) * INVERSE_ROOT
    part = to_row(part)
    high = part.astype(bf16).astype(f32)
    low = part - high
    zeros = jnp.zeros((1, 2 * HD - ROWS), f32)
    lines = [
        high[:, :HD],
        jnp.concatenate([high[:, HD:], zeros], axis=1),
        low[:, :HD],
        jnp.concatenate([low[:, HD:], zeros], axis=1),
    ]
    lines = jnp.concatenate(lines, axis=0).astype(bf16)
    stores = [store]
    stores += send_lanes(
        D, WIDE, lambda piece, lanes: lines, pieces_ref, pieces_hbm, sems.at[pl.ds(6, 1)]
    )
    done = 0
    for slot in range(HEADS):
        first = pl.multiple_of(head_of[slot] * HD, HD)
        wide[:, pl.ds(slot * ROWS, ROWS)] = dot(
            attended_ref[pl.ds(first, HD), :], scaled, COLS_BY_COLS
        )
        if (slot + 1) % 4 == 0:
            full = (slot + 1) * ROWS // HD * HD
            stores += send_lanes(done, full, lambda piece, lanes: wide[
                pl.ds((piece % NX * NZ + piece // NX) * SHARE, SHARE), lanes
            ].astype(bf16), pieces_ref, pieces_hbm, sems.at[pl.ds(2 + slot // 4, 1)])
            done = full
    wait(stores)


def input_kernel(
    frames_ref, partner_ref, moved_ref,
    weight_ref, scale_ref, got_ref, scaled_hbm, attended_hbm, residual_hbm,
    even_ref, odd_ref, layer_out_ref,
    scaled_ref, attended_ref, residual_ref, sems,
):
    balanced = pl.ds(0, BAL_ROWS)
    fetch = start(
        sems,
        (scaled_hbm, scaled_ref),
        (residual_hbm.at[:, balanced], residual_ref),
        (attended_hbm.at[:, balanced], attended_ref),
    )
    kept, incoming, holds_two = my_counts(frames_ref, partner_ref, moved_ref)
    block = lax.axis_index("y") * NC + lax.axis_index("c")
    fetch[0].wait()
    scaled = scaled_ref[...]
    for index, other in enumerate(EVEN):
        for ref, partner in ((even_ref, other), (odd_ref, other + 1)):
            first = pl.multiple_of((block ^ partner) * HD, HD)
            part = dot(weight_ref[:, pl.ds(first, HD)], scaled, ROWS_BY_COLS)
            ref[pl.ds(index * HD, HD), :] = part.astype(bf16)
    received = dot(got_ref[pl.ds(0, ROWS), :], light_places(kept, incoming), COLS_BY_COLS)
    wait(fetch[1:])
    own = to_column(scale_ref[...]) * dot(weight_ref[...], attended_ref[...])
    own = (residual_ref[...].astype(f32) + own).astype(bf16).astype(f32)
    keep = positions((ROWS, BAL_ROWS), 1) < kept
    layer_out_ref[...] = jnp.where(keep, own, received).astype(bf16)


def slots_kernel(pieces_ref, copies_hbm, scale_grad_ref, by_slot, sems):
    total = pieces_ref[0].astype(f32)
    for piece in range(1, N_DP):
        total = total + pieces_ref[piece].astype(f32)
    for slot in range(HEADS):
        by_slot[slot] = total[:, slot * ROWS : (slot + 1) * ROWS].astype(bf16)
    copies = [
        (by_slot, copies_hbm.at[pl.ds(z * HEADS, HEADS)]) for z in range(NZ)
    ]
    copies = start(sems, *copies)
    lines = total[0:2, D:] + total[2:4, D:]
    scale_grad_ref[...] = jnp.concatenate([lines[0:1, :], lines[1:2, : ROWS - HD]], axis=1)
    wait(copies)


def join_kernel(owned_ref, whole_ref, joined):
    for z in range(NZ):
        for block in range(N_FSDP):
            joined[pl.ds(z * SHARE, SHARE), pl.ds(block * ROWS, ROWS)] = owned_ref[
                z * N_FSDP + block
            ].astype(f32)
    whole_ref[...] = joined[...].astype(bf16)


def split(values):
    high = values.astype(bf16)
    return high, (values - high.astype(f32)).astype(bf16)


def mul(a, b):
    a_high, a_low = split(a)
    b_high, b_low = split(b)
    return dot(
        jnp.concatenate([a_high, a_high, a_low], axis=1),
        jnp.concatenate([b_high, b_low, b_high], axis=0),
    )


def ortho_kernel(
    grad_ref, left_ref, first_ref, second_ref, third_ref,
    out_hbm, input_grad_hbm,
    out_ref, input_grad_ref, sems,
):
    total = left_ref[...].astype(f32)
    for ref in (first_ref, second_ref, third_ref):
        total = total + ref[...].astype(f32)
    input_grad_ref[...] = total.astype(bf16)
    stores = start(sems.at[pl.ds(PARTS, 1)], (input_grad_ref, input_grad_hbm))
    grad = grad_ref[...]
    gram = dot(grad, grad, COLS_BY_COLS)
    eye = jnp.where(same(HD), 1.0, 0.0).astype(f32)
    squares = jnp.sum(jnp.sum(gram * eye, axis=1, keepdims=True), axis=0, keepdims=True)
    norm = jnp.sqrt(squares) + EPSILON
    gram = gram / norm / norm
    total = None
    for sweep in range(ITERS):
        step = coeff_linear * eye + coeff_square * gram + coeff_cubic * mul(gram, gram)
        total = step if total is None else mul(total, step)
        if sweep < ITERS - 1:
            gram = mul(mul(step, gram), step)
    total = jnp.concatenate(split(total * (0.2 * math.sqrt(D) / norm)), axis=1)
    for index, first in enumerate(range(0, D, D // PARTS)):
        cut = pl.ds(first, D // PARTS)
        out = dot(grad_ref[:, cut], total, ROWS_BY_COLS)
        out_ref[cut, :] = (out[:, :HD] + out[:, HD:]).astype(bf16)
        stores += start(sems.at[pl.ds(index, 1)], (out_ref.at[cut, :], out_hbm.at[cut, :]))
    wait(stores)


S, V, H = pltpu.SMEM, pltpu.VMEM, pltpu.HBM
FREE = pl.CostEstimate(flops=0, bytes_accessed=0, transcendentals=0)


def call(kernel, name, places, arrays, outs, scratch=(), cost=None):
    arrays = [
        pltpu.with_memory_space_constraint(array, H) if place is H else array
        for array, place in zip(arrays, places)
    ]
    return pl.pallas_call(
        kernel,
        out_shape=[
            H(shape, dtype) if place is H else jax.ShapeDtypeStruct(shape, dtype)
            for shape, dtype, place in outs
        ],
        in_specs=[pl.BlockSpec(memory_space=place) for place in places],
        out_specs=[pl.BlockSpec(memory_space=place) for shape, dtype, place in outs],
        scratch_shapes=list(scratch),
        compiler_params=pltpu.CompilerParams(vmem_limit_bytes=32 * 1024 * 1024),
        name=name,
        cost_estimate=cost,
    )(*arrays)


def exchange(pieces, axes):
    return lax.all_to_all(pieces, axes, split_axis=0, concat_axis=0, tiled=True)


def crossed(array, axis, size, bit):
    return lax.ppermute(array, axis, [(i, i ^ bit) for i in range(size)])


EVEN = (0, 8, 4, 12, 2, 10, 6, 14)


def add_kernel(*refs, parts):
    in_refs, out_refs = refs[:-parts], refs[-parts:]
    rows = in_refs[0].shape[0] // parts
    for index, out_ref in enumerate(out_refs):
        cut = pl.ds(index * rows, rows)
        total = in_refs[0][cut, :].astype(f32)
        for ref in in_refs[1:]:
            total = total + ref[cut, :].astype(f32)
        out_ref[...] = total.astype(bf16)


def add(arrays, parts):
    rows = arrays[0].shape[0] // parts
    return call(
        functools.partial(add_kernel, parts=parts), "add", [V] * len(arrays), arrays,
        [((rows, CAP_ROWS), bf16, V)] * parts, cost=FREE,
    )


def body(
    attended, residual, grad_out, out_weight, layer_scale, frames, partner, moved_tiles, owner_slot
):
    scale_row = layer_scale[None, :]
    ints = pltpu.SMEM((N_DP,), jnp.int32)
    dma = pltpu.SemaphoreType.DMA

    (window,) = call(
        project_kernel, "project", [H] * 8,
        (frames, partner, moved_tiles, attended, residual, grad_out, out_weight, scale_row),
        [((PAD_ROWS, MOVE_ROWS), bf16, V)],
        [
            ints, ints, ints,
            V((A, MOVE_ROWS), bf16), V((ROWS, MOVE_ROWS), bf16), V((ROWS, BAL_ROWS), bf16),
            V((ROWS, A), bf16), V((1, ROWS), f32),
            dma((6,)), dma((A // CHUNK,)), dma((A // CHUNK,)),
        ],
    )
    pieces = exchange(window.reshape(N_DP, PAD_ROWS // N_DP, MOVE_ROWS), ("z", "x"))
    (pieces,) = call(
        forward_kernel, "forward", [S, V], (partner, pieces),
        [((N_DP, PAD_ROWS // N_DP, MOVE_ROWS), bf16, V)],
    )
    pieces = exchange(pieces, ("z", "x"))
    got = pieces.reshape(PAD_ROWS, MOVE_ROWS)

    scaled, pieces = call(
        weight_grad_kernel, "weight_grad", [S] * 4 + [V] * 5,
        (
            frames, partner, moved_tiles, owner_slot,
            attended, grad_out, out_weight, scale_row, got,
        ),
        [((ROWS, CAP_ROWS), bf16, H), ((N_DP, SHARE, WIDE), bf16, H)],
        [
            pltpu.SMEM((HEADS,), jnp.int32), V((HD, D), f32),
            V((ROWS, CAP_ROWS), bf16), V((N_DP, SHARE, WIDE), bf16), dma((7,)),
        ],
    )
    summed = exchange(pieces, ("z", "x"))

    half = ((A // 2, CAP_ROWS), bf16, V)
    even, odd, layer_out = call(
        input_kernel, "input_grad", [S] * 3 + [V] * 3 + [H] * 3,
        (
            frames, partner, moved_tiles,
            out_weight, scale_row, got, scaled, attended, residual,
        ),
        [half, half, ((ROWS, BAL_ROWS), bf16, V)],
        [
            V((ROWS, CAP_ROWS), bf16), V((A, BAL_ROWS), bf16), V((ROWS, BAL_ROWS), bf16),
            dma((3,)),
        ],
        FREE,
    )
    left, other = add((even, crossed(odd, "c", NC, 1)), 2)
    summed, _ = lax.optimization_barrier((summed, left))
    copies, scale_grad = call(
        slots_kernel, "slots", [V], (summed,),
        [((NZ * HEADS, SHARE, ROWS), bf16, H), ((1, ROWS), f32, V)],
        [V((HEADS, SHARE, ROWS), bf16), dma((NZ,))],
    )
    owned = exchange(copies, ("z", "y", "c"))
    left, *others = add((left, crossed(other, "y", NY, 1)), 4)
    owned, _ = lax.optimization_barrier((owned, left))
    others = [crossed(other, "y", NY, step) for other, step in zip(others[1:] + others[:1], (2, 6, 4))]
    (copies,) = call(
        join_kernel, "join", [V], (owned,),
        [((BY_X, D), bf16, V)],
        [V((BY_X, D), f32)],
    )
    whole = lax.all_gather(copies, "x", axis=0, tiled=True)
    ortho_update, input_grad = call(
        ortho_kernel, "ortho", [V] * 5, (whole, left, *others),
        [((D, HD), bf16, H), ((HD, CAP_ROWS), bf16, H)],
        [V((D, HD), bf16), V((HD, CAP_ROWS), bf16), dma((PARTS + 1,))],
    )
    return (layer_out, input_grad, scale_grad.reshape(ROWS), ortho_update[:, None, :])


def solution(mesh):
    chips = Mesh(mesh.devices.reshape(NZ, NX, NY, NC), ("z", "x", "y", "c"))
    dp, fsdp = ("z", "x"), ("y", "c")
    placed = (
        P(None, dp),
        P(fsdp, dp),
        P(fsdp, dp),
        P(fsdp, None),
        P(fsdp),
        P(),
        P(),
        P(),
        P(),
    )
    return jax.shard_map(
        body,
        mesh=chips,
        in_specs=placed,
        out_specs=(P(fsdp, dp), P(fsdp, dp), P(fsdp), P(None, fsdp, None)),
        check_vma=False,
    )
```

```python
import functools
import math

import jax
import jax.numpy as jnp
from jax import lax
from jax.experimental import pallas as pl
from jax.experimental.pallas import tpu as pltpu
from jax.sharding import Mesh, PartitionSpec as P

D = 3200
HEADS = 16
HD = 128
FRAME = 256
TILE = 16
ITERS = 5
A = 2048
CAP_ROWS = 512
MOVE_ROWS = 256
BAL_ROWS = 384
N_DP = 32
N_FSDP = 16

NZ, NX, NY, NC = 8, 4, 8, 2
ROWS = D // N_FSDP
BY_X = HD // NX
SHARE = HD // N_DP
WIDE = D + HD
PAD_ROWS = 256
CHUNK = 1024
PARTS = 5

coeff_linear = 3.4445
coeff_square = -4.775
coeff_cubic = 2.0315
EPSILON = 1e-07
INVERSE_ROOT = 1.0 / math.sqrt(N_DP * BAL_ROWS)

bf16 = jnp.bfloat16
f32 = jnp.float32

ROWS_BY_COLS = (((0,), (0,)), ((), ()))
COLS_BY_COLS = (((1,), (1,)), ((), ()))


def positions(shape, dimension):
    return lax.broadcasted_iota(jnp.int32, shape, dimension)


def dot(a, b, dims=(((1,), (0,)), ((), ()))):
    return lax.dot_general(a, b, dims, preferred_element_type=f32)


def same(size):
    return positions((size, size), 0) == positions((size, size), 1)


def to_column(row):
    size = row.shape[1]
    return jnp.sum(jnp.where(same(size), row, 0.0), axis=1, keepdims=True)


def to_row(column):
    size = column.shape[0]
    return jnp.sum(jnp.where(same(size), column, 0.0), axis=0, keepdims=True)


def my_counts(frames_ref, partner_ref, moved_ref):
    replica = lax.axis_index("z") * NX + lax.axis_index("x")
    mate = partner_ref[replica]
    kept = frames_ref[replica] * FRAME - moved_ref[replica] * TILE
    incoming = moved_ref[mate] * TILE
    holds_two = (frames_ref[replica] > frames_ref[mate]).astype(jnp.int32)
    return kept, incoming, holds_two


def light_places(kept, incoming):
    bal_col = positions((BAL_ROWS, MOVE_ROWS), 0)
    win_col = positions((BAL_ROWS, MOVE_ROWS), 1)
    hit = bal_col == win_col + (kept + incoming - MOVE_ROWS)
    hit = hit & (win_col >= MOVE_ROWS - incoming)
    return jnp.where(hit, 1.0, 0.0).astype(bf16)


def start(sems, *pairs):
    copies = [pltpu.make_async_copy(a, b, sems.at[i]) for i, (a, b) in enumerate(pairs)]
    for copy in copies:
        copy.start()
    return copies


def wait(copies):
    for copy in copies:
        copy.wait()


def project_kernel(
    frames_hbm, partner_hbm, moved_hbm,
    attended_hbm, residual_hbm, grad_hbm, weight_hbm, scale_hbm,
    window_ref,
    frames_ref, partner_ref, moved_ref,
    attended_ref, residual_ref, grad_ref, weight_ref, scale_ref,
    small_sems, attended_sems, weight_sems,
):
    late = pl.ds(CAP_ROWS - MOVE_ROWS, MOVE_ROWS)
    small = start(
        small_sems,
        (frames_hbm, frames_ref),
        (partner_hbm, partner_ref),
        (moved_hbm, moved_ref),
        (scale_hbm, scale_ref),
        (grad_hbm, grad_ref),
        (residual_hbm.at[:, late], residual_ref),
    )
    cuts = [pl.ds(first, CHUNK) for first in range(0, A, CHUNK)]
    attended = start(
        attended_sems, *[(attended_hbm.at[cut, late], attended_ref.at[cut, :]) for cut in cuts]
    )
    weight = start(
        weight_sems, *[(weight_hbm.at[:, cut], weight_ref.at[:, cut]) for cut in cuts]
    )
    wait(small[:5])
    kept, incoming, holds_two = my_counts(frames_ref, partner_ref, moved_ref)
    gains = to_column(scale_ref[...])
    grad_win = dot(grad_ref[...], light_places(kept, incoming))
    window_ref[pl.ds(ROWS, PAD_ROWS - ROWS), :] = jnp.zeros(
        (PAD_ROWS - ROWS, MOVE_ROWS), bf16
    )
    projected = None
    for index, cut in enumerate(cuts):
        attended[index].wait()
        weight[index].wait()
        part = dot(weight_ref[:, cut], attended_ref[cut, :])
        projected = part if projected is None else projected + part
    small[5].wait()
    layer = (residual_ref[...].astype(f32) + gains * projected).astype(bf16)
    layer_win = layer.astype(f32)
    window_ref[pl.ds(0, ROWS), :] = jnp.where(holds_two == 1, layer_win, grad_win).astype(bf16)


def forward_kernel(partner_ref, pieces_ref, out_ref):
    for replica in range(N_DP):
        out_ref[replica] = pieces_ref[partner_ref[replica]]


def send_lanes(first, last, value, pieces_ref, pieces_hbm, sems):
    lanes = pl.ds(first, last - first)
    for piece in range(N_DP):
        pieces_ref[piece, :, lanes] = value(piece, lanes)
    return start(sems, (pieces_ref.at[:, :, lanes], pieces_hbm.at[:, :, lanes]))


def weight_grad_kernel(
    frames_ref, partner_ref, moved_ref, slot_ref,
    attended_ref, grad_ref, weight_ref, scale_ref, got_ref,
    scaled_hbm, pieces_hbm,
    head_of, wide, scaled_ref, pieces_ref, sems,
):
    kept, incoming, holds_two = my_counts(frames_ref, partner_ref, moved_ref)
    for head in range(HEADS):
        head_of[slot_ref[head]] = head
    own = grad_ref[...].astype(f32)
    own = jnp.concatenate([own, jnp.zeros((ROWS, CAP_ROWS - BAL_ROWS), f32)], axis=1)
    got = got_ref[pl.ds(0, ROWS), :].astype(f32)
    got = jnp.where(holds_two == 1, got, 0.0)
    got = jnp.concatenate([jnp.zeros((ROWS, CAP_ROWS - MOVE_ROWS), f32), got], axis=1)
    grad = jnp.where(positions((ROWS, CAP_ROWS), 1) < kept, own, got)
    scaled = (grad * to_column(scale_ref[...])).astype(bf16)
    scaled_ref[...] = scaled
    (store,) = start(sems.at[pl.ds(1, 1)], (scaled_ref, scaled_hbm))
    projected = dot(weight_ref[...], attended_ref[...])
    part = jnp.sum(grad * projected, axis=1, keepdims=True) * INVERSE_ROOT
    part = to_row(part)
    high = part.astype(bf16).astype(f32)
    low = part - high
    zeros = jnp.zeros((1, 2 * HD - ROWS), f32)
    lines = [
        high[:, :HD],
        jnp.concatenate([high[:, HD:], zeros], axis=1),
        low[:, :HD],
        jnp.concatenate([low[:, HD:], zeros], axis=1),
    ]
    lines = jnp.concatenate(lines, axis=0).astype(bf16)
    stores = [store]
    stores += send_lanes(
        D, WIDE, lambda piece, lanes: lines, pieces_ref, pieces_hbm, sems.at[pl.ds(6, 1)]
    )
    done = 0
    for slot in range(HEADS):
        first = pl.multiple_of(head_of[slot] * HD, HD)
        wide[:, pl.ds(slot * ROWS, ROWS)] = dot(
            attended_ref[pl.ds(first, HD), :], scaled, COLS_BY_COLS
        )
        if (slot + 1) % 4 == 0:
            full = (slot + 1) * ROWS // HD * HD
            stores += send_lanes(done, full, lambda piece, lanes: wide[
                pl.ds((piece % NX * NZ + piece // NX) * SHARE, SHARE), lanes
            ].astype(bf16), pieces_ref, pieces_hbm, sems.at[pl.ds(2 + slot // 4, 1)])
            done = full
    wait(stores)


def blocks_of(weight_ref, scaled, odd, out_ref):
    block = lax.axis_index("y") * NC + lax.axis_index("c")
    for index, other in enumerate(EVEN):
        first = pl.multiple_of((block ^ (other + odd)) * HD, HD)
        part = dot(weight_ref[:, pl.ds(first, HD)], scaled, ROWS_BY_COLS)
        out_ref[pl.ds(index * HD, HD), :] = part.astype(bf16)


def odd_kernel(weight_ref, scaled_hbm, odd_ref, scaled_ref, sems):
    wait(start(sems, (scaled_hbm, scaled_ref)))
    blocks_of(weight_ref, scaled_ref[...], 1, odd_ref)


def even_kernel(
    frames_ref, partner_ref, moved_ref,
    weight_ref, scale_ref, got_ref, scaled_hbm, attended_hbm, residual_hbm,
    even_ref, layer_out_ref,
    scaled_ref, attended_ref, residual_ref, sems,
):
    balanced = pl.ds(0, BAL_ROWS)
    fetch = start(
        sems,
        (scaled_hbm, scaled_ref),
        (residual_hbm.at[:, balanced], residual_ref),
        (attended_hbm.at[:, balanced], attended_ref),
    )
    kept, incoming, holds_two = my_counts(frames_ref, partner_ref, moved_ref)
    fetch[0].wait()
    blocks_of(weight_ref, scaled_ref[...], 0, even_ref)
    received = dot(got_ref[pl.ds(0, ROWS), :], light_places(kept, incoming), COLS_BY_COLS)
    wait(fetch[1:])
    own = to_column(scale_ref[...]) * dot(weight_ref[...], attended_ref[...])
    own = (residual_ref[...].astype(f32) + own).astype(bf16).astype(f32)
    keep = positions((ROWS, BAL_ROWS), 1) < kept
    layer_out_ref[...] = jnp.where(keep, own, received).astype(bf16)


def slots_kernel(pieces_ref, copies_hbm, scale_grad_ref, by_slot, sems):
    total = pieces_ref[0].astype(f32)
    for piece in range(1, N_DP):
        total = total + pieces_ref[piece].astype(f32)
    for slot in range(HEADS):
        by_slot[slot] = total[:, slot * ROWS : (slot + 1) * ROWS].astype(bf16)
    copies = [
        (by_slot, copies_hbm.at[pl.ds(z * HEADS, HEADS)]) for z in range(NZ)
    ]
    copies = start(sems, *copies)
    lines = total[0:2, D:] + total[2:4, D:]
    scale_grad_ref[...] = jnp.concatenate([lines[0:1, :], lines[1:2, : ROWS - HD]], axis=1)
    wait(copies)


def join_kernel(owned_ref, whole_ref, joined):
    for z in range(NZ):
        for block in range(N_FSDP):
            joined[pl.ds(z * SHARE, SHARE), pl.ds(block * ROWS, ROWS)] = owned_ref[
                z * N_FSDP + block
            ].astype(f32)
    whole_ref[...] = joined[...].astype(bf16)


def split(values):
    high = values.astype(bf16)
    return high, (values - high.astype(f32)).astype(bf16)


def mul(a, b):
    a_high, a_low = split(a)
    b_high, b_low = split(b)
    return dot(
        jnp.concatenate([a_high, a_high, a_low], axis=1),
        jnp.concatenate([b_high, b_low, b_high], axis=0),
    )


def ortho_kernel(
    grad_ref, left_ref, first_ref, second_ref, third_ref,
    out_hbm, input_grad_hbm,
    out_ref, input_grad_ref, sems,
):
    total = left_ref[...].astype(f32)
    for ref in (first_ref, second_ref, third_ref):
        total = total + ref[...].astype(f32)
    input_grad_ref[...] = total.astype(bf16)
    stores = start(sems.at[pl.ds(PARTS, 1)], (input_grad_ref, input_grad_hbm))
    grad = grad_ref[...]
    gram = dot(grad, grad, COLS_BY_COLS)
    eye = jnp.where(same(HD), 1.0, 0.0).astype(f32)
    squares = jnp.sum(jnp.sum(gram * eye, axis=1, keepdims=True), axis=0, keepdims=True)
    norm = jnp.sqrt(squares) + EPSILON
    gram = gram / norm / norm
    total = None
    for sweep in range(ITERS):
        step = coeff_linear * eye + coeff_square * gram + coeff_cubic * mul(gram, gram)
        total = step if total is None else mul(total, step)
        if sweep < ITERS - 1:
            gram = mul(mul(step, gram), step)
    total = jnp.concatenate(split(total * (0.2 * math.sqrt(D) / norm)), axis=1)
    for index, first in enumerate(range(0, D, D // PARTS)):
        cut = pl.ds(first, D // PARTS)
        out = dot(grad_ref[:, cut], total, ROWS_BY_COLS)
        out_ref[cut, :] = (out[:, :HD] + out[:, HD:]).astype(bf16)
        stores += start(sems.at[pl.ds(index, 1)], (out_ref.at[cut, :], out_hbm.at[cut, :]))
    wait(stores)


S, V, H = pltpu.SMEM, pltpu.VMEM, pltpu.HBM
FREE = pl.CostEstimate(flops=0, bytes_accessed=0, transcendentals=0)


def call(kernel, name, places, arrays, outs, scratch=(), cost=None):
    arrays = [
        pltpu.with_memory_space_constraint(array, H) if place is H else array
        for array, place in zip(arrays, places)
    ]
    return pl.pallas_call(
        kernel,
        out_shape=[
            H(shape, dtype) if place is H else jax.ShapeDtypeStruct(shape, dtype)
            for shape, dtype, place in outs
        ],
        in_specs=[pl.BlockSpec(memory_space=place) for place in places],
        out_specs=[pl.BlockSpec(memory_space=place) for shape, dtype, place in outs],
        scratch_shapes=list(scratch),
        compiler_params=pltpu.CompilerParams(vmem_limit_bytes=32 * 1024 * 1024),
        name=name,
        cost_estimate=cost,
    )(*arrays)


def exchange(pieces, axes):
    return lax.all_to_all(pieces, axes, split_axis=0, concat_axis=0, tiled=True)


def crossed(array, axis, size, bit):
    return lax.ppermute(array, axis, [(i, i ^ bit) for i in range(size)])


EVEN = (0, 8, 4, 12, 2, 10, 6, 14)


def add_kernel(*refs, parts):
    in_refs, out_refs = refs[:-parts], refs[-parts:]
    rows = in_refs[0].shape[0] // parts
    for index, out_ref in enumerate(out_refs):
        cut = pl.ds(index * rows, rows)
        total = in_refs[0][cut, :].astype(f32)
        for ref in in_refs[1:]:
            total = total + ref[cut, :].astype(f32)
        out_ref[...] = total.astype(bf16)


def add(arrays, parts):
    rows = arrays[0].shape[0] // parts
    return call(
        functools.partial(add_kernel, parts=parts), "add", [V] * len(arrays), arrays,
        [((rows, CAP_ROWS), bf16, V)] * parts, cost=FREE,
    )


def body(
    attended, residual, grad_out, out_weight, layer_scale, frames, partner, moved_tiles, owner_slot
):
    scale_row = layer_scale[None, :]
    ints = pltpu.SMEM((N_DP,), jnp.int32)
    dma = pltpu.SemaphoreType.DMA

    (window,) = call(
        project_kernel, "project", [H] * 8,
        (frames, partner, moved_tiles, attended, residual, grad_out, out_weight, scale_row),
        [((PAD_ROWS, MOVE_ROWS), bf16, V)],
        [
            ints, ints, ints,
            V((A, MOVE_ROWS), bf16), V((ROWS, MOVE_ROWS), bf16), V((ROWS, BAL_ROWS), bf16),
            V((ROWS, A), bf16), V((1, ROWS), f32),
            dma((6,)), dma((A // CHUNK,)), dma((A // CHUNK,)),
        ],
    )
    pieces = exchange(window.reshape(N_DP, PAD_ROWS // N_DP, MOVE_ROWS), ("z", "x"))
    (pieces,) = call(
        forward_kernel, "forward", [S, V], (partner, pieces),
        [((N_DP, PAD_ROWS // N_DP, MOVE_ROWS), bf16, V)],
    )
    pieces = exchange(pieces, ("z", "x"))
    got = pieces.reshape(PAD_ROWS, MOVE_ROWS)

    scaled, pieces = call(
        weight_grad_kernel, "weight_grad", [S] * 4 + [V] * 5,
        (
            frames, partner, moved_tiles, owner_slot,
            attended, grad_out, out_weight, scale_row, got,
        ),
        [((ROWS, CAP_ROWS), bf16, H), ((N_DP, SHARE, WIDE), bf16, H)],
        [
            pltpu.SMEM((HEADS,), jnp.int32), V((HD, D), f32),
            V((ROWS, CAP_ROWS), bf16), V((N_DP, SHARE, WIDE), bf16), dma((7,)),
        ],
    )
    summed = exchange(pieces, ("z", "x"))

    half = ((A // 2, CAP_ROWS), bf16, V)
    (odd,) = call(
        odd_kernel, "input_grad_odd", [V, H], (out_weight, scaled), [half],
        [V((ROWS, CAP_ROWS), bf16), dma((1,))],
        FREE,
    )
    odd = crossed(odd, "c", NC, 1)
    even, layer_out = call(
        even_kernel, "input_grad_even", [S] * 3 + [V] * 3 + [H] * 3,
        (
            frames, partner, moved_tiles,
            out_weight, scale_row, got, scaled, attended, residual,
        ),
        [half, ((ROWS, BAL_ROWS), bf16, V)],
        [
            V((ROWS, CAP_ROWS), bf16), V((A, BAL_ROWS), bf16), V((ROWS, BAL_ROWS), bf16),
            dma((3,)),
        ],
        FREE,
    )
    left, other = add((even, odd), 2)
    summed, _ = lax.optimization_barrier((summed, left))
    copies, scale_grad = call(
        slots_kernel, "slots", [V], (summed,),
        [((NZ * HEADS, SHARE, ROWS), bf16, H), ((1, ROWS), f32, V)],
        [V((HEADS, SHARE, ROWS), bf16), dma((NZ,))],
    )
    owned = exchange(copies, ("z", "y", "c"))
    left, *others = add((left, crossed(other, "y", NY, 1)), 4)
    owned, _ = lax.optimization_barrier((owned, left))
    others = [crossed(other, "y", NY, step) for other, step in zip(others[1:] + others[:1], (2, 6, 4))]
    (copies,) = call(
        join_kernel, "join", [V], (owned,),
        [((BY_X, D), bf16, V)],
        [V((BY_X, D), f32)],
    )
    whole = lax.all_gather(copies, "x", axis=0, tiled=True)
    ortho_update, input_grad = call(
        ortho_kernel, "ortho", [V] * 5, (whole, left, *others),
        [((D, HD), bf16, H), ((HD, CAP_ROWS), bf16, H)],
        [V((D, HD), bf16), V((HD, CAP_ROWS), bf16), dma((PARTS + 1,))],
    )
    return (layer_out, input_grad, scale_grad.reshape(ROWS), ortho_update[:, None, :])


def solution(mesh):
    chips = Mesh(mesh.devices.reshape(NZ, NX, NY, NC), ("z", "x", "y", "c"))
    dp, fsdp = ("z", "x"), ("y", "c")
    placed = (
        P(None, dp),
        P(fsdp, dp),
        P(fsdp, dp),
        P(fsdp, None),
        P(fsdp),
        P(),
        P(),
        P(),
        P(),
    )
    return jax.shard_map(
        body,
        mesh=chips,
        in_specs=placed,
        out_specs=(P(fsdp, dp), P(fsdp, dp), P(fsdp), P(None, fsdp, None)),
        check_vma=False,
    )
```

```python
import functools
import math

import jax
import jax.numpy as jnp
from jax import lax
from jax.experimental import pallas as pl
from jax.experimental.pallas import tpu as pltpu
from jax.sharding import Mesh, PartitionSpec as P

D = 3200
HEADS = 16
HD = 128
FRAME = 256
TILE = 16
ITERS = 5
A = 2048
CAP_ROWS = 512
MOVE_ROWS = 256
BAL_ROWS = 384
N_DP = 32
N_FSDP = 16

NZ, NX, NY, NC = 8, 4, 8, 2
ROWS = D // N_FSDP
BY_X = HD // NX
SHARE = HD // N_DP
WIDE = D + HD
PAD_ROWS = 256
CHUNK = 1024
PARTS = 5

coeff_linear = 3.4445
coeff_square = -4.775
coeff_cubic = 2.0315
EPSILON = 1e-07
INVERSE_ROOT = 1.0 / math.sqrt(N_DP * BAL_ROWS)

bf16 = jnp.bfloat16
f32 = jnp.float32

ROWS_BY_COLS = (((0,), (0,)), ((), ()))
COLS_BY_COLS = (((1,), (1,)), ((), ()))


def positions(shape, dimension):
    return lax.broadcasted_iota(jnp.int32, shape, dimension)


def dot(a, b, dims=(((1,), (0,)), ((), ()))):
    return lax.dot_general(a, b, dims, preferred_element_type=f32)


def same(size):
    return positions((size, size), 0) == positions((size, size), 1)


def to_column(row):
    size = row.shape[1]
    return jnp.sum(jnp.where(same(size), row, 0.0), axis=1, keepdims=True)


def to_row(column):
    size = column.shape[0]
    return jnp.sum(jnp.where(same(size), column, 0.0), axis=0, keepdims=True)


def my_counts(frames_ref, partner_ref, moved_ref):
    replica = lax.axis_index("z") * NX + lax.axis_index("x")
    mate = partner_ref[replica]
    kept = frames_ref[replica] * FRAME - moved_ref[replica] * TILE
    incoming = moved_ref[mate] * TILE
    holds_two = (frames_ref[replica] > frames_ref[mate]).astype(jnp.int32)
    return kept, incoming, holds_two


def light_places(kept, incoming):
    bal_col = positions((BAL_ROWS, MOVE_ROWS), 0)
    win_col = positions((BAL_ROWS, MOVE_ROWS), 1)
    hit = bal_col == win_col + (kept + incoming - MOVE_ROWS)
    hit = hit & (win_col >= MOVE_ROWS - incoming)
    return jnp.where(hit, 1.0, 0.0).astype(bf16)


def start(sems, *pairs):
    copies = [pltpu.make_async_copy(a, b, sems.at[i]) for i, (a, b) in enumerate(pairs)]
    for copy in copies:
        copy.start()
    return copies


def wait(copies):
    for copy in copies:
        copy.wait()


def project_kernel(
    frames_hbm, partner_hbm, moved_hbm,
    attended_hbm, residual_hbm, grad_hbm, weight_hbm, scale_hbm,
    window_ref,
    frames_ref, partner_ref, moved_ref,
    attended_ref, residual_ref, grad_ref, weight_ref, scale_ref,
    small_sems, attended_sems, weight_sems,
):
    late = pl.ds(CAP_ROWS - MOVE_ROWS, MOVE_ROWS)
    small = start(
        small_sems,
        (frames_hbm, frames_ref),
        (partner_hbm, partner_ref),
        (moved_hbm, moved_ref),
        (scale_hbm, scale_ref),
        (grad_hbm, grad_ref),
        (residual_hbm.at[:, late], residual_ref),
    )
    cuts = [pl.ds(first, CHUNK) for first in range(0, A, CHUNK)]
    attended = start(
        attended_sems, *[(attended_hbm.at[cut, late], attended_ref.at[cut, :]) for cut in cuts]
    )
    weight = start(
        weight_sems, *[(weight_hbm.at[:, cut], weight_ref.at[:, cut]) for cut in cuts]
    )
    wait(small[:5])
    kept, incoming, holds_two = my_counts(frames_ref, partner_ref, moved_ref)
    gains = to_column(scale_ref[...])
    grad_win = dot(grad_ref[...], light_places(kept, incoming))
    window_ref[pl.ds(ROWS, PAD_ROWS - ROWS), :] = jnp.zeros(
        (PAD_ROWS - ROWS, MOVE_ROWS), bf16
    )
    projected = None
    for index, cut in enumerate(cuts):
        attended[index].wait()
        weight[index].wait()
        part = dot(weight_ref[:, cut], attended_ref[cut, :])
        projected = part if projected is None else projected + part
    small[5].wait()
    layer = (residual_ref[...].astype(f32) + gains * projected).astype(bf16)
    layer_win = layer.astype(f32)
    window_ref[pl.ds(0, ROWS), :] = jnp.where(holds_two == 1, layer_win, grad_win).astype(bf16)


def forward_kernel(partner_ref, pieces_ref, out_ref):
    for replica in range(N_DP):
        out_ref[replica] = pieces_ref[partner_ref[replica]]


def send_lanes(first, last, value, pieces_ref, pieces_hbm, sems):
    lanes = pl.ds(first, last - first)
    for piece in range(N_DP):
        pieces_ref[piece, :, lanes] = value(piece, lanes)
    return start(sems, (pieces_ref.at[:, :, lanes], pieces_hbm.at[:, :, lanes]))


def weight_grad_kernel(
    frames_ref, partner_ref, moved_ref, slot_ref,
    attended_ref, grad_ref, weight_ref, scale_ref, got_ref,
    scaled_hbm, pieces_hbm,
    head_of, wide, scaled_ref, pieces_ref, sems,
):
    kept, incoming, holds_two = my_counts(frames_ref, partner_ref, moved_ref)
    for head in range(HEADS):
        head_of[slot_ref[head]] = head
    own = grad_ref[...].astype(f32)
    own = jnp.concatenate([own, jnp.zeros((ROWS, CAP_ROWS - BAL_ROWS), f32)], axis=1)
    got = got_ref[pl.ds(0, ROWS), :].astype(f32)
    got = jnp.where(holds_two == 1, got, 0.0)
    got = jnp.concatenate([jnp.zeros((ROWS, CAP_ROWS - MOVE_ROWS), f32), got], axis=1)
    grad = jnp.where(positions((ROWS, CAP_ROWS), 1) < kept, own, got)
    scaled = (grad * to_column(scale_ref[...])).astype(bf16)
    scaled_ref[...] = scaled
    (store,) = start(sems.at[pl.ds(1, 1)], (scaled_ref, scaled_hbm))
    projected = dot(weight_ref[...], attended_ref[...])
    part = jnp.sum(grad * projected, axis=1, keepdims=True) * INVERSE_ROOT
    part = to_row(part)
    high = part.astype(bf16).astype(f32)
    low = part - high
    zeros = jnp.zeros((1, 2 * HD - ROWS), f32)
    lines = [
        high[:, :HD],
        jnp.concatenate([high[:, HD:], zeros], axis=1),
        low[:, :HD],
        jnp.concatenate([low[:, HD:], zeros], axis=1),
    ]
    lines = jnp.concatenate(lines, axis=0).astype(bf16)
    stores = [store]
    stores += send_lanes(
        D, WIDE, lambda piece, lanes: lines, pieces_ref, pieces_hbm, sems.at[pl.ds(6, 1)]
    )
    done = 0
    for slot in range(HEADS):
        first = pl.multiple_of(head_of[slot] * HD, HD)
        wide[:, pl.ds(slot * ROWS, ROWS)] = dot(
            attended_ref[pl.ds(first, HD), :], scaled, COLS_BY_COLS
        )
        if (slot + 1) % 4 == 0:
            full = (slot + 1) * ROWS // HD * HD
            stores += send_lanes(done, full, lambda piece, lanes: wide[
                pl.ds((piece % NX * NZ + piece // NX) * SHARE, SHARE), lanes
            ].astype(bf16), pieces_ref, pieces_hbm, sems.at[pl.ds(2 + slot // 4, 1)])
            done = full
    wait(stores)


def input_kernel(
    frames_ref, partner_ref, moved_ref,
    weight_ref, scale_ref, got_ref, scaled_hbm, attended_hbm, residual_hbm,
    even_ref, odd_ref, layer_out_ref,
    scaled_ref, attended_ref, residual_ref, sems,
):
    balanced = pl.ds(0, BAL_ROWS)
    fetch = start(
        sems,
        (scaled_hbm, scaled_ref),
        (residual_hbm.at[:, balanced], residual_ref),
        (attended_hbm.at[:, balanced], attended_ref),
    )
    kept, incoming, holds_two = my_counts(frames_ref, partner_ref, moved_ref)
    block = lax.axis_index("y") * NC + lax.axis_index("c")
    fetch[0].wait()
    scaled = scaled_ref[...]
    for index, other in enumerate(EVEN):
        for ref, partner in ((even_ref, other), (odd_ref, other + 1)):
            first = pl.multiple_of((block ^ partner) * HD, HD)
            part = dot(weight_ref[:, pl.ds(first, HD)], scaled, ROWS_BY_COLS)
            ref[pl.ds(index * HD, HD), :] = part.astype(bf16)
    received = dot(got_ref[pl.ds(0, ROWS), :], light_places(kept, incoming), COLS_BY_COLS)
    wait(fetch[1:])
    own = to_column(scale_ref[...]) * dot(weight_ref[...], attended_ref[...])
    own = (residual_ref[...].astype(f32) + own).astype(bf16).astype(f32)
    keep = positions((ROWS, BAL_ROWS), 1) < kept
    layer_out_ref[...] = jnp.where(keep, own, received).astype(bf16)


def slots_kernel(pieces_ref, copies_ref, scale_grad_ref):
    total = pieces_ref[0].astype(f32)
    for piece in range(1, N_DP):
        total = total + pieces_ref[piece].astype(f32)
    for slot in range(HEADS):
        part = total[:, slot * ROWS : (slot + 1) * ROWS].astype(bf16)
        for z in range(NZ):
            copies_ref[z * HEADS + slot] = part
    lines = total[0:2, D:] + total[2:4, D:]
    scale_grad_ref[...] = jnp.concatenate([lines[0:1, :], lines[1:2, : ROWS - HD]], axis=1)


def join_kernel(owned_ref, whole_ref, joined):
    for z in range(NZ):
        for block in range(N_FSDP):
            joined[pl.ds(z * SHARE, SHARE), pl.ds(block * ROWS, ROWS)] = owned_ref[
                z * N_FSDP + block
            ].astype(f32)
    whole_ref[...] = joined[...].astype(bf16)


def split(values):
    high = values.astype(bf16)
    return high, (values - high.astype(f32)).astype(bf16)


def mul(a, b):
    a_high, a_low = split(a)
    b_high, b_low = split(b)
    return dot(
        jnp.concatenate([a_high, a_high, a_low], axis=1),
        jnp.concatenate([b_high, b_low, b_high], axis=0),
    )


def ortho_kernel(
    grad_ref, left_ref, first_ref, second_ref, third_ref,
    out_hbm, input_grad_hbm,
    out_ref, input_grad_ref, sems,
):
    total = left_ref[...].astype(f32)
    for ref in (first_ref, second_ref, third_ref):
        total = total + ref[...].astype(f32)
    input_grad_ref[...] = total.astype(bf16)
    stores = start(sems.at[pl.ds(PARTS, 1)], (input_grad_ref, input_grad_hbm))
    grad = grad_ref[...]
    gram = dot(grad, grad, COLS_BY_COLS)
    eye = jnp.where(same(HD), 1.0, 0.0).astype(f32)
    squares = jnp.sum(jnp.sum(gram * eye, axis=1, keepdims=True), axis=0, keepdims=True)
    norm = jnp.sqrt(squares) + EPSILON
    gram = gram / norm / norm
    total = None
    for sweep in range(ITERS):
        step = coeff_linear * eye + coeff_square * gram + coeff_cubic * mul(gram, gram)
        total = step if total is None else mul(total, step)
        if sweep < ITERS - 1:
            gram = mul(mul(step, gram), step)
    total = jnp.concatenate(split(total * (0.2 * math.sqrt(D) / norm)), axis=1)
    for index, first in enumerate(range(0, D, D // PARTS)):
        cut = pl.ds(first, D // PARTS)
        out = dot(grad_ref[:, cut], total, ROWS_BY_COLS)
        out_ref[cut, :] = (out[:, :HD] + out[:, HD:]).astype(bf16)
        stores += start(sems.at[pl.ds(index, 1)], (out_ref.at[cut, :], out_hbm.at[cut, :]))
    wait(stores)


S, V, H = pltpu.SMEM, pltpu.VMEM, pltpu.HBM
FREE = pl.CostEstimate(flops=0, bytes_accessed=0, transcendentals=0)


def call(kernel, name, places, arrays, outs, scratch=(), cost=None):
    arrays = [
        pltpu.with_memory_space_constraint(array, H) if place is H else array
        for array, place in zip(arrays, places)
    ]
    return pl.pallas_call(
        kernel,
        out_shape=[
            H(shape, dtype) if place is H else jax.ShapeDtypeStruct(shape, dtype)
            for shape, dtype, place in outs
        ],
        in_specs=[pl.BlockSpec(memory_space=place) for place in places],
        out_specs=[pl.BlockSpec(memory_space=place) for shape, dtype, place in outs],
        scratch_shapes=list(scratch),
        compiler_params=pltpu.CompilerParams(vmem_limit_bytes=32 * 1024 * 1024),
        name=name,
        cost_estimate=cost,
    )(*arrays)


def exchange(pieces, axes):
    return lax.all_to_all(pieces, axes, split_axis=0, concat_axis=0, tiled=True)


def crossed(array, axis, size, bit):
    return lax.ppermute(array, axis, [(i, i ^ bit) for i in range(size)])


EVEN = (0, 8, 4, 12, 2, 10, 6, 14)


def add_kernel(*refs, parts):
    in_refs, out_refs = refs[:-parts], refs[-parts:]
    rows = in_refs[0].shape[0] // parts
    for index, out_ref in enumerate(out_refs):
        cut = pl.ds(index * rows, rows)
        total = in_refs[0][cut, :].astype(f32)
        for ref in in_refs[1:]:
            total = total + ref[cut, :].astype(f32)
        out_ref[...] = total.astype(bf16)


def add(arrays, parts):
    rows = arrays[0].shape[0] // parts
    return call(
        functools.partial(add_kernel, parts=parts), "add", [V] * len(arrays), arrays,
        [((rows, CAP_ROWS), bf16, V)] * parts, cost=FREE,
    )


def body(
    attended, residual, grad_out, out_weight, layer_scale, frames, partner, moved_tiles, owner_slot
):
    scale_row = layer_scale[None, :]
    ints = pltpu.SMEM((N_DP,), jnp.int32)
    dma = pltpu.SemaphoreType.DMA

    (window,) = call(
        project_kernel, "project", [H] * 8,
        (frames, partner, moved_tiles, attended, residual, grad_out, out_weight, scale_row),
        [((PAD_ROWS, MOVE_ROWS), bf16, V)],
        [
            ints, ints, ints,
            V((A, MOVE_ROWS), bf16), V((ROWS, MOVE_ROWS), bf16), V((ROWS, BAL_ROWS), bf16),
            V((ROWS, A), bf16), V((1, ROWS), f32),
            dma((6,)), dma((A // CHUNK,)), dma((A // CHUNK,)),
        ],
    )
    pieces = exchange(window.reshape(N_DP, PAD_ROWS // N_DP, MOVE_ROWS), ("z", "x"))
    (pieces,) = call(
        forward_kernel, "forward", [S, V], (partner, pieces),
        [((N_DP, PAD_ROWS // N_DP, MOVE_ROWS), bf16, V)],
    )
    pieces = exchange(pieces, ("z", "x"))
    got = pieces.reshape(PAD_ROWS, MOVE_ROWS)

    scaled, pieces = call(
        weight_grad_kernel, "weight_grad", [S] * 4 + [V] * 5,
        (
            frames, partner, moved_tiles, owner_slot,
            attended, grad_out, out_weight, scale_row, got,
        ),
        [((ROWS, CAP_ROWS), bf16, H), ((N_DP, SHARE, WIDE), bf16, H)],
        [
            pltpu.SMEM((HEADS,), jnp.int32), V((HD, D), f32),
            V((ROWS, CAP_ROWS), bf16), V((N_DP, SHARE, WIDE), bf16), dma((7,)),
        ],
    )
    summed = exchange(pieces, ("z", "x"))

    half = ((A // 2, CAP_ROWS), bf16, V)
    even, odd, layer_out = call(
        input_kernel, "input_grad", [S] * 3 + [V] * 3 + [H] * 3,
        (
            frames, partner, moved_tiles,
            out_weight, scale_row, got, scaled, attended, residual,
        ),
        [half, half, ((ROWS, BAL_ROWS), bf16, V)],
        [
            V((ROWS, CAP_ROWS), bf16), V((A, BAL_ROWS), bf16), V((ROWS, BAL_ROWS), bf16),
            dma((3,)),
        ],
        FREE,
    )
    left, other = add((even, crossed(odd, "c", NC, 1)), 2)
    summed, _ = lax.optimization_barrier((summed, left))
    copies, scale_grad = call(
        slots_kernel, "slots", [V], (summed,),
        [((NZ * HEADS, SHARE, ROWS), bf16, V), ((1, ROWS), f32, V)],
    )
    owned = exchange(copies, ("z", "y", "c"))
    left, *others = add((left, crossed(other, "y", NY, 1)), 4)
    owned, _ = lax.optimization_barrier((owned, left))
    others = [crossed(other, "y", NY, step) for other, step in zip(others[1:] + others[:1], (2, 6, 4))]
    (copies,) = call(
        join_kernel, "join", [V], (owned,),
        [((BY_X, D), bf16, V)],
        [V((BY_X, D), f32)],
    )
    whole = lax.all_gather(copies, "x", axis=0, tiled=True)
    ortho_update, input_grad = call(
        ortho_kernel, "ortho", [V] * 5, (whole, left, *others),
        [((D, HD), bf16, H), ((HD, CAP_ROWS), bf16, H)],
        [V((D, HD), bf16), V((HD, CAP_ROWS), bf16), dma((PARTS + 1,))],
    )
    return (layer_out, input_grad, scale_grad.reshape(ROWS), ortho_update[:, None, :])


def solution(mesh):
    chips = Mesh(mesh.devices.reshape(NZ, NX, NY, NC), ("z", "x", "y", "c"))
    dp, fsdp = ("z", "x"), ("y", "c")
    placed = (
        P(None, dp),
        P(fsdp, dp),
        P(fsdp, dp),
        P(fsdp, None),
        P(fsdp),
        P(),
        P(),
        P(),
        P(),
    )
    return jax.shard_map(
        body,
        mesh=chips,
        in_specs=placed,
        out_specs=(P(fsdp, dp), P(fsdp, dp), P(fsdp), P(None, fsdp, None)),
        check_vma=False,
    )
```
